32 devices in a mesh: span: 4 (over z), ha: 2 (over x), wa: 4 (over y, core).
Axes of the slice: x: 2, y: 2, z: 4, core: 2. Of those that a mesh axis runs over, the one named last changes fastest.
Arguments:
- queries: bfloat16 [4, 3, 8, 48, 768], P('span', None, 'ha', 'wa'), may hold values from -5 to 5
- cache_keys: bfloat16 [4, 3, 8, 48, 768], P('span', None, 'ha', 'wa'), may hold values from -5 to 5
- cache_values: bfloat16 [4, 3, 8, 48, 768], P('span', None, 'ha', 'wa'), may hold values from -16 to 16
- grad_attended: bfloat16 [4, 3, 8, 48, 768], P('span', None, 'ha', 'wa'), may hold values from -16 to 16
- radius: int32 [6], replicated, may hold values from 1 to 2, as said below
- frame_count: int32 [4], replicated, may hold values from 1 to 3, as said below
Outputs:
- attended: bfloat16 [4, 3, 8, 48, 768], P('span', None, 'ha', 'wa')
- grad_queries: bfloat16 [4, 3, 8, 48, 768], P('span', None, 'ha', 'wa')
- grad_keys: bfloat16 [4, 3, 8, 48, 768], P('span', None, 'ha', 'wa')
- grad_values: bfloat16 [4, 3, 8, 48, 768], P('span', None, 'ha', 'wa')
The draws below stay inside these ranges and needn't reach their ends.
Inputs may be any that keep to these rules, and one draw needn't show every extreme that they name: Some head has radius 2 and some other head has radius 1. Frame slots of block c at or past frame_count[c] hold padding; some block has all 3 slots live.
All inputs are finite; a program needn't handle non-finite values.
Results may differ from the reference program's by a relative error of at most 0.02.
Values may be sent and summed in bfloat16 or wider, within the bound.
No kernel may reach another device: no remote copies, remote signals or barrier semaphores. Data moves between devices by JAX's collectives and lax.ppermute only.
A program may use at most 128 MiB of HBM per device.

```python
import math
import jax
import jax.numpy as jnp
from jax import lax

HEADS = 6
DH = 128
FR = 3
RMAX = 2
BLOCKS = 4
HT = 8
WT = 48


def paired_field(key, which):
    base = jax.random.fold_in(key, 29)
    layout = (BLOCKS, FR, HT, WT, HEADS * DH)
    first_key, second_key = jax.random.split(base, 2)
    query_part = jnp.clip(jax.random.normal(first_key, layout, jnp.float32), -4.5, 4.5)
    key_part = jnp.clip(jax.random.normal(second_key, layout, jnp.float32), -4.5, 4.5)
    if which == 0:
        return query_part.astype(jnp.bfloat16)
    return key_part.astype(jnp.bfloat16)


def draw_queries(key, part):
    return paired_field(key, 0)


def draw_cache_keys(key, part):
    return paired_field(key, 1)


def draw_radius(key, part):
    base = jax.random.fold_in(key, 41)
    first_key, second_key = jax.random.split(base)
    values = jax.random.randint(first_key, (HEADS,), 1, RMAX + 1)
    order = jax.random.permutation(second_key, HEADS)
    head_ids = jnp.arange(HEADS)
    values = jnp.where(head_ids == order[0], RMAX, values)
    values = jnp.where(head_ids == order[1], 1, values)
    return values.astype(jnp.int32)


def draw_frame_count(key, part):
    base = jax.random.fold_in(key, 53)
    first_key, second_key = jax.random.split(base)
    values = jax.random.randint(first_key, (BLOCKS,), 1, FR + 1)
    fullest = jax.random.randint(second_key, (), 0, BLOCKS)
    return jnp.where(jnp.arange(BLOCKS) == fullest, FR, values).astype(jnp.int32)


def level_of(key, shape, shards, low, largest):
    factor_of, own = 1.0, jax.random.fold_in(key, 6)
    for position, parts in shards:
        steps = jnp.exp(jax.random.uniform(jax.random.fold_in(own, position), (parts,), jnp.float32, low / len(shards), largest / len(shards)))
        factor_of = factor_of * jnp.repeat(steps, shape[position] // parts).reshape([-1 if axis == position else 1 for axis in range(len(shape))])
    return factor_of


def gaussian(own_key, extent, width, most, pieces=(), dtype=jnp.bfloat16):
    entries = jax.random.normal(own_key, extent, jnp.float32) * width
    if len(pieces) > 0:
        entries = level_of(own_key, extent, pieces, -0.22, 0.18) * entries
    return jnp.clip(entries, min=-most, max=most).astype(dtype)


def setup_inputs(seed: int = 0) -> dict:
    streams_of = jax.random.split(jax.random.key(seed), 7)
    return {
        "queries": draw_queries(jax.random.fold_in(streams_of[6], 71), 0),
        "cache_keys": draw_cache_keys(jax.random.fold_in(streams_of[6], 71), 0),
        "cache_values": gaussian(streams_of[2], (BLOCKS, FR, HT, WT, HEADS * DH), 4.0, 16.0, ((0, 4), (2, 2), (3, 4))),
        "grad_attended": gaussian(streams_of[3], (BLOCKS, FR, HT, WT, HEADS * DH), 4.0, 16.0, ((0, 4), (2, 2), (3, 4))),
        "radius": draw_radius(jax.random.fold_in(streams_of[6], 71), 0),
        "frame_count": draw_frame_count(jax.random.fold_in(streams_of[6], 71), 0),
    }


def shifted(field, along_y, along_x):
    return jnp.roll(field, (-along_y, -along_x), axis=(2, 3))

def rounded(values_f32):
    return lax.optimization_barrier(values_f32.astype(jnp.bfloat16)).astype(jnp.float32)

def reference(queries, cache_keys, cache_values, grad_attended, radius, frame_count):
    layout = (BLOCKS, FR, HT, WT, HEADS, DH)
    query_all = queries.astype(jnp.float32).reshape(layout)
    key_all = cache_keys.astype(jnp.float32).reshape(layout)
    value_all = cache_values.astype(jnp.float32).reshape(layout)
    upstream = grad_attended.astype(jnp.float32).reshape(layout)
    scale = 1.0 / math.sqrt(DH)
    block_ids = jnp.arange(BLOCKS)
    causal = block_ids[None, :] <= block_ids[:, None]
    frame_live = jnp.arange(FR)[None, :] < frame_count[:, None]
    row_ids = jnp.arange(HT)
    col_ids = jnp.arange(WT)
    offsets = [(0, 0)]
    for along_y in range(-RMAX, RMAX + 1):
        for along_x in range(-RMAX, RMAX + 1):
            if along_y != 0 or along_x != 0:
                offsets.append((along_y, along_x))

    def visible(along_y, along_x):
        inside_rows = (row_ids + along_y >= 0) & (row_ids + along_y < HT)
        inside_cols = (col_ids + along_x >= 0) & (col_ids + along_x < WT)
        inside = inside_rows[:, None] & inside_cols[None, :]
        within = radius >= max(abs(along_y), abs(along_x))
        return causal[:, None, :, None, None, None, None] & frame_live[None, None, :, :, None, None, None] & inside[None, None, None, None, :, :, None] & within[None, None, None, None, None, None, :]
    top = jnp.full((BLOCKS, FR, HT, WT, HEADS), -jnp.inf, jnp.float32)
    total = jnp.zeros((BLOCKS, FR, HT, WT, HEADS), jnp.float32)
    accum = jnp.zeros(layout, jnp.float32)
    for along_y, along_x in offsets:
        key_moved = shifted(key_all, along_y, along_x)
        value_moved = shifted(value_all, along_y, along_x)
        allowed = visible(along_y, along_x)
        score = jnp.einsum('cfyxhd,gkyxhd->cfgkyxh', query_all, key_moved) * scale
        score = jnp.where(allowed, score, -jnp.inf)
        new_top = jnp.maximum(top, lax.optimization_barrier(jnp.max(score, axis=(2, 3))))
        weight = jnp.exp(score - new_top[:, :, None, None])
        fading = jnp.exp(top - new_top)
        total = total * fading + lax.optimization_barrier(jnp.sum(weight, axis=(2, 3)))
        accum = accum * fading[..., None] + jnp.einsum('cfgkyxh,gkyxhd->cfyxhd', rounded(weight), value_moved)
        top = new_top
    attended = lax.optimization_barrier((accum / total[..., None]).astype(jnp.bfloat16))
    log_total = top + jnp.log(total)
    delta = lax.optimization_barrier(jnp.sum(upstream * attended.astype(jnp.float32), axis=-1))
    grad_q = jnp.zeros(layout, jnp.float32)
    grad_k = jnp.zeros(layout, jnp.float32)
    grad_v = jnp.zeros(layout, jnp.float32)
    for along_y, along_x in offsets:
        key_moved = shifted(key_all, along_y, along_x)
        value_moved = shifted(value_all, along_y, along_x)
        allowed = visible(along_y, along_x)
        score = jnp.einsum('cfyxhd,gkyxhd->cfgkyxh', query_all, key_moved) * scale
        prob = jnp.exp(jnp.where(allowed, score - log_total[:, :, None, None], -jnp.inf))
        grad_v = grad_v + shifted(jnp.einsum('cfgkyxh,cfyxhd->gkyxhd', rounded(prob), upstream), -along_y, -along_x)
        push = jnp.einsum('cfyxhd,gkyxhd->cfgkyxh', upstream, value_moved)
        slope = rounded(prob * (push - delta[:, :, None, None]))
        grad_q = grad_q + jnp.einsum('cfgkyxh,gkyxhd->cfyxhd', slope, key_moved)
        grad_k = grad_k + shifted(jnp.einsum('cfgkyxh,cfyxhd->gkyxhd', slope, query_all), -along_y, -along_x)
    final = (BLOCKS, FR, HT, WT, HEADS * DH)
    return (attended.reshape(final), (grad_q * scale).astype(jnp.bfloat16).reshape(final), (grad_k * scale).astype(jnp.bfloat16).reshape(final), grad_v.astype(jnp.bfloat16).reshape(final))
```

```python
import functools
import math

import jax
import jax.numpy as jnp
import numpy as np
from jax import lax
from jax.experimental import pallas as pl
from jax.experimental.pallas import tpu as pltpu
from jax.sharding import PartitionSpec as P

RMAX = 2
FAR = 99.0
LOG2E = math.log2(math.e)
VMEM_LIMIT = 56 * 1024 * 1024


def round_up(value, unit):
    return (value + unit - 1) // unit * unit


def dot_nt(a, b):
    return lax.dot_general(a, b, (((1,), (1,)), ((), ())), preferred_element_type=jnp.float32)


def dot_nn(a, b):
    return lax.dot_general(a, b, (((1,), (0,)), ((), ())), preferred_element_type=jnp.float32)


class Side:
    def __init__(self, kind, axis, count, tile):
        index = lax.axis_index(axis)
        if kind == "same":
            delta, start, length = 0, 0, tile
            self.send_start = 0
            self.pairs = [(i, i) for i in range(count)]
        else:
            delta = 1 - 2 * index if kind == "swap" else kind
            length = RMAX
            start = jnp.where(delta > 0, tile, -RMAX)
            if kind == "swap":
                self.send_start = jnp.where(index == 0, tile - RMAX, 0)
                self.pairs = [(0, 1), (1, 0)]
            else:
                self.send_start = tile - RMAX if kind < 0 else 0
                self.pairs = [(i + kind, i) for i in range(count) if 0 <= i + kind < count]
        self.length = length
        self.start = start
        self.valid = (index + delta >= 0) & (index + delta < count)
        self.delta = delta


def sides(axis, count, tile):
    kinds = [] if count == 1 else ["swap"] if count == 2 else [-1, 1]
    return [Side(kind, axis, count, tile) for kind in ["same"] + kinds]


class Geometry:
    def __init__(self, frames, tile_h, tile_w, count_h, count_w):
        self.frames, self.tile_h, self.tile_w = frames, tile_h, tile_w
        self.count_h, self.count_w = count_h, count_w
        self.tokens = frames * tile_h * tile_w
        pieces = [
            (row, col)
            for col in sides("wa", count_w, tile_w)
            for row in sides("ha", count_h, tile_h)
        ]
        self.own, self.pieces = pieces[0], sorted(
            pieces[1:], key=lambda piece: -piece[0].length * piece[1].length
        )
        self.sizes = [round_up(r.length * frames * c.length, 16) for r, c in self.pieces]
        self.offsets = [int(v) for v in self.tokens + np.cumsum([0] + self.sizes)[:-1]]
        self.used = self.tokens + sum(self.sizes)
        self.wide = round_up(self.used, 128)
        index, rows, cols, frame = [], [], [], []
        for number, (row, col) in enumerate([self.own] + self.pieces):
            size = self.tokens if number == 0 else self.sizes[number - 1]
            count = row.length * frames * col.length
            yy, ff, xx = np.unravel_index(np.arange(count), (row.length, frames, col.length))
            pad = (0, size - count)
            live = np.pad(np.ones(count, bool), pad)
            yy, ff, xx = (np.pad(v, pad).astype(np.int32) for v in (yy, ff, xx))
            send = ((row.send_start + yy) * frames + ff) * tile_w + col.send_start + xx
            index.append(jnp.where(live, send, -1))
            valid = live & row.valid & col.valid
            rows.append(jnp.where(valid, row.start + yy, 1000))
            cols.append(jnp.where(valid, col.start + xx, 1000))
            frame.append(ff)
        pad = (0, self.wide - self.used)
        index = jnp.pad(jnp.concatenate(index), pad, constant_values=-1)
        rows = jnp.pad(jnp.concatenate(rows), pad, constant_values=1000)
        cols = jnp.pad(jnp.concatenate(cols), pad, constant_values=1000)
        self.frame = np.pad(np.concatenate(frame), pad).astype(np.int32)
        self.select = (index[:, None] == jnp.arange(self.tokens)[None, :]).astype(jnp.bfloat16)
        own = slice(0, self.tokens)
        gap = jnp.maximum(
            jnp.abs(rows[own][:, None] - rows[None, :]), jnp.abs(cols[own][:, None] - cols[None, :])
        )
        self.gap = jnp.minimum(gap, 99).astype(jnp.float32)

    def permute(self, piece, x):
        row, col = piece
        pairs = [
            (a * self.count_w + c, b * self.count_w + d)
            for a, b in row.pairs
            for c, d in col.pairs
        ]
        return lax.ppermute(x, ("ha", "wa"), pairs)

    def groups(self):
        for f in range(self.frames):
            for y in range(self.tile_h):
                yield f, y, (y * self.frames + f) * self.tile_w


def whole(memory=pltpu.VMEM):
    return pl.BlockSpec(memory_space=memory)


def params():
    return pltpu.CompilerParams(vmem_limit_bytes=VMEM_LIMIT)


def tidy(geo, info, arrays, blocks):
    width = arrays[0].shape[-1]
    tokens = geo.tokens

    def kernel(info_ref, *refs):
        ins, own_ref, sends = refs[:4], refs[4], refs[5 : 4 + blocks]
        compact, sems = refs[4 + blocks], refs[5 + blocks]
        for number, ref in enumerate(ins):
            for f, y, at in geo.groups():
                compact[number, at : at + geo.tile_w, :] = ref[f, y]
        place = info_ref[0]
        copies = [pltpu.make_async_copy(compact, own_ref, sems.at[0])]
        for r in range(1, blocks):
            first = jnp.where(place + r < blocks, 0, 2)
            copies.append(
                pltpu.make_async_copy(compact.at[pl.ds(first, 2)], sends[r - 1], sems.at[r])
            )
        for copy in copies:
            copy.start()
        for copy in copies:
            copy.wait()

    out = pl.pallas_call(
        kernel,
        in_specs=[whole(pltpu.SMEM)] + [whole()] * 4,
        out_specs=[whole(pl.ANY)] * blocks,
        out_shape=[jax.ShapeDtypeStruct((4, tokens, width), jnp.bfloat16)]
        + [jax.ShapeDtypeStruct((2, tokens, width), jnp.bfloat16)] * (blocks - 1),
        scratch_shapes=[
            pltpu.VMEM((4, tokens, width), jnp.bfloat16),
            pltpu.SemaphoreType.DMA((blocks,)),
        ],
        compiler_params=params(),
        name="tidy",
    )(info, *arrays)
    return out[0], out[1:]


def borders(geo, x):
    count, tokens, width = x.shape

    def kernel(select_ref, x_ref, *outs):
        for a in range(count):
            picked = dot_nn(select_ref[tokens:, :], x_ref[a]).astype(jnp.bfloat16)
            for out, size, offset in zip(outs, geo.sizes, geo.offsets):
                out[a] = picked[offset - tokens : offset - tokens + size]

    return pl.pallas_call(
        kernel,
        in_specs=[whole()] * 2,
        out_specs=[whole()] * len(geo.sizes),
        out_shape=[jax.ShapeDtypeStruct((count, size, width), jnp.bfloat16) for size in geo.sizes],
        compiler_params=params(),
        name="borders",
    )(geo.select, x)


def exchange(geo, messages):
    return [geo.permute(piece, message) for piece, message in zip(geo.pieces, messages)]


def gather_copies(geo, parts, first, target, sems):
    places = [(0, geo.tokens)] + list(zip(geo.offsets, geo.sizes))
    return [
        pltpu.make_async_copy(
            part.at[pl.ds(first, 2)], target.at[:, pl.ds(offset, size)], sems.at[number]
        )
        for number, (part, (offset, size)) in enumerate(zip(parts, places))
    ]


def clear_tail(geo, wide, slots):
    if geo.wide > geo.used:
        tail = jnp.zeros((geo.wide - geo.used, wide.shape[-1]), jnp.bfloat16)
        for slot in slots:
            for a in range(2):
                wide[slot, a, geo.used :, :] = tail


def forward(geo, info, blocks, heads, own, slots):
    tokens, wide_rows = geo.tokens, geo.wide
    width = own.shape[-1]
    depth = width // heads
    scale = LOG2E / math.sqrt(depth)
    per = 1 + len(geo.pieces)
    stat_rows = round_up(2 * heads, 8)

    def kernel(info_ref, gap_ref, frame_ref, select_ref, qg_ref, *refs):
        parts = [refs[n * per : (n + 1) * per] for n in range(blocks)]
        attended_ref, column_ref, packed_ref = refs[blocks * per : blocks * per + 3]
        wide, top_ref, total_ref, accum, sems = refs[blocks * per + 3 :]
        place = info_ref[0]
        for r in range(blocks):

            @pl.when(r <= place)
            def _():
                for copy in gather_copies(geo, parts[r], 0, wide.at[r], sems.at[r]):
                    copy.start()

        clear_tail(geo, wide, range(blocks))
        top_ref[...] = jnp.full(top_ref.shape, -jnp.inf, jnp.float32)
        total_ref[...] = jnp.zeros(total_ref.shape, jnp.float32)
        accum[...] = jnp.zeros(accum.shape, jnp.float32)
        for r in range(blocks):

            @pl.when(r <= place)
            def _():
                for copy in gather_copies(geo, parts[r], 0, wide.at[r], sems.at[r]):
                    copy.wait()

        def step(slot, carry):
            live = info_ref[1 + heads + slot]
            gap = jnp.where(frame_ref[...] < live, gap_ref[...], FAR)
            for h in range(heads):
                lanes = slice(h * depth, (h + 1) * depth)
                reach = info_ref[1 + h].astype(jnp.float32)
                score = dot_nt(qg_ref[0, :, lanes], wide[slot, 0, :, lanes]) * scale
                score = jnp.where(gap <= reach, score, -jnp.inf)
                top = top_ref[h]
                new_top = jnp.maximum(top, jnp.max(score, axis=1, keepdims=True))
                weight = jnp.exp2(score - new_top)
                fading = jnp.exp2(top - new_top)
                top_ref[h] = new_top
                total_ref[h] = total_ref[h] * fading + jnp.sum(weight, axis=1, keepdims=True)
                accum[:, lanes] = accum[:, lanes] * fading + dot_nn(
                    weight.astype(jnp.bfloat16), wide[slot, 1, :, lanes]
                )
            return carry

        lax.fori_loop(0, place + 1, step, 0)
        lane = lax.broadcasted_iota(jnp.int32, (tokens, 128), 1)
        column = jnp.zeros((tokens, 128), jnp.float32)
        for h in range(heads):
            lanes = slice(h * depth, (h + 1) * depth)
            total = total_ref[h]
            rounded = (accum[:, lanes] / total).astype(jnp.bfloat16).astype(jnp.float32)
            accum[:, lanes] = rounded
            log_total = top_ref[h] + jnp.log2(total)
            delta = jnp.sum(
                rounded * qg_ref[1, :, lanes].astype(jnp.float32), axis=1, keepdims=True
            )
            column = jnp.where(lane == h, log_total, column)
            column = jnp.where(lane == heads + h, delta, column)
        column_ref[...] = column
        for f, y, at in geo.groups():
            attended_ref[f, y] = accum[at : at + geo.tile_w, :].astype(jnp.bfloat16)
        packed = jnp.zeros((wide_rows, 128), jnp.float32)
        rest = column
        for _ in range(3):
            part = rest.astype(jnp.bfloat16)
            rest = rest - part.astype(jnp.float32)
            packed = packed + dot_nn(select_ref[...], part)
        packed_ref[...] = jnp.transpose(packed)[:stat_rows]

    flat = [ref for slot in slots for ref in slot]
    return pl.pallas_call(
        kernel,
        in_specs=[whole(pltpu.SMEM)] + [whole()] * 4 + [whole(pl.ANY)] * len(flat),
        out_specs=[whole()] * 3,
        out_shape=[
            jax.ShapeDtypeStruct((geo.frames, geo.tile_h, geo.tile_w, width), jnp.bfloat16),
            jax.ShapeDtypeStruct((tokens, 128), jnp.float32),
            jax.ShapeDtypeStruct((stat_rows, wide_rows), jnp.float32),
        ],
        scratch_shapes=[
            pltpu.VMEM((blocks, 2, wide_rows, width), jnp.bfloat16),
            pltpu.VMEM((heads, tokens, 1), jnp.float32),
            pltpu.VMEM((heads, tokens, 1), jnp.float32),
            pltpu.VMEM((tokens, width), jnp.float32),
            pltpu.SemaphoreType.DMA((blocks, per)),
        ],
        compiler_params=params(),
        name="forward",
    )(info, geo.gap, jnp.asarray(geo.frame)[None, :], geo.select, own[2:], *flat)


def backward(geo, info, blocks, heads, own, column, gathered, slots):
    tokens, wide_rows = geo.tokens, geo.wide
    width = own.shape[-1]
    depth = width // heads
    natural = 1.0 / math.sqrt(depth)
    scale = LOG2E * natural
    per = 1 + len(geo.pieces)
    stat_rows = gathered.shape[1]
    count = blocks + 1

    def kernel(info_ref, gap_ref, frame_ref, row_frame_ref, own_ref, column_ref, all_ref, *refs):
        parts = [refs[n * per : (n + 1) * per] for n in range(count)]
        outs = refs[count * per : count * per + 3]
        wide, accum, stats, sems = refs[count * per + 3 :]
        place = info_ref[0]
        copies = [
            gather_copies(geo, parts[n], 2 if n == blocks else 0, wide.at[n], sems.at[n])
            for n in range(count)
        ]
        for group in copies:
            for copy in group:
                copy.start()
        clear_tail(geo, wide, range(count))
        accum[...] = jnp.zeros(accum.shape, jnp.float32)
        lane = lax.broadcasted_iota(jnp.int32, (stat_rows, wide_rows), 1)
        base = 1 + heads + blocks
        for n in range(1, count):
            row = all_ref[info_ref[base + (n - 1) * per]]
            for number, offset in enumerate(geo.offsets):
                other = all_ref[info_ref[base + (n - 1) * per + number + 1]]
                row = jnp.where(lane >= offset, other, row)
            stats[n] = row
        for group in copies:
            for copy in group:
                copy.wait()

        def query_step(slot, carry):
            live = info_ref[1 + heads + slot]
            gap = jnp.where(frame_ref[...] < live, gap_ref[...], FAR)
            for h in range(heads):
                lanes = slice(h * depth, (h + 1) * depth)
                reach = info_ref[1 + h].astype(jnp.float32)
                log_total = column_ref[:, h : h + 1]
                delta = column_ref[:, heads + h : heads + h + 1]
                key = wide[slot, 0, :, lanes]
                score = dot_nt(own_ref[2, :, lanes], key) * scale - log_total
                prob = jnp.exp2(jnp.where(gap <= reach, score, -jnp.inf))
                push = dot_nt(own_ref[3, :, lanes], wide[slot, 1, :, lanes])
                slope = (prob * (push - delta)).astype(jnp.bfloat16)
                accum[0, :, lanes] += dot_nn(slope, key)
            return carry

        lax.fori_loop(0, place + 1, query_step, 0)
        key_gap = jnp.where(row_frame_ref[...] < info_ref[1 + heads], gap_ref[...], FAR)

        def key_step(slot, carry):
            for h in range(heads):
                lanes = slice(h * depth, (h + 1) * depth)
                reach = info_ref[1 + h].astype(jnp.float32)
                log_total = stats[slot, h : h + 1, :]
                delta = stats[slot, heads + h : heads + h + 1, :]
                query = wide[slot, 0, :, lanes]
                grad = wide[slot, 1, :, lanes]
                score = dot_nt(own_ref[0, :, lanes], query) * scale - log_total
                prob = jnp.exp2(jnp.where(key_gap <= reach, score, -jnp.inf))
                accum[2, :, lanes] += dot_nn(prob.astype(jnp.bfloat16), grad)
                push = dot_nt(own_ref[1, :, lanes], grad)
                slope = (prob * (push - delta)).astype(jnp.bfloat16)
                accum[1, :, lanes] += dot_nn(slope, query)
            return carry

        lax.fori_loop(place + 1, blocks + 1, key_step, 0)
        for number, factor in enumerate((natural, natural, None)):
            for f, y, at in geo.groups():
                value = accum[number, at : at + geo.tile_w, :]
                value = value if factor is None else value * factor
                outs[number][f, y] = value.astype(jnp.bfloat16)

    flat = [ref for slot in slots for ref in slot]
    final = jax.ShapeDtypeStruct((geo.frames, geo.tile_h, geo.tile_w, width), jnp.bfloat16)
    frame = jnp.asarray(geo.frame)
    return pl.pallas_call(
        kernel,
        in_specs=[whole(pltpu.SMEM)] + [whole()] * 6 + [whole(pl.ANY)] * len(flat),
        out_specs=[whole()] * 3,
        out_shape=[final] * 3,
        scratch_shapes=[
            pltpu.VMEM((count, 2, wide_rows, width), jnp.bfloat16),
            pltpu.VMEM((3, tokens, width), jnp.float32),
            pltpu.VMEM((count, stat_rows, wide_rows), jnp.float32),
            pltpu.SemaphoreType.DMA((count, per)),
        ],
        compiler_params=params(),
        name="backward",
    )(info, geo.gap, frame[None, :], frame[:tokens, None], own, column, gathered, *flat)


def shards(queries, cache_keys, cache_values, grad_attended, radius, frame_count, sizes):
    blocks, count_h, count_w = sizes
    frames, tile_h, tile_w, width = queries.shape[1:]
    heads = radius.shape[0]
    geo = Geometry(frames, tile_h, tile_w, count_h, count_w)
    place = lax.axis_index("span")
    at_h, at_w = lax.axis_index("ha"), lax.axis_index("wa")
    block_of = [jnp.mod(place - n, blocks) for n in range(blocks)]
    counts = jnp.take(frame_count, jnp.stack(block_of))
    sources = []
    for block in block_of[1:] + [place]:
        for row, col in [geo.own] + geo.pieces:
            near_h = jnp.clip(at_h + row.delta, 0, count_h - 1)
            near_w = jnp.clip(at_w + col.delta, 0, count_w - 1)
            sources.append((block * count_h + near_h) * count_w + near_w)
    info = jnp.concatenate([place[None], radius, counts, jnp.stack(sources)]).astype(jnp.int32)

    arrays = [x[0] for x in (cache_keys, cache_values, queries, grad_attended)]
    own, sends = tidy(geo, info, arrays, blocks)
    received = [
        lax.ppermute(x, "span", [(i, (i + n) % blocks) for i in range(blocks)])
        for n, x in enumerate(sends, 1)
    ]
    slots = [[own] + exchange(geo, borders(geo, own))]
    for x in received:
        slots.append([x] + exchange(geo, borders(geo, x)))
    attended, column, packed = forward(geo, info, blocks, heads, own, slots)
    gathered = lax.all_gather(packed, ("span", "ha", "wa"), axis=0)
    grads = backward(geo, info, blocks, heads, own, column, gathered, slots + [slots[0]])
    return tuple(x[None] for x in (attended, *grads))


def solution(mesh):
    placed = P("span", None, "ha", "wa", None)
    sizes = tuple(mesh.shape[name] for name in ("span", "ha", "wa"))
    return jax.shard_map(
        functools.partial(shards, sizes=sizes),
        mesh=mesh,
        in_specs=(placed,) * 4 + (P(), P()),
        out_specs=(placed,) * 4,
        check_vma=False,
    )
```

```python
import functools
import math

import jax
import jax.numpy as jnp
import ml_dtypes
import numpy as np
from jax import lax
from jax.experimental import pallas as pl
from jax.experimental.pallas import tpu as pltpu
from jax.sharding import PartitionSpec as P

RMAX = 2
FAR = 99.0
LOG2E = math.log2(math.e)
LANES = 128


def round_up(value, unit):
    return (value + unit - 1) // unit * unit


def dot_nt(a, b):
    return lax.dot_general(a, b, (((1,), (1,)), ((), ())), preferred_element_type=jnp.float32)


def dot_nn(a, b):
    return lax.dot_general(a, b, (((1,), (0,)), ((), ())), preferred_element_type=jnp.float32)


class Side:
    def __init__(self, kind, count, tile, variant):
        self.count = count
        self.swap = kind == "swap"
        if kind == "same":
            self.delta, self.start, self.length, self.send_start = 0, 0, tile, 0
        else:
            self.delta = 1 - 2 * variant if self.swap else kind
            send_up = (variant == 0) if self.swap else (kind < 0)
            self.length = RMAX
            self.start = tile if self.delta > 0 else -RMAX
            self.send_start = tile - RMAX if send_up else 0
        shift = 1 if self.swap else self.delta
        self.pairs = [((i + shift) % count, i) for i in range(count)]

    def place(self, index):
        delta = 1 - 2 * index if self.swap else self.delta
        other = index + delta
        inside = (other >= 0) & (other < self.count)
        return jnp.where(inside, other, index), inside


def sides(count, tile, variant):
    kinds = [] if count == 1 else ["swap"] if count == 2 else [-1, 1]
    return [Side(kind, count, tile, variant) for kind in ["same"] + kinds]


class Geometry:
    def __init__(self, frames, tile_h, tile_w, count_h, count_w):
        self.frames, self.tile_h, self.tile_w = frames, tile_h, tile_w
        self.count_h, self.count_w = count_h, count_w
        self.tokens = frames * tile_h * tile_w
        self.groups = frames * tile_w
        self.variants_h = 2 if count_h == 2 else 1
        self.variants_w = 2 if count_w == 2 else 1
        select, gaps = [], []
        for variant_h in range(self.variants_h):
            for variant_w in range(self.variants_w):
                one, gap = self.variant(variant_h, variant_w)
                select.append(one)
                gaps.append(gap)
        self.select = np.stack(select).astype(ml_dtypes.bfloat16)
        self.gap = np.stack(gaps).astype(np.float32)

    def variant(self, variant_h, variant_w):
        rows_of = sides(self.count_h, self.tile_h, variant_h)
        cols_of = sides(self.count_w, self.tile_w, variant_w)
        pieces = [(row, col) for col in cols_of for row in rows_of]
        own, rest = pieces[0], sorted(pieces[1:], key=lambda p: -p[0].length * p[1].length)
        sizes = [self.tokens]
        sizes += [round_up(r.length * self.frames * c.length, 16) for r, c in rest]
        offsets = np.cumsum([0] + sizes)
        self.pieces, self.sizes = rest, sizes[1:]
        self.offsets = [int(v) for v in offsets[1:-1]]
        self.used = int(offsets[-1])
        self.wide = round_up(self.used, LANES)
        index = np.full(self.wide, -1)
        rows = np.full(self.wide, 1000)
        cols = np.full(self.wide, 1000)
        frame = np.zeros(self.wide, np.int32)
        for at, (row, col) in zip(offsets, [own] + rest):
            count = self.frames * col.length * row.length
            span = slice(int(at), int(at) + count)
            ff, xx, yy = np.unravel_index(
                np.arange(count), (self.frames, col.length, row.length)
            )
            index[span] = (ff * self.tile_w + col.send_start + xx) * self.tile_h
            index[span] += row.send_start + yy
            rows[span] = row.start + yy
            cols[span] = col.start + xx
            frame[span] = ff
        self.frame = frame
        mine = slice(0, self.tokens)
        gap = np.maximum(
            np.abs(rows[mine][:, None] - rows[None, :]), np.abs(cols[mine][:, None] - cols[None, :])
        )
        select = index[:, None] == np.arange(self.tokens)[None, :]
        return select, np.minimum(gap, FAR)

    def which(self):
        at_h = lax.axis_index("ha") if self.variants_h == 2 else 0
        at_w = lax.axis_index("wa") if self.variants_w == 2 else 0
        return at_h * self.variants_w + at_w

    def near(self, gap_ref):
        lane = lax.broadcasted_iota(jnp.int32, (1, self.wide), 1)
        far = jnp.zeros((1, self.wide), jnp.float32)
        for (row, col), offset, size in zip(self.pieces, self.offsets, self.sizes):
            inside = row.place(lax.axis_index("ha"))[1] & col.place(lax.axis_index("wa"))[1]
            cost = jnp.where(inside, 0.0, FAR)
            far = jnp.where((lane >= offset) & (lane < offset + size), cost, far)
        return gap_ref[self.which()] + far

    def permute(self, piece, x):
        row, col = piece
        pairs = [
            (a * self.count_w + c, b * self.count_w + d)
            for a, b in row.pairs
            for c, d in col.pairs
        ]
        return lax.ppermute(x, ("ha", "wa"), pairs)

    def exchange(self, messages):
        return [self.permute(piece, message) for piece, message in zip(self.pieces, messages)]


def whole(memory=pltpu.VMEM):
    return pl.BlockSpec(memory_space=memory)


def call(kernel, name, in_specs, out_specs, out_shape, scratch, mib, cost, aliases=None):
    return pl.pallas_call(
        kernel,
        in_specs=in_specs,
        out_specs=out_specs,
        out_shape=out_shape,
        scratch_shapes=scratch,
        compiler_params=pltpu.CompilerParams(vmem_limit_bytes=mib * 1024 * 1024),
        cost_estimate=pl.CostEstimate(
            flops=int(cost * 1e9), bytes_accessed=int(cost * 2e6), transcendentals=0
        ),
        input_output_aliases=aliases or {},
        name=name,
    )


def tidy(geo, arrays, blocks):
    width = arrays[0].shape[-1]
    tokens, tile_h = geo.tokens, geo.tile_h

    def kernel(*refs):
        ins, own_ref, sends = refs[:4], refs[4], refs[5 : 4 + blocks]
        compact, sems = refs[4 + blocks], refs[5 + blocks]
        for number, ref in enumerate(ins):
            for group in range(geo.groups):
                compact[number, group * tile_h : (group + 1) * tile_h, :] = ref[group]
        place = lax.axis_index("span")
        copies = []
        for r in range(1, blocks):
            first = jnp.where(place + r < blocks, 0, 2)
            copies.append(
                pltpu.make_async_copy(compact.at[pl.ds(first, 2)], sends[r - 1], sems.at[r])
            )
        copies.append(pltpu.make_async_copy(compact, own_ref, sems.at[0]))
        for copy in copies:
            copy.start()
        for copy in copies:
            copy.wait()

    out = call(
        kernel,
        "tidy",
        [whole()] * 4,
        [whole(pl.ANY)] * blocks,
        [jax.ShapeDtypeStruct((4, tokens, width), jnp.bfloat16)]
        + [jax.ShapeDtypeStruct((2, tokens, width), jnp.bfloat16)] * (blocks - 1),
        [pltpu.VMEM((4, tokens, width), jnp.bfloat16), pltpu.SemaphoreType.DMA((blocks,))],
        12,
        2,
    )(*arrays)
    return out[0], out[1:]


def borders(geo, x):
    count, tokens, width = x.shape
    select = geo.select[:, tokens : geo.used]

    def kernel(select_ref, x_ref, *outs):
        chosen = select_ref[geo.which()]
        for a in range(count):
            picked = dot_nn(chosen, x_ref[a]).astype(jnp.bfloat16)
            for out, size, offset in zip(outs, geo.sizes, geo.offsets):
                out[a] = picked[offset - tokens : offset - tokens + size]

    return call(
        kernel,
        "borders",
        [whole()] * 2,
        [whole()] * len(geo.sizes),
        [jax.ShapeDtypeStruct((count, size, width), jnp.bfloat16) for size in geo.sizes],
        [],
        12,
        2,
    )(select, x)


def spread_copies(geo, parts, first, target, sems):
    places = [(0, geo.tokens)] + list(zip(geo.offsets, geo.sizes))
    return [
        pltpu.make_async_copy(
            part.at[pl.ds(first, 2)], target.at[:, pl.ds(offset, size)], sems.at[number]
        )
        for number, (part, (offset, size)) in enumerate(zip(parts, places))
    ]


def clear_tail(geo, wide):
    if geo.wide > geo.used:
        tail = jnp.zeros((geo.wide - geo.used, wide.shape[-1]), jnp.bfloat16)
        for slot in range(wide.shape[0]):
            for a in range(2):
                wide[slot, a, geo.used :, :] = tail


def set_bias(bias_ref, gap):
    for reach in range(1, RMAX + 1):
        bias_ref[reach - 1] = jnp.where(gap <= reach, 0.0, -jnp.inf)


def forward(geo, blocks, heads, small, own, slot, parts, state):
    tokens, wide_rows = geo.tokens, geo.wide
    width = own.shape[-1]
    depth = width // heads
    scale = LOG2E / math.sqrt(depth)
    per = len(parts)
    stat_rows = round_up(2 * heads, 8)
    first, last = slot == 0, slot == blocks - 1
    lanes = [slice(h * depth, (h + 1) * depth) for h in range(heads)]

    def kernel(radius_ref, live_ref, gap_ref, frame_ref, select_ref, own_ref, *refs):
        parts_refs, refs = refs[:per], refs[per:]
        state_in, refs = (None, refs) if first else (refs[0], refs[1:])
        outs, refs = (refs[:3], refs[3:]) if last else (refs[:1], refs[1:])
        wide, qg, held, bias_ref, sems = refs
        place = lax.axis_index("span")
        active = slot <= place
        spread = spread_copies(geo, parts_refs, 0, wide.at[0], sems)
        common = [pltpu.make_async_copy(own_ref.at[pl.ds(2, 2)], qg, sems.at[per])]
        if not first:
            common.append(pltpu.make_async_copy(state_in, held, sems.at[per + 1]))
        lane = lax.broadcasted_iota(jnp.int32, (tokens, LANES), 1)

        def begin(copies):
            for copy in copies:
                copy.start()

        def end(copies):
            for copy in copies:
                copy.wait()

        def prepare():
            live = live_ref[lax.rem(place - slot + blocks, blocks)]
            set_bias(bias_ref, jnp.where(frame_ref[...] < live, geo.near(gap_ref), FAR))
            clear_tail(geo, wide)

        def attend():
            column = held[:, width:]
            ahead = dot_nt(qg[0, :, lanes[0]], wide[0, 0, :, lanes[0]])
            for h in range(heads):
                score = ahead
                if h + 1 < heads:
                    ahead = dot_nt(qg[0, :, lanes[h + 1]], wide[0, 0, :, lanes[h + 1]])
                score = score * scale + bias_ref[radius_ref[h] - 1]
                top = column[:, h : h + 1]
                new_top = jnp.maximum(top, jnp.max(score, axis=1, keepdims=True))
                weight = jnp.exp2(score - new_top)
                fading = jnp.exp2(top - new_top)
                total = column[:, heads + h : heads + h + 1] * fading
                total = total + jnp.sum(weight, axis=1, keepdims=True)
                column = jnp.where(lane == h, new_top, column)
                column = jnp.where(lane == heads + h, total, column)
                held[:, lanes[h]] = held[:, lanes[h]] * fading + dot_nn(
                    weight.astype(jnp.bfloat16), wide[0, 1, :, lanes[h]]
                )
            held[:, width:] = column

        def finish():
            attended_ref, column_ref, packed_ref = outs
            column = jnp.zeros((tokens, LANES), jnp.float32)
            stats = held[:, width:]
            for h in range(heads):
                total = stats[:, heads + h : heads + h + 1]
                rounded = (held[:, lanes[h]] / total).astype(jnp.bfloat16).astype(jnp.float32)
                held[:, lanes[h]] = rounded
                log_total = stats[:, h : h + 1] + jnp.log2(total)
                grad = qg[1, :, lanes[h]].astype(jnp.float32)
                delta = jnp.sum(rounded * grad, axis=1, keepdims=True)
                column = jnp.where(lane == h, log_total, column)
                column = jnp.where(lane == heads + h, delta, column)
            column_ref[...] = column
            packed = jnp.zeros((wide_rows, LANES), jnp.float32)
            rest = column
            chosen = select_ref[geo.which()]
            for _ in range(3):
                part = rest.astype(jnp.bfloat16)
                rest = rest - part.astype(jnp.float32)
                packed = packed + dot_nn(chosen, part)
            packed_ref[...] = jnp.transpose(packed)[:stat_rows]
            for group in range(geo.groups):
                at = slice(group * geo.tile_h, (group + 1) * geo.tile_h)
                attended_ref[group] = held[at, :width].astype(jnp.bfloat16)

        if first:
            held[:, :width] = jnp.zeros((tokens, width), jnp.float32)
            held[:, width:] = jnp.where(lane < heads, -jnp.inf, 0.0)
        if last:
            begin(common)

            @pl.when(active)
            def _():
                begin(spread)
                prepare()

            end(common)

            @pl.when(active)
            def _():
                end(spread)
                attend()

            finish()
        else:

            @pl.when(active)
            def _():
                begin(spread + common)
                prepare()
                end(spread + common)
                attend()
                store = pltpu.make_async_copy(held, outs[0], sems.at[per + 2])
                store.start()
                store.wait()

    ins = [*small, geo.gap, geo.frame[None, :], geo.select, own, *parts]
    specs = [whole(pltpu.SMEM)] * 2 + [whole()] * 3 + [whole(pl.ANY)] * (1 + per)
    aliases = {}
    held_shape = jax.ShapeDtypeStruct((tokens, width + LANES), jnp.float32)
    if not first:
        if not last:
            aliases = {len(ins): 0}
        ins.append(state)
        specs.append(whole(pl.ANY))
    shapes = [held_shape]
    if last:
        shapes = [
            jax.ShapeDtypeStruct((geo.groups, geo.tile_h, width), jnp.bfloat16),
            jax.ShapeDtypeStruct((tokens, LANES), jnp.float32),
            jax.ShapeDtypeStruct((stat_rows, wide_rows), jnp.float32),
        ]
    return call(
        kernel,
        "forward",
        specs,
        [whole()] * 3 if last else [whole(pl.ANY)],
        shapes,
        [
            pltpu.VMEM((1, 2, wide_rows, width), jnp.bfloat16),
            pltpu.VMEM((2, tokens, width), jnp.bfloat16),
            pltpu.VMEM((tokens, width + LANES), jnp.float32),
            pltpu.VMEM((RMAX, tokens, wide_rows), jnp.float32),
            pltpu.SemaphoreType.DMA((per + 3,)),
        ],
        16,
        3,
        aliases,
    )(*ins)


def merge(geo, pieces):
    def kernel(*refs):
        out = refs[-1]
        row = refs[0][...]
        lane = lax.broadcasted_iota(jnp.int32, row.shape, 1)
        for ref, offset in zip(refs[1:-1], geo.offsets):
            row = jnp.where(lane >= offset, ref[...], row)
        out[...] = row

    return call(
        kernel,
        "merge",
        [whole()] * len(pieces),
        whole(),
        jax.ShapeDtypeStruct(pieces[0].shape, jnp.float32),
        [],
        4,
        1,
    )(*pieces)


def query_grads(geo, blocks, heads, small, own, column, slots):
    tokens, wide_rows = geo.tokens, geo.wide
    width = own.shape[-1]
    depth = width // heads
    natural = 1.0 / math.sqrt(depth)
    scale = LOG2E * natural
    per = len(slots[0])
    lanes = [slice(h * depth, (h + 1) * depth) for h in range(heads)]

    def kernel(radius_ref, live_ref, gap_ref, frame_ref, column_ref, own_ref, *refs):
        parts, refs = refs[: blocks * per], refs[blocks * per :]
        out, wide, qg, accum, bias_ref, sems = refs
        place = lax.axis_index("span")
        load = pltpu.make_async_copy(own_ref.at[pl.ds(2, 2)], qg, sems.at[blocks, 0])
        spreads = [
            spread_copies(geo, parts[n * per : (n + 1) * per], 0, wide.at[n], sems.at[n])
            for n in range(blocks)
        ]
        load.start()
        for n in range(blocks):

            @pl.when(n <= place)
            def _():
                for copy in spreads[n]:
                    copy.start()

        clear_tail(geo, wide)
        accum[...] = jnp.zeros(accum.shape, jnp.float32)
        near = geo.near(gap_ref)
        load.wait()
        for n in range(blocks):

            @pl.when(n <= place)
            def _():
                for copy in spreads[n]:
                    copy.wait()

        def step(slot, carry):
            live = live_ref[lax.rem(place - slot + blocks, blocks)]
            set_bias(bias_ref, jnp.where(frame_ref[...] < live, near, FAR))

            def products(h):
                return (
                    dot_nt(qg[0, :, lanes[h]], wide[slot, 0, :, lanes[h]]),
                    dot_nt(qg[1, :, lanes[h]], wide[slot, 1, :, lanes[h]]),
                )

            ahead = products(0)
            for h in range(heads):
                score, push = ahead
                if h + 1 < heads:
                    ahead = products(h + 1)
                score = score * scale + bias_ref[radius_ref[h] - 1]
                prob = jnp.exp2(score - column_ref[:, h : h + 1])
                slope = prob * (push - column_ref[:, heads + h : heads + h + 1])
                accum[:, lanes[h]] += dot_nn(
                    slope.astype(jnp.bfloat16), wide[slot, 0, :, lanes[h]]
                )
            return carry

        lax.fori_loop(0, place + 1, step, 0)
        for group in range(geo.groups):
            at = slice(group * geo.tile_h, (group + 1) * geo.tile_h)
            out[group] = (accum[at, :] * natural).astype(jnp.bfloat16)

    flat = [part for slot in slots for part in slot]
    return call(
        kernel,
        "query_grads",
        [whole(pltpu.SMEM)] * 2 + [whole()] * 3 + [whole(pl.ANY)] * (1 + len(flat)),
        whole(),
        jax.ShapeDtypeStruct((geo.groups, geo.tile_h, width), jnp.bfloat16),
        [
            pltpu.VMEM((blocks, 2, wide_rows, width), jnp.bfloat16),
            pltpu.VMEM((2, tokens, width), jnp.bfloat16),
            pltpu.VMEM((tokens, width), jnp.float32),
            pltpu.VMEM((RMAX, tokens, wide_rows), jnp.float32),
            pltpu.SemaphoreType.DMA((blocks + 1, per)),
        ],
        8 + 3 * blocks,
        6,
    )(*small, geo.gap, geo.frame[None, :], column, own, *flat)


def key_grads(geo, blocks, heads, small, own, stats, slots):
    tokens, wide_rows = geo.tokens, geo.wide
    width = own.shape[-1]
    depth = width // heads
    natural = 1.0 / math.sqrt(depth)
    scale = LOG2E * natural
    per = len(slots[0])
    stat_rows = stats[0].shape[0]
    lanes = [slice(h * depth, (h + 1) * depth) for h in range(heads)]

    def kernel(radius_ref, live_ref, gap_ref, frame_ref, own_ref, *refs):
        parts, refs = refs[: blocks * per], refs[blocks * per :]
        stat_refs, refs = refs[:blocks], refs[blocks:]
        outs, refs = refs[:2], refs[2:]
        wide, kv, rows, accum, bias_ref, sems = refs
        place = lax.axis_index("span")
        loads = [pltpu.make_async_copy(own_ref.at[pl.ds(0, 2)], kv, sems.at[blocks, 0])]
        for n in range(blocks):
            loads += spread_copies(
                geo,
                parts[n * per : (n + 1) * per],
                2 if n == 0 else 0,
                wide.at[n],
                sems.at[n],
            )
        for copy in loads:
            copy.start()
        clear_tail(geo, wide)
        accum[...] = jnp.zeros(accum.shape, jnp.float32)
        for n in range(blocks):
            rows[n] = stat_refs[n][...]
        live = frame_ref[...] < live_ref[place]
        set_bias(bias_ref, jnp.where(live, geo.near(gap_ref), FAR))
        for copy in loads:
            copy.wait()

        def step(count, carry):
            slot = jnp.where(count == place, 0, count)

            def products(h):
                return (
                    dot_nt(kv[0, :, lanes[h]], wide[slot, 0, :, lanes[h]]),
                    dot_nt(kv[1, :, lanes[h]], wide[slot, 1, :, lanes[h]]),
                )

            ahead = products(0)
            for h in range(heads):
                score, push = ahead
                if h + 1 < heads:
                    ahead = products(h + 1)
                score = score * scale + bias_ref[radius_ref[h] - 1]
                prob = jnp.exp2(score - rows[slot, h : h + 1, :])
                accum[1, :, lanes[h]] += dot_nn(
                    prob.astype(jnp.bfloat16), wide[slot, 1, :, lanes[h]]
                )
                slope = prob * (push - rows[slot, heads + h : heads + h + 1, :])
                accum[0, :, lanes[h]] += dot_nn(
                    slope.astype(jnp.bfloat16), wide[slot, 0, :, lanes[h]]
                )
            return carry

        lax.fori_loop(place, blocks, step, 0)
        for group in range(geo.groups):
            at = slice(group * geo.tile_h, (group + 1) * geo.tile_h)
            outs[0][group] = (accum[0, at, :] * natural).astype(jnp.bfloat16)
            outs[1][group] = accum[1, at, :].astype(jnp.bfloat16)

    flat = [part for slot in slots for part in slot]
    final = jax.ShapeDtypeStruct((geo.groups, geo.tile_h, width), jnp.bfloat16)
    frame = np.broadcast_to(geo.frame[: geo.tokens, None], (tokens, LANES))[:, :1]
    return call(
        kernel,
        "key_grads",
        [whole(pltpu.SMEM)] * 2
        + [whole()] * 2
        + [whole(pl.ANY)] * (1 + len(flat))
        + [whole()] * blocks,
        [whole()] * 2,
        [final] * 2,
        [
            pltpu.VMEM((blocks, 2, wide_rows, width), jnp.bfloat16),
            pltpu.VMEM((2, tokens, width), jnp.bfloat16),
            pltpu.VMEM((blocks, stat_rows, wide_rows), jnp.float32),
            pltpu.VMEM((2, tokens, width), jnp.float32),
            pltpu.VMEM((RMAX, tokens, wide_rows), jnp.float32),
            pltpu.SemaphoreType.DMA((blocks + 1, per)),
        ],
        10 + 3 * blocks,
        6,
    )(*small, geo.gap, frame, own, *flat, *stats)


def rotate(x, by, blocks):
    return lax.ppermute(x, "span", [(i, (i + by) % blocks) for i in range(blocks)])


def shards(queries, cache_keys, cache_values, grad_attended, radius, frame_count, sizes):
    blocks, count_h, count_w = sizes
    frames, tile_h, tile_w, width = queries.shape[1:]
    heads = radius.shape[0]
    geo = Geometry(frames, tile_h, tile_w, count_h, count_w)
    small = (radius, frame_count)

    def grouped(x):
        return jnp.transpose(x[0], (0, 2, 1, 3)).reshape(geo.groups, tile_h, width)

    def restored(x):
        x = x.reshape(frames, tile_w, tile_h, width)
        return jnp.transpose(x, (0, 2, 1, 3))[None]

    arrays = [grouped(x) for x in (cache_keys, cache_values, queries, grad_attended)]
    own, sends = tidy(geo, arrays, blocks)
    received = [own] + [rotate(x, n, blocks) for n, x in enumerate(sends, 1)]
    slots, state = [], None
    for n, x in enumerate(received):
        slots.append([x] + geo.exchange(borders(geo, x)))
        state = forward(geo, blocks, heads, small, own, n, slots[n], state)
        if n < blocks - 1:
            state = state[0]
    attended, column, packed = state
    own_stats = merge(geo, [packed] + geo.exchange([packed] * len(geo.pieces)))
    stats = [own_stats] + [rotate(own_stats, n, blocks) for n in range(1, blocks)]
    grad_q = query_grads(geo, blocks, heads, small, own, column, slots)
    grad_k, grad_v = key_grads(geo, blocks, heads, small, own, stats, slots)
    return tuple(restored(x) for x in (attended, grad_q, grad_k, grad_v))


def solution(mesh):
    placed = P("span", None, "ha", "wa", None)
    sizes = tuple(mesh.shape[name] for name in ("span", "ha", "wa"))
    return jax.shard_map(
        functools.partial(shards, sizes=sizes),
        mesh=mesh,
        in_specs=(placed,) * 4 + (P(), P()),
        out_specs=(placed,) * 4,
        check_vma=False,
    )
```

```python
import functools
import math

import jax
import jax.numpy as jnp
import ml_dtypes
import numpy as np
from jax import lax
from jax.experimental import pallas as pl
from jax.experimental.pallas import tpu as pltpu
from jax.sharding import PartitionSpec as P

RMAX = 2
FAR = 99.0
LOG2E = math.log2(math.e)
LANES = 128


def round_up(value, unit):
    return (value + unit - 1) // unit * unit


def dot_nt(a, b):
    return lax.dot_general(a, b, (((1,), (1,)), ((), ())), preferred_element_type=jnp.float32)


def dot_nn(a, b):
    return lax.dot_general(a, b, (((1,), (0,)), ((), ())), preferred_element_type=jnp.float32)


class Side:
    def __init__(self, kind, count, tile, variant):
        self.count = count
        self.swap = kind == "swap"
        if kind == "same":
            self.delta, self.start, self.length, self.send_start = 0, 0, tile, 0
        else:
            self.delta = 1 - 2 * variant if self.swap else kind
            send_up = (variant == 0) if self.swap else (kind < 0)
            self.length = RMAX
            self.start = tile if self.delta > 0 else -RMAX
            self.send_start = tile - RMAX if send_up else 0
        shift = 1 if self.swap else self.delta
        self.pairs = [((i + shift) % count, i) for i in range(count)]

    def place(self, index):
        delta = 1 - 2 * index if self.swap else self.delta
        other = index + delta
        inside = (other >= 0) & (other < self.count)
        return jnp.where(inside, other, index), inside


def sides(count, tile, variant):
    kinds = [] if count == 1 else ["swap"] if count == 2 else [-1, 1]
    return [Side(kind, count, tile, variant) for kind in ["same"] + kinds]


class Geometry:
    def __init__(self, frames, tile_h, tile_w, count_h, count_w):
        self.frames, self.tile_h, self.tile_w = frames, tile_h, tile_w
        self.count_h, self.count_w = count_h, count_w
        self.tokens = frames * tile_h * tile_w
        self.groups = frames * tile_w
        self.variants_h = 2 if count_h == 2 else 1
        self.variants_w = 2 if count_w == 2 else 1
        select, gaps = [], []
        for variant_h in range(self.variants_h):
            for variant_w in range(self.variants_w):
                one, gap = self.variant(variant_h, variant_w)
                select.append(one)
                gaps.append(gap)
        self.select = np.stack(select).astype(ml_dtypes.bfloat16)
        self.gap = np.stack(gaps).astype(np.float32)

    def variant(self, variant_h, variant_w):
        rows_of = sides(self.count_h, self.tile_h, variant_h)
        cols_of = sides(self.count_w, self.tile_w, variant_w)
        pieces = [(row, col) for col in cols_of for row in rows_of]
        own, rest = pieces[0], sorted(pieces[1:], key=lambda p: -p[0].length * p[1].length)
        sizes = [self.tokens]
        sizes += [round_up(r.length * self.frames * c.length, 16) for r, c in rest]
        offsets = np.cumsum([0] + sizes)
        self.pieces, self.sizes = rest, sizes[1:]
        self.offsets = [int(v) for v in offsets[1:-1]]
        self.used = int(offsets[-1])
        self.wide = round_up(self.used, LANES)
        index = np.full(self.wide, -1)
        rows = np.full(self.wide, 1000)
        cols = np.full(self.wide, 1000)
        frame = np.zeros(self.wide, np.int32)
        for at, (row, col) in zip(offsets, [own] + rest):
            count = self.frames * col.length * row.length
            span = slice(int(at), int(at) + count)
            ff, xx, yy = np.unravel_index(
                np.arange(count), (self.frames, col.length, row.length)
            )
            index[span] = (ff * self.tile_w + col.send_start + xx) * self.tile_h
            index[span] += row.send_start + yy
            rows[span] = row.start + yy
            cols[span] = col.start + xx
            frame[span] = ff
        self.frame = frame
        mine = slice(0, self.tokens)
        gap = np.maximum(
            np.abs(rows[mine][:, None] - rows[None, :]), np.abs(cols[mine][:, None] - cols[None, :])
        )
        select = index[:, None] == np.arange(self.tokens)[None, :]
        return select, np.minimum(gap, FAR)

    def which(self):
        at_h = lax.axis_index("ha") if self.variants_h == 2 else 0
        at_w = lax.axis_index("wa") if self.variants_w == 2 else 0
        return at_h * self.variants_w + at_w

    def near(self, gap_ref):
        lane = lax.broadcasted_iota(jnp.int32, (1, self.wide), 1)
        far = jnp.zeros((1, self.wide), jnp.float32)
        for (row, col), offset, size in zip(self.pieces, self.offsets, self.sizes):
            inside = row.place(lax.axis_index("ha"))[1] & col.place(lax.axis_index("wa"))[1]
            cost = jnp.where(inside, 0.0, FAR)
            far = jnp.where((lane >= offset) & (lane < offset + size), cost, far)
        return gap_ref[self.which()] + far

    def permute(self, piece, x):
        row, col = piece
        pairs = [
            (a * self.count_w + c, b * self.count_w + d)
            for a, b in row.pairs
            for c, d in col.pairs
        ]
        return lax.ppermute(x, ("ha", "wa"), pairs)

    def exchange(self, messages):
        return [self.permute(piece, message) for piece, message in zip(self.pieces, messages)]


def whole(memory=pltpu.VMEM):
    return pl.BlockSpec(memory_space=memory)


def call(kernel, name, in_specs, out_specs, out_shape, scratch, mib, cost, aliases=None):
    return pl.pallas_call(
        kernel,
        in_specs=in_specs,
        out_specs=out_specs,
        out_shape=out_shape,
        scratch_shapes=scratch,
        compiler_params=pltpu.CompilerParams(vmem_limit_bytes=mib * 1024 * 1024),
        cost_estimate=pl.CostEstimate(
            flops=int(cost * 1e9), bytes_accessed=int(cost * 2e6), transcendentals=0
        ),
        input_output_aliases=aliases or {},
        name=name,
    )


def pick(table, place):
    value = jnp.int32(table[0])
    for index, entry in enumerate(table[1:], 1):
        if entry != table[0]:
            value = jnp.where(place == index, entry, value)
    return value


def relay(blocks):
    held = [[(s, (s % 2 == 0) != bool(chain)) for s in range(blocks)] for chain in range(2)]
    fresh = [[] for _ in range(blocks)]
    for number in range(1, blocks):
        for chain in range(2):
            moved = [held[chain][a] for a in swap(blocks, chain, number)]
            held[chain] = moved
            for s, (block, keys) in enumerate(moved):
                if block != s and keys == (block < s) and block not in [b for _, b in fresh[s]]:
                    fresh[s].append(((chain, number), block))
    batches = []
    for n in range(blocks - 1):
        steps = sorted({fresh[s][n][0] for s in range(blocks)}, key=lambda step: step[::-1])
        which = [steps.index(fresh[s][n][0]) for s in range(blocks)]
        batches.append((steps, which, [fresh[s][n][1] for s in range(blocks)]))
    return batches


def swap(blocks, chain, number):
    start = (chain + number + 1) % 2
    partner = list(range(blocks))
    for low in range(start, blocks - 1, 2):
        partner[low], partner[low + 1] = low + 1, low
    return partner


def tidy(geo, arrays, blocks):
    width = arrays[0].shape[-1]
    tokens, tile_h = geo.tokens, geo.tile_h

    def kernel(*refs):
        ins, (own_ref, even_ref, odd_ref, stage, sems) = refs[:4], refs[4:]
        copies = [
            pltpu.make_async_copy(ref, stage.at[number], sems.at[number])
            for number, ref in enumerate(ins)
        ]
        for copy in copies:
            copy.start()
        for number, copy in enumerate(copies):
            copy.wait()
            for group in range(geo.groups):
                own_ref[number, group * tile_h : (group + 1) * tile_h, :] = stage[number, group]
        odd = lax.rem(lax.axis_index("span"), 2)
        even_ref[...] = own_ref[pl.ds(2 * odd, 2)]
        odd_ref[...] = own_ref[pl.ds(2 - 2 * odd, 2)]

    pair = jax.ShapeDtypeStruct((2, tokens, width), jnp.bfloat16)
    return call(
        kernel,
        "tidy",
        [whole(pltpu.HBM)] * 4,
        [whole()] * 3,
        [jax.ShapeDtypeStruct((4, tokens, width), jnp.bfloat16), pair, pair],
        [
            pltpu.VMEM((4, geo.groups, tile_h, width), jnp.bfloat16),
            pltpu.SemaphoreType.DMA((4,)),
        ],
        12,
        2,
    )(*arrays)


def borders(geo, which, candidates):
    count, tokens, width = candidates[0].shape
    select = geo.select[:, tokens : geo.used]
    several = len(candidates) > 1

    def kernel(select_ref, *refs):
        ins, outs = refs[: len(candidates)], refs[len(candidates) :]
        chosen = select_ref[geo.which()]
        pieces = outs[1:] if several else outs
        number = pick(which, lax.axis_index("span"))

        def work(x_ref):
            for a in range(count):
                x = x_ref[a]
                if several:
                    outs[0][a] = x
                picked = dot_nn(chosen, x).astype(jnp.bfloat16)
                for out, size, offset in zip(pieces, geo.sizes, geo.offsets):
                    out[a] = picked[offset - tokens : offset - tokens + size]

        if not several:
            work(ins[0])
            return
        for index, ref in enumerate(ins):
            pl.when(number == index)(functools.partial(work, ref))

    sizes = ([tokens] if several else []) + geo.sizes
    out = call(
        kernel,
        "borders",
        [whole()] * (1 + len(candidates)),
        [whole()] * len(sizes),
        [jax.ShapeDtypeStruct((count, size, width), jnp.bfloat16) for size in sizes],
        [],
        12,
        1,
    )(select, *candidates)
    return (out[0], out[1:]) if several else (candidates[0], out)


def set_bias(bias_ref, gap):
    for reach in range(1, RMAX + 1):
        bias_ref[reach - 1] = jnp.where(gap <= reach, 0.0, -jnp.inf)


def fit(x, lanes):
    return x if x.shape[1] == lanes else jnp.broadcast_to(x[:, :1], (x.shape[0], lanes))


def repeat(x, lanes):
    return jnp.concatenate([x] * (lanes // LANES), axis=1)


def forward(geo, blocks, heads, small, own, sources, parts, state, last):
    tokens, wide_rows = geo.tokens, geo.wide
    count, _, width = parts[0].shape
    depth = width // heads
    scale = LOG2E / math.sqrt(depth)
    per = len(parts)
    stat_rows = round_up(2 * heads, 8)
    first = state is None
    lanes = [slice(h * depth, (h + 1) * depth) for h in range(heads)]

    def kernel(radius_ref, live_ref, gap_ref, frame_ref, select_ref, own_ref, *refs):
        parts_refs, refs = refs[:per], refs[per:]
        state_in, refs = (None, refs) if first else (refs[:3], refs[3:])
        wide, refs = refs[0], refs[1:]
        if last:
            outs, (accum, top, total, bias_ref) = refs[:4], refs[4:]
        else:
            accum, top, total, bias_ref = refs
        place = lax.axis_index("span")
        source = place if first else pick(sources, place)
        active = source <= place

        for a in range(count):
            wide[a, :tokens] = parts_refs[0][a]
            for ref, offset, size in zip(parts_refs[1:], geo.offsets, geo.sizes):
                wide[a, offset : offset + size] = ref[a]
            if wide_rows > geo.used:
                wide[a, geo.used :] = jnp.zeros((wide_rows - geo.used, width), jnp.bfloat16)
        if first:
            accum[...] = jnp.zeros(accum.shape, jnp.float32)
            top[...] = jnp.full(top.shape, -jnp.inf, jnp.float32)
            total[...] = jnp.zeros(total.shape, jnp.float32)
        else:
            for old, new in zip(state_in, (accum, top, total)):
                new[...] = old[...]

        def attend():
            live = live_ref[source]
            set_bias(bias_ref, jnp.where(frame_ref[...] < live, geo.near(gap_ref), FAR))
            ones = jnp.ones((wide_rows, LANES), jnp.bfloat16)
            ahead = dot_nt(own_ref[2, :, lanes[0]], wide[0, :, lanes[0]])
            for h in range(heads):
                score = ahead
                if h + 1 < heads:
                    ahead = dot_nt(own_ref[2, :, lanes[h + 1]], wide[0, :, lanes[h + 1]])
                score = score * scale + bias_ref[radius_ref[h] - 1]
                best = jnp.max(score, axis=1, keepdims=True)
                new_top = jnp.maximum(top[h], best)
                fading = jnp.exp2(top[h] - new_top)
                top[h] = new_top
                weight = jnp.exp2(score - repeat(new_top, wide_rows)).astype(jnp.bfloat16)
                value = jnp.concatenate([wide[1, :, lanes[h]], ones], axis=1)
                both = dot_nn(weight, value)
                accum[:, lanes[h]] = accum[:, lanes[h]] * fit(fading, depth) + both[:, :depth]
                total[h] = total[h] * fading + both[:, depth:]

        def finish():
            attended_ref, lse_ref, delta_ref, packed_ref = outs
            lane = lax.broadcasted_iota(jnp.int32, (tokens, LANES), 1)
            column = jnp.zeros((tokens, LANES), jnp.float32)
            for h in range(heads):
                rounded = (accum[:, lanes[h]] / fit(total[h], depth)).astype(jnp.bfloat16)
                rounded = rounded.astype(jnp.float32)
                accum[:, lanes[h]] = rounded
                lse = top[h] + jnp.log2(total[h])
                grad = own_ref[3, :, lanes[h]].astype(jnp.float32)
                delta = jnp.sum(rounded * grad, axis=1, keepdims=True)
                delta = jnp.broadcast_to(delta, (tokens, LANES))
                lse_ref[h] = lse
                delta_ref[h] = delta
                column = jnp.where(lane == h, lse, column)
                column = jnp.where(lane == heads + h, delta, column)
            packed = jnp.zeros((wide_rows, LANES), jnp.float32)
            rest = column
            chosen = select_ref[geo.which()]
            for _ in range(3):
                part = rest.astype(jnp.bfloat16)
                rest = rest - part.astype(jnp.float32)
                packed = packed + dot_nn(chosen, part)
            packed_ref[...] = jnp.transpose(packed)[:stat_rows]
            for group in range(geo.groups):
                at = slice(group * geo.tile_h, (group + 1) * geo.tile_h)
                attended_ref[group] = accum[at, :].astype(jnp.bfloat16)

        if first:
            attend()
        else:
            pl.when(active)(attend)
        if last:
            finish()

    ins = [*small, geo.gap, geo.frame[None, :], geo.select, own, *parts]
    ins += [] if first else list(state)
    stat = (heads, tokens, LANES)
    running = [(tokens, width), stat, stat]
    shapes = [jax.ShapeDtypeStruct((count, wide_rows, width), jnp.bfloat16)]
    scratch = []
    if last:
        shapes += [
            jax.ShapeDtypeStruct((geo.groups, geo.tile_h, width), jnp.bfloat16),
            jax.ShapeDtypeStruct(stat, jnp.float32),
            jax.ShapeDtypeStruct(stat, jnp.float32),
            jax.ShapeDtypeStruct((stat_rows, wide_rows), jnp.float32),
        ]
        scratch += [pltpu.VMEM(shape, jnp.float32) for shape in running]
    else:
        shapes += [jax.ShapeDtypeStruct(shape, jnp.float32) for shape in running]
    return call(
        kernel,
        "forward",
        [whole(pltpu.SMEM)] * 2 + [whole()] * (len(ins) - 2),
        [whole()] * len(shapes),
        shapes,
        scratch + [pltpu.VMEM((RMAX, tokens, wide_rows), jnp.float32)],
        20,
        3,
    )(*ins)


def merge(geo, pieces):
    def kernel(*refs):
        out = refs[-1]
        row = refs[0][...]
        lane = lax.broadcasted_iota(jnp.int32, row.shape, 1)
        for ref, offset in zip(refs[1:-1], geo.offsets):
            row = jnp.where(lane >= offset, ref[...], row)
        out[...] = row

    return call(
        kernel,
        "merge",
        [whole()] * len(pieces),
        whole(),
        jax.ShapeDtypeStruct(pieces[0].shape, jnp.float32),
        [],
        4,
        0.1,
    )(*pieces)


def query_grads(geo, heads, small, own, lse, delta, sources, wides):
    tokens, wide_rows = geo.tokens, geo.wide
    width = own.shape[-1]
    depth = width // heads
    natural = 1.0 / math.sqrt(depth)
    scale = LOG2E * natural
    lanes = [slice(h * depth, (h + 1) * depth) for h in range(heads)]

    def kernel(radius_ref, live_ref, gap_ref, frame_ref, lse_ref, delta_ref, own_ref, *refs):
        wide_refs, (out, accum, bias_ref) = refs[: len(wides)], refs[len(wides) :]
        place = lax.axis_index("span")
        accum[...] = jnp.zeros(accum.shape, jnp.float32)

        def step(wide, source):
            live = live_ref[source]
            set_bias(bias_ref, jnp.where(frame_ref[...] < live, geo.near(gap_ref), FAR))

            def products(h):
                return (
                    dot_nt(own_ref[2, :, lanes[h]], wide[0, :, lanes[h]]),
                    dot_nt(own_ref[3, :, lanes[h]], wide[1, :, lanes[h]]),
                )

            ahead = products(0)
            for h in range(heads):
                score, push = ahead
                if h + 1 < heads:
                    ahead = products(h + 1)
                score = score * scale + bias_ref[radius_ref[h] - 1]
                prob = jnp.exp2(score - repeat(lse_ref[h], wide_rows))
                slope = prob * (push - repeat(delta_ref[h], wide_rows))
                accum[:, lanes[h]] += dot_nn(slope.astype(jnp.bfloat16), wide[0, :, lanes[h]])

        step(wide_refs[0], place)
        for wide, table in zip(wide_refs[1:], sources):
            source = pick(table, place)
            pl.when(source < place)(functools.partial(step, wide, source))
        for group in range(geo.groups):
            at = slice(group * geo.tile_h, (group + 1) * geo.tile_h)
            out[group] = (accum[at, :] * natural).astype(jnp.bfloat16)

    return call(
        kernel,
        "query_grads",
        [whole(pltpu.SMEM)] * 2 + [whole()] * (5 + len(wides)),
        whole(),
        jax.ShapeDtypeStruct((geo.groups, geo.tile_h, width), jnp.bfloat16),
        [
            pltpu.VMEM((tokens, width), jnp.float32),
            pltpu.VMEM((RMAX, tokens, wide_rows), jnp.float32),
        ],
        8 + 3 * len(wides),
        4,
    )(*small, geo.gap, geo.frame[None, :], lse, delta, own, *wides)


def key_grads(geo, blocks, heads, small, own, stats, sources, wides):
    tokens, wide_rows = geo.tokens, geo.wide
    width = own.shape[-1]
    depth = width // heads
    natural = 1.0 / math.sqrt(depth)
    scale = LOG2E * natural
    stat_rows = stats[0].shape[0]
    lanes = [slice(h * depth, (h + 1) * depth) for h in range(heads)]

    def kernel(radius_ref, live_ref, gap_ref, frame_ref, own_ref, *refs):
        wide_refs, refs = refs[: len(wides)], refs[len(wides) :]
        stat_refs, refs = refs[:blocks], refs[blocks:]
        outs, (rows, accum, bias_ref) = refs[:2], refs[2:]
        place = lax.axis_index("span")
        accum[...] = jnp.zeros(accum.shape, jnp.float32)
        for n in range(blocks):
            rows[n] = stat_refs[n][...]
        live = frame_ref[...] < live_ref[place]
        set_bias(bias_ref, jnp.where(live, geo.near(gap_ref), FAR))

        def step(wide, base, rotation):
            def products(h):
                return (
                    dot_nt(own_ref[0, :, lanes[h]], wide[base, :, lanes[h]]),
                    dot_nt(own_ref[1, :, lanes[h]], wide[base + 1, :, lanes[h]]),
                )

            ahead = products(0)
            for h in range(heads):
                score, push = ahead
                if h + 1 < heads:
                    ahead = products(h + 1)
                score = score * scale + bias_ref[radius_ref[h] - 1]
                prob = jnp.exp2(score - rows[rotation, h : h + 1, :])
                accum[1, :, lanes[h]] += dot_nn(
                    prob.astype(jnp.bfloat16), wide[base + 1, :, lanes[h]]
                )
                slope = prob * (push - rows[rotation, heads + h : heads + h + 1, :])
                accum[0, :, lanes[h]] += dot_nn(
                    slope.astype(jnp.bfloat16), wide[base, :, lanes[h]]
                )

        step(wide_refs[0], 2, 0)
        for wide, table in zip(wide_refs[1:], sources):
            source = pick(table, place)
            rotation = lax.rem(place - source + blocks, blocks)
            pl.when(source > place)(functools.partial(step, wide, 0, rotation))
        for group in range(geo.groups):
            at = slice(group * geo.tile_h, (group + 1) * geo.tile_h)
            outs[0][group] = (accum[0, at, :] * natural).astype(jnp.bfloat16)
            outs[1][group] = accum[1, at, :].astype(jnp.bfloat16)

    final = jax.ShapeDtypeStruct((geo.groups, geo.tile_h, width), jnp.bfloat16)
    return call(
        kernel,
        "key_grads",
        [whole(pltpu.SMEM)] * 2 + [whole()] * (3 + len(wides) + blocks),
        [whole()] * 2,
        [final] * 2,
        [
            pltpu.VMEM((blocks, stat_rows, wide_rows), jnp.float32),
            pltpu.VMEM((2, tokens, width), jnp.float32),
            pltpu.VMEM((RMAX, tokens, wide_rows), jnp.float32),
        ],
        10 + 3 * blocks,
        5,
    )(*small, geo.gap, geo.frame[: tokens, None], own, *wides, *stats)


def rotate(x, by, blocks):
    return lax.ppermute(x, "span", [(i, (i + by) % blocks) for i in range(blocks)])


def shards(queries, cache_keys, cache_values, grad_attended, radius, frame_count, sizes):
    blocks, count_h, count_w = sizes
    frames, tile_h, tile_w, width = queries.shape[1:]
    heads = radius.shape[0]
    geo = Geometry(frames, tile_h, tile_w, count_h, count_w)
    small = (radius, frame_count)

    def grouped(x):
        return jnp.transpose(x[0], (0, 2, 1, 3)).reshape(geo.groups, tile_h, width)

    def restored(x):
        x = x.reshape(frames, tile_w, tile_h, width)
        return jnp.transpose(x, (0, 2, 1, 3))[None]

    arrays = [grouped(x) for x in (cache_keys, cache_values, queries, grad_attended)]
    own, *chains = tidy(geo, arrays, blocks)
    batches = relay(blocks)
    needed = {step for steps, _, _ in batches for step in steps}
    moved = {}
    for number in range(1, blocks):
        for chain in range(2):
            if any(c == chain and n >= number for c, n in needed):
                pairs = list(enumerate(swap(blocks, chain, number)))
                chains[chain] = lax.ppermute(chains[chain], "span", pairs)
                moved[chain, number] = chains[chain]

    same = list(range(blocks))
    todo = [([own], [0] * blocks, same)]
    todo += [([moved[step] for step in steps], which, blks) for steps, which, blks in batches]
    wides, state = [], None
    for n, (candidates, which, table) in enumerate(todo):
        x, messages = borders(geo, which, candidates)
        parts = [x] + geo.exchange(messages)
        last = n == len(todo) - 1
        wide, *state = forward(geo, blocks, heads, small, own, table, parts, state, last)
        wides.append(wide)
    attended, lse, delta, packed = state
    sources = [table for _, _, table in todo[1:]]
    own_stats = merge(geo, [packed] + geo.exchange([packed] * len(geo.pieces)))
    stats = [own_stats] + [rotate(own_stats, n, blocks) for n in range(1, blocks)]
    grad_q = query_grads(geo, heads, small, own, lse, delta, sources, wides)
    grad_k, grad_v = key_grads(geo, blocks, heads, small, own, stats, sources, wides)
    return tuple(restored(x) for x in (attended, grad_q, grad_k, grad_v))


def solution(mesh):
    placed = P("span", None, "ha", "wa", None)
    sizes = tuple(mesh.shape[name] for name in ("span", "ha", "wa"))
    return jax.shard_map(
        functools.partial(shards, sizes=sizes),
        mesh=mesh,
        in_specs=(placed,) * 4 + (P(), P()),
        out_specs=(placed,) * 4,
        check_vma=False,
    )
```

```python
import functools
import math

import jax
import jax.numpy as jnp
import ml_dtypes
import numpy as np
from jax import lax
from jax.experimental import pallas as pl
from jax.experimental.pallas import tpu as pltpu
from jax.sharding import PartitionSpec as P

RMAX = 2
FAR = 99.0
LOG2E = math.log2(math.e)
LANES = 128


def round_up(value, unit):
    return (value + unit - 1) // unit * unit


def dot_nt(a, b):
    return lax.dot_general(a, b, (((1,), (1,)), ((), ())), preferred_element_type=jnp.float32)


def dot_nn(a, b):
    return lax.dot_general(a, b, (((1,), (0,)), ((), ())), preferred_element_type=jnp.float32)


class Side:
    def __init__(self, kind, count, tile, variant):
        self.count = count
        self.swap = kind == "swap"
        if kind == "same":
            self.delta, self.start, self.length, self.send_start = 0, 0, tile, 0
        else:
            self.delta = 1 - 2 * variant if self.swap else kind
            send_up = (variant == 0) if self.swap else (kind < 0)
            self.length = RMAX
            self.start = tile if self.delta > 0 else -RMAX
            self.send_start = tile - RMAX if send_up else 0
        shift = 1 if self.swap else self.delta
        self.pairs = [((i + shift) % count, i) for i in range(count)]

    def place(self, index):
        delta = 1 - 2 * index if self.swap else self.delta
        other = index + delta
        inside = (other >= 0) & (other < self.count)
        return jnp.where(inside, other, index), inside


def sides(count, tile, variant):
    kinds = [] if count == 1 else ["swap"] if count == 2 else [-1, 1]
    return [Side(kind, count, tile, variant) for kind in ["same"] + kinds]


class Geometry:
    def __init__(self, frames, tile_h, tile_w, count_h, count_w):
        self.frames, self.tile_h, self.tile_w = frames, tile_h, tile_w
        self.count_h, self.count_w = count_h, count_w
        self.tokens = frames * tile_h * tile_w
        self.groups = frames * tile_w
        self.variants_h = 2 if count_h == 2 else 1
        self.variants_w = 2 if count_w == 2 else 1
        found = [
            self.variant(variant_h, variant_w)
            for variant_h in range(self.variants_h)
            for variant_w in range(self.variants_w)
        ]
        direct, tall, gap = (np.stack(arrays) for arrays in zip(*found))
        own = np.arange(self.tokens)
        self.row_select = self.one_hot(direct[:, self.tokens : self.tall], self.tokens)
        self.col_select = self.one_hot(tall[:, self.tall : self.used], self.tall)
        self.select = self.one_hot(direct, self.tokens)
        self.gap = gap.astype(np.float32)
        assert (direct[:, : self.tokens] == own).all()

    def one_hot(self, index, count):
        return (index[..., None] == np.arange(count)).astype(ml_dtypes.bfloat16)

    def variant(self, variant_h, variant_w):
        row_own, *rows_of = sides(self.count_h, self.tile_h, variant_h)
        col_own, *cols_of = sides(self.count_w, self.tile_w, variant_w)
        self.row_sides, self.col_sides = rows_of, cols_of
        direct, tall, rows, cols, frame = [], [], [], [], []
        self.ranges = []

        def add(row, col, base):
            ff, xx, yy = np.unravel_index(
                np.arange(self.frames * col.length * row.length),
                (self.frames, col.length, row.length),
            )
            start = len(direct)
            own_x, own_y = col.send_start + xx, row.send_start + yy
            direct.extend((ff * self.tile_w + own_x) * self.tile_h + own_y)
            tall.extend(base + (ff * self.tile_w + own_x) * row.length + yy)
            rows.extend(row.start + yy)
            cols.extend(col.start + xx)
            frame.extend(ff)
            self.ranges.append((start, len(direct), row, col))

        def pad(unit):
            count = round_up(len(direct), unit) - len(direct)
            for array, value in zip((direct, tall, rows, cols, frame), (-1, -1, 1000, 1000, 0)):
                array.extend([value] * count)

        add(row_own, col_own, 0)
        bases = []
        self.row_places, self.col_places = [], []
        for row in rows_of:
            bases.append(len(direct))
            add(row, col_own, bases[-1])
            pad(16)
            self.row_places.append((bases[-1], len(direct) - bases[-1]))
        self.tall = len(direct)
        for col in cols_of:
            start = len(direct)
            for row, base in zip([row_own] + rows_of, [0] + bases):
                add(row, col, base)
            pad(16)
            self.col_places.append((start, len(direct) - start))
        self.used = len(direct)
        pad(LANES)
        self.wide = len(direct)
        self.frame = np.array(frame, np.int32)
        rows, cols = np.array(rows), np.array(cols)
        mine = slice(0, self.tokens)
        gap = np.maximum(
            np.abs(rows[mine][:, None] - rows[None, :]), np.abs(cols[mine][:, None] - cols[None, :])
        )
        return np.array(direct), np.array(tall), np.minimum(gap, FAR)

    def which(self):
        at_h = lax.axis_index("ha") if self.variants_h == 2 else 0
        at_w = lax.axis_index("wa") if self.variants_w == 2 else 0
        return at_h * self.variants_w + at_w

    def near(self, gap_ref):
        lane = lax.broadcasted_iota(jnp.int32, (1, self.wide), 1)
        far = jnp.zeros((1, self.wide), jnp.float32)
        for start, end, row, col in self.ranges[1:]:
            inside = row.place(lax.axis_index("ha"))[1] & col.place(lax.axis_index("wa"))[1]
            cost = jnp.where(inside, 0.0, FAR)
            far = jnp.where((lane >= start) & (lane < end), cost, far)
        return gap_ref[self.which()] + far

    def permute(self, row, col, x):
        pairs = [
            (a * self.count_w + c, b * self.count_w + d)
            for a, b in row.pairs
            for c, d in col.pairs
        ]
        return lax.ppermute(x, ("ha", "wa"), pairs)

    def exchange_rows(self, messages):
        own = self.ranges[0][3]
        return [self.permute(row, own, x) for row, x in zip(self.row_sides, messages)]

    def exchange_cols(self, messages):
        own = self.ranges[0][2]
        return [self.permute(own, col, x) for col, x in zip(self.col_sides, messages)]

    def exchange_all(self, x):
        return [self.permute(row, col, x) for _, _, row, col in self.ranges[1:]]


def whole(memory=pltpu.VMEM):
    return pl.BlockSpec(memory_space=memory)


def call(kernel, name, in_specs, out_specs, out_shape, scratch, mib, cost, aliases=None):
    return pl.pallas_call(
        kernel,
        in_specs=in_specs,
        out_specs=out_specs,
        out_shape=out_shape,
        scratch_shapes=scratch,
        compiler_params=pltpu.CompilerParams(vmem_limit_bytes=mib * 1024 * 1024),
        cost_estimate=pl.CostEstimate(
            flops=int(cost * 1e9), bytes_accessed=int(cost * 2e6), transcendentals=0
        ),
        input_output_aliases=aliases or {},
        name=name,
    )


def pick(table, place):
    value = jnp.int32(table[0])
    for index, entry in enumerate(table[1:], 1):
        if entry != table[0]:
            value = jnp.where(place == index, entry, value)
    return value


def relay(blocks):
    held = [[(s, (s % 2 == 0) != bool(chain)) for s in range(blocks)] for chain in range(2)]
    fresh = [[] for _ in range(blocks)]
    for number in range(1, blocks):
        for chain in range(2):
            moved = [held[chain][a] for a in swap(blocks, chain, number)]
            held[chain] = moved
            for s, (block, keys) in enumerate(moved):
                if block != s and keys == (block < s) and block not in [b for _, b in fresh[s]]:
                    fresh[s].append(((chain, number), block))
    batches = []
    for n in range(blocks - 1):
        steps = sorted({fresh[s][n][0] for s in range(blocks)}, key=lambda step: step[::-1])
        which = [steps.index(fresh[s][n][0]) for s in range(blocks)]
        batches.append((steps, which, [fresh[s][n][1] for s in range(blocks)]))
    return batches


def swap(blocks, chain, number):
    start = (chain + number + 1) % 2
    partner = list(range(blocks))
    for low in range(start, blocks - 1, 2):
        partner[low], partner[low + 1] = low + 1, low
    return partner


def tidy(geo, arrays, blocks):
    width = arrays[0].shape[-1]
    tokens, tile_h = geo.tokens, geo.tile_h

    def kernel(*refs):
        ins, (own_ref, even_ref, odd_ref, stage, sems) = refs[:4], refs[4:]
        copies = [
            pltpu.make_async_copy(ref, stage.at[number], sems.at[number])
            for number, ref in enumerate(ins)
        ]
        for copy in copies:
            copy.start()
        for number, copy in enumerate(copies):
            copy.wait()
            for group in range(geo.groups):
                own_ref[number, group * tile_h : (group + 1) * tile_h, :] = stage[number, group]
        odd = lax.rem(lax.axis_index("span"), 2)
        even_ref[...] = own_ref[pl.ds(2 * odd, 2)]
        odd_ref[...] = own_ref[pl.ds(2 - 2 * odd, 2)]

    pair = jax.ShapeDtypeStruct((2, tokens, width), jnp.bfloat16)
    return call(
        kernel,
        "tidy",
        [whole(pltpu.HBM)] * 4,
        [whole()] * 3,
        [jax.ShapeDtypeStruct((4, tokens, width), jnp.bfloat16), pair, pair],
        [
            pltpu.VMEM((4, geo.groups, tile_h, width), jnp.bfloat16),
            pltpu.SemaphoreType.DMA((4,)),
        ],
        60,
        2,
    )(*arrays)


def pack_rows(geo, which, candidates, after):
    count, tokens, width = candidates[0].shape
    several = len(candidates) > 1
    sides = len(geo.row_places)

    def kernel(select_ref, *refs):
        ins, outs = refs[: len(candidates)], refs[len(candidates) + len(after) :]
        chosen = select_ref[geo.which()]
        pieces = outs[1:] if several else outs
        number = pick(which, lax.axis_index("span"))

        def work(x_ref):
            for a in range(count):
                x = x_ref[a]
                if several:
                    outs[0][a] = x
                picked = dot_nn(chosen, x).astype(jnp.bfloat16)
                for out, (start, size) in zip(pieces[a // 2 * sides :], geo.row_places):
                    out[a % 2] = picked[start - tokens : start - tokens + size]

        if not several:
            work(ins[0])
            return
        for index, ref in enumerate(ins):
            pl.when(number == index)(functools.partial(work, ref))

    sizes = [tokens] if several else []
    sizes += [size for _, size in geo.row_places] * (count // 2)
    out = call(
        kernel,
        "pack_rows",
        [whole()] * (1 + len(candidates)) + [whole(pl.ANY)] * len(after),
        [whole()] * len(sizes),
        [jax.ShapeDtypeStruct((2, size, width), jnp.bfloat16) for size in sizes],
        [],
        12,
        1,
    )(geo.row_select, *candidates, *after)
    return (out[0], out[1:]) if several else (candidates[0], out)


def pack_cols(geo, x, base, rows, after):
    count, tokens, width = 2, *x.shape[1:]

    def kernel(select_ref, x_ref, *refs):
        row_refs, refs = refs[: len(rows)], refs[len(rows) + len(after) :]
        outs, tall = refs[:-1], refs[-1]
        chosen = select_ref[geo.which()]
        for a in range(count):
            tall[a, :tokens] = x_ref[base + a]
            for ref, (start, size) in zip(row_refs, geo.row_places):
                tall[a, start : start + size] = ref[a]
            picked = dot_nn(chosen, tall[a]).astype(jnp.bfloat16)
            for out, (start, size) in zip(outs, geo.col_places):
                out[a] = picked[start - geo.tall : start - geo.tall + size]

    return call(
        kernel,
        "pack_cols",
        [whole()] * (2 + len(rows)) + [whole(pl.ANY)] * len(after),
        [whole()] * len(geo.col_places),
        [jax.ShapeDtypeStruct((count, size, width), jnp.bfloat16) for _, size in geo.col_places],
        [pltpu.VMEM((count, geo.tall, width), jnp.bfloat16)],
        12,
        1,
    )(geo.col_select, x, *rows, *after)


def set_bias(bias_ref, gap):
    for reach in range(1, RMAX + 1):
        bias_ref[reach - 1] = jnp.where(gap <= reach, 0.0, -jnp.inf)


def fit(x, lanes):
    return x if x.shape[1] == lanes else jnp.broadcast_to(x[:, :1], (x.shape[0], lanes))


def repeat(x, lanes):
    return jnp.concatenate([x] * (lanes // LANES), axis=1)


def spread(geo, base, parts, wide):
    for a in range(2):
        wide[a, : geo.tokens] = parts[0][base + a]
        for ref, (start, size) in zip(parts[1:], geo.row_places + geo.col_places):
            wide[a, start : start + size] = ref[a]
        if geo.wide > geo.used:
            wide[a, geo.used :] = jnp.zeros((geo.wide - geo.used, wide.shape[-1]), jnp.bfloat16)


def lay_out(geo, parts):
    def kernel(*refs):
        spread(geo, 2, refs[:-1], refs[-1])

    return call(
        kernel,
        "lay_out",
        [whole()] * len(parts),
        whole(),
        jax.ShapeDtypeStruct((2, geo.wide, parts[0].shape[-1]), jnp.bfloat16),
        [],
        12,
        0.3,
    )(*parts)


def forward(geo, blocks, heads, small, own, sources, parts, state, last, after):
    tokens, wide_rows = geo.tokens, geo.wide
    count, width = 2, own.shape[-1]
    depth = width // heads
    scale = LOG2E / math.sqrt(depth)
    per = len(parts)
    stat_rows = round_up(2 * heads, 8)
    first = state is None
    lanes = [slice(h * depth, (h + 1) * depth) for h in range(heads)]

    def kernel(radius_ref, live_ref, gap_ref, frame_ref, select_ref, own_ref, *refs):
        parts_refs, refs = refs[:per], refs[per:]
        state_in, refs = (None, refs) if first else (refs[:3], refs[3:])
        wide, *refs = refs[len(after) :]
        if last:
            outs, (accum, top, total, bias_ref) = refs[:4], refs[4:]
        else:
            accum, top, total, bias_ref = refs
        place = lax.axis_index("span")
        source = place if first else pick(sources, place)
        active = source <= place

        spread(geo, 0, parts_refs, wide)
        if first:
            accum[...] = jnp.zeros(accum.shape, jnp.float32)
            top[...] = jnp.full(top.shape, -jnp.inf, jnp.float32)
            total[...] = jnp.zeros(total.shape, jnp.float32)
        else:
            for old, new in zip(state_in, (accum, top, total)):
                new[...] = old[...]

        def attend():
            live = live_ref[source]
            set_bias(bias_ref, jnp.where(frame_ref[...] < live, geo.near(gap_ref), FAR))
            ones = jnp.ones((wide_rows, LANES), jnp.bfloat16)
            ahead = dot_nt(own_ref[2, :, lanes[0]], wide[0, :, lanes[0]])
            for h in range(heads):
                score = ahead
                if h + 1 < heads:
                    ahead = dot_nt(own_ref[2, :, lanes[h + 1]], wide[0, :, lanes[h + 1]])
                score = score * scale + bias_ref[radius_ref[h] - 1]
                best = jnp.max(score, axis=1, keepdims=True)
                new_top = jnp.maximum(top[h], best)
                fading = jnp.exp2(top[h] - new_top)
                top[h] = new_top
                weight = jnp.exp2(score - repeat(new_top, wide_rows)).astype(jnp.bfloat16)
                value = jnp.concatenate([wide[1, :, lanes[h]], ones], axis=1)
                both = dot_nn(weight, value)
                accum[:, lanes[h]] = accum[:, lanes[h]] * fit(fading, depth) + both[:, :depth]
                total[h] = total[h] * fading + both[:, depth:]

        def finish():
            attended_ref, lse_ref, delta_ref, packed_ref = outs
            lane = lax.broadcasted_iota(jnp.int32, (tokens, LANES), 1)
            column = jnp.zeros((tokens, LANES), jnp.float32)
            for h in range(heads):
                rounded = (accum[:, lanes[h]] / fit(total[h], depth)).astype(jnp.bfloat16)
                rounded = rounded.astype(jnp.float32)
                accum[:, lanes[h]] = rounded
                lse = top[h] + jnp.log2(total[h])
                grad = own_ref[3, :, lanes[h]].astype(jnp.float32)
                delta = jnp.sum(rounded * grad, axis=1, keepdims=True)
                delta = jnp.broadcast_to(delta, (tokens, LANES))
                lse_ref[h] = lse
                delta_ref[h] = delta
                column = jnp.where(lane == h, lse, column)
                column = jnp.where(lane == heads + h, delta, column)
            packed = jnp.zeros((wide_rows, LANES), jnp.float32)
            rest = column
            chosen = select_ref[geo.which()]
            for _ in range(3):
                part = rest.astype(jnp.bfloat16)
                rest = rest - part.astype(jnp.float32)
                packed = packed + dot_nn(chosen, part)
            packed_ref[...] = jnp.transpose(packed)[:stat_rows]
            for group in range(geo.groups):
                at = slice(group * geo.tile_h, (group + 1) * geo.tile_h)
                attended_ref[group] = accum[at, :].astype(jnp.bfloat16)

        if first:
            attend()
        else:
            pl.when(active)(attend)
        if last:
            finish()

    ins = [*small, geo.gap, geo.frame[None, :], geo.select, own, *parts]
    ins += [] if first else list(state)
    stat = (heads, tokens, LANES)
    running = [(tokens, width), stat, stat]
    shapes = [jax.ShapeDtypeStruct((count, wide_rows, width), jnp.bfloat16)]
    scratch = []
    if last:
        shapes += [
            jax.ShapeDtypeStruct((geo.groups, geo.tile_h, width), jnp.bfloat16),
            jax.ShapeDtypeStruct(stat, jnp.float32),
            jax.ShapeDtypeStruct(stat, jnp.float32),
            jax.ShapeDtypeStruct((stat_rows, wide_rows), jnp.float32),
        ]
        scratch += [pltpu.VMEM(shape, jnp.float32) for shape in running]
    else:
        shapes += [jax.ShapeDtypeStruct(shape, jnp.float32) for shape in running]
    return call(
        kernel,
        "forward",
        [whole(pltpu.SMEM)] * 2 + [whole()] * (len(ins) - 2) + [whole(pl.ANY)] * len(after),
        [whole()] * len(shapes),
        shapes,
        scratch + [pltpu.VMEM((RMAX, tokens, wide_rows), jnp.float32)],
        20,
        3,
    )(*ins, *after)


def merge(geo, pieces, after):
    def kernel(*refs):
        out = refs[-1]
        row = refs[0][...]
        lane = lax.broadcasted_iota(jnp.int32, row.shape, 1)
        for ref, (start, *_) in zip(refs[1:], geo.ranges[1:]):
            row = jnp.where(lane >= start, ref[...], row)
        out[...] = row

    return call(
        kernel,
        "merge",
        [whole()] * len(pieces) + [whole(pl.ANY)] * len(after),
        whole(),
        jax.ShapeDtypeStruct(pieces[0].shape, jnp.float32),
        [],
        4,
        0.1,
    )(*pieces, *after)


def query_grads(geo, heads, small, own, lse, delta, sources, wides, state, last, after):
    tokens, wide_rows = geo.tokens, geo.wide
    width = own.shape[-1]
    depth = width // heads
    natural = 1.0 / math.sqrt(depth)
    scale = LOG2E * natural
    lanes = [slice(h * depth, (h + 1) * depth) for h in range(heads)]

    def kernel(radius_ref, live_ref, gap_ref, frame_ref, lse_ref, delta_ref, own_ref, *refs):
        wide_refs, refs = refs[: len(wides)], refs[len(wides) :]
        state_in, refs = (None, refs) if state is None else (refs[0], refs[1:])
        refs = refs[len(after) :]
        out, accum, bias_ref = refs if last else (None, *refs)
        place = lax.axis_index("span")
        accum[...] = jnp.zeros(accum.shape, jnp.float32) if state is None else state_in[...]

        def step(wide, source):
            live = live_ref[source]
            set_bias(bias_ref, jnp.where(frame_ref[...] < live, geo.near(gap_ref), FAR))

            def products(h):
                return (
                    dot_nt(own_ref[2, :, lanes[h]], wide[0, :, lanes[h]]),
                    dot_nt(own_ref[3, :, lanes[h]], wide[1, :, lanes[h]]),
                )

            ahead = products(0)
            for h in range(heads):
                score, push = ahead
                if h + 1 < heads:
                    ahead = products(h + 1)
                score = score * scale + bias_ref[radius_ref[h] - 1]
                prob = jnp.exp2(score - repeat(lse_ref[h], wide_rows))
                slope = prob * (push - repeat(delta_ref[h], wide_rows))
                accum[:, lanes[h]] += dot_nn(slope.astype(jnp.bfloat16), wide[0, :, lanes[h]])

        for wide, table in zip(wide_refs, sources):
            if table == list(range(len(table))):
                step(wide, place)
            else:
                source = pick(table, place)
                pl.when(source < place)(functools.partial(step, wide, source))
        if last:
            for group in range(geo.groups):
                at = slice(group * geo.tile_h, (group + 1) * geo.tile_h)
                out[group] = (accum[at, :] * natural).astype(jnp.bfloat16)

    ins = [*small, geo.gap, geo.frame[None, :], lse, delta, own, *wides]
    ins += [] if state is None else [state]
    running = (tokens, width)
    shape = jax.ShapeDtypeStruct(running, jnp.float32)
    if last:
        shape = jax.ShapeDtypeStruct((geo.groups, geo.tile_h, width), jnp.bfloat16)
    return call(
        kernel,
        "query_grads",
        [whole(pltpu.SMEM)] * 2 + [whole()] * (len(ins) - 2) + [whole(pl.ANY)] * len(after),
        whole(),
        shape,
        ([pltpu.VMEM(running, jnp.float32)] if last else [])
        + [pltpu.VMEM((RMAX, tokens, wide_rows), jnp.float32)],
        14,
        3,
    )(*ins, *after)


def key_grads(geo, blocks, heads, small, own, stats, sources, wides, state, last):
    tokens, wide_rows = geo.tokens, geo.wide
    width = own.shape[-1]
    depth = width // heads
    natural = 1.0 / math.sqrt(depth)
    scale = LOG2E * natural
    stat_rows = stats[0].shape[0]
    lanes = [slice(h * depth, (h + 1) * depth) for h in range(heads)]

    def kernel(radius_ref, live_ref, gap_ref, frame_ref, own_ref, *refs):
        wide_refs, refs = refs[: len(wides)], refs[len(wides) :]
        stat_refs, refs = refs[: len(stats)], refs[len(stats) :]
        state_in, refs = (None, refs) if state is None else (refs[0], refs[1:])
        outs, refs = (refs[:2], refs[2:]) if last else (None, refs)
        accum, rows, bias_ref = refs
        place = lax.axis_index("span")
        accum[...] = jnp.zeros(accum.shape, jnp.float32) if state is None else state_in[...]
        for n, ref in enumerate(stat_refs):
            rows[n] = ref[...]
        live = frame_ref[...] < live_ref[place]
        set_bias(bias_ref, jnp.where(live, geo.near(gap_ref), FAR))

        def step(wide, rotation):
            def products(h):
                return (
                    dot_nt(own_ref[0, :, lanes[h]], wide[0, :, lanes[h]]),
                    dot_nt(own_ref[1, :, lanes[h]], wide[1, :, lanes[h]]),
                )

            ahead = products(0)
            for h in range(heads):
                score, push = ahead
                if h + 1 < heads:
                    ahead = products(h + 1)
                score = score * scale + bias_ref[radius_ref[h] - 1]
                prob = jnp.exp2(score - rows[rotation, h : h + 1, :])
                accum[1, :, lanes[h]] += dot_nn(
                    prob.astype(jnp.bfloat16), wide[1, :, lanes[h]]
                )
                slope = prob * (push - rows[rotation, heads + h : heads + h + 1, :])
                accum[0, :, lanes[h]] += dot_nn(
                    slope.astype(jnp.bfloat16), wide[0, :, lanes[h]]
                )

        for wide, table in zip(wide_refs, sources):
            if table == list(range(blocks)):
                step(wide, 0)
            else:
                source = pick(table, place)
                rotation = lax.rem(place - source + blocks, blocks)
                pl.when(source > place)(functools.partial(step, wide, rotation - 1))
        if last:
            for group in range(geo.groups):
                at = slice(group * geo.tile_h, (group + 1) * geo.tile_h)
                outs[0][group] = (accum[0, at, :] * natural).astype(jnp.bfloat16)
                outs[1][group] = accum[1, at, :].astype(jnp.bfloat16)

    ins = [*small, geo.gap, geo.frame[:tokens, None], own, *wides, *stats]
    ins += [] if state is None else [state]
    running = (2, tokens, width)
    shapes = [jax.ShapeDtypeStruct(running, jnp.float32)]
    if last:
        shapes = [jax.ShapeDtypeStruct((geo.groups, geo.tile_h, width), jnp.bfloat16)] * 2
    return call(
        kernel,
        "key_grads",
        [whole(pltpu.SMEM)] * 2 + [whole()] * (len(ins) - 2),
        [whole()] * len(shapes),
        shapes,
        ([pltpu.VMEM(running, jnp.float32)] if last else [])
        + [
            pltpu.VMEM((len(stats), stat_rows, wide_rows), jnp.float32),
            pltpu.VMEM((RMAX, tokens, wide_rows), jnp.float32),
        ],
        10 + 2 * len(wides),
        3,
    )(*ins)


def rotate(x, by, blocks):
    return lax.ppermute(x, "span", [(i, (i + by) % blocks) for i in range(blocks)])


def shards(queries, cache_keys, cache_values, grad_attended, radius, frame_count, sizes):
    blocks, count_h, count_w = sizes
    frames, tile_h, tile_w, width = queries.shape[1:]
    heads = radius.shape[0]
    geo = Geometry(frames, tile_h, tile_w, count_h, count_w)
    small = (radius, frame_count)

    def grouped(x):
        return jnp.transpose(x[0], (0, 2, 1, 3)).reshape(geo.groups, tile_h, width)

    def restored(x):
        x = x.reshape(frames, tile_w, tile_h, width)
        return jnp.transpose(x, (0, 2, 1, 3))[None]

    arrays = [grouped(x) for x in (cache_keys, cache_values, queries, grad_attended)]
    own, *chains = tidy(geo, arrays, blocks)
    batches = relay(blocks)
    needed = {step for steps, _, _ in batches for step in steps}
    sources = [list(range(blocks))] + [blks for _, _, blks in batches]
    hops = [0] + [max(number for _, number in steps) for steps, _, _ in batches]
    moved = {}

    def hop(number, after):
        for chain in range(2):
            if any(c == chain and n >= number for c, n in needed):
                x = chains[chain]
                x = lax.optimization_barrier((x, *after))[0] if after else x
                pairs = list(enumerate(swap(blocks, chain, number)))
                moved[chain, number] = chains[chain] = lax.ppermute(x, "span", pairs)

    def take(n):
        if n == 0:
            return pack_rows(geo, [0] * blocks, [own], [])
        steps, which, _ = batches[n - 1]
        waits = [x for (_, number), x in moved.items() if number <= hops[n]]
        return pack_rows(geo, which, [moved[step] for step in steps], waits + ready)

    hop(1, [])
    ready = []
    x, messages = take(0)
    half = len(geo.row_places)
    rows, asked = geo.exchange_rows(messages[:half]), geo.exchange_rows(messages[half:])
    wides, state = [], None
    for n in range(blocks):
        last = n == blocks - 1
        messages = pack_cols(geo, x, 0, rows, [state[0]] if state else [])
        ready = list(messages[:1])
        parts = [x] + rows + geo.exchange_cols(messages)
        after = []
        if not last:
            for number in range(hops[n] + 2, hops[n + 1] + 2):
                hop(number, ready)
            x, messages = take(n + 1)
            rows = geo.exchange_rows(messages)
            after = list(messages[:1])
        if n == 1:
            after.append(asked)
        wide, *state = forward(
            geo, blocks, heads, small, own, sources[n], parts, state, last, after
        )
        wides.append(wide)
        if n == 0:
            messages = pack_cols(geo, own, 2, asked, [state[0]])
            asked = lay_out(geo, [own] + asked + geo.exchange_cols(messages))
    attended, lse, delta, packed = state
    cut = (blocks + 1) // 2

    def query_part(first, end, begun, after):
        return query_grads(
            geo, heads, small, own, lse, delta, sources[first:end], wides[first:end], begun,
            end == blocks, after,
        )

    def key_part(first, end, brought, begun):
        return key_grads(
            geo, blocks, heads, small, own, brought, sources[first:end], ([asked] + wides[1:])[first:end],
            begun, end == blocks,
        )

    begun = query_part(0, cut, None, [])
    own_stats = merge(geo, [packed] + geo.exchange_all(packed), [begun])
    stats = [rotate(own_stats, n, blocks) for n in range(1, blocks)]
    grad_q = query_part(cut, blocks, begun, [own_stats])
    begun = key_part(0, 1, [own_stats], None)[0]
    grad_k, grad_v = key_part(1, blocks, stats, begun)
    return tuple(restored(x) for x in (attended, grad_q, grad_k, grad_v))


def solution(mesh):
    placed = P("span", None, "ha", "wa", None)
    sizes = tuple(mesh.shape[name] for name in ("span", "ha", "wa"))
    return jax.shard_map(
        functools.partial(shards, sizes=sizes),
        mesh=mesh,
        in_specs=(placed,) * 4 + (P(), P()),
        out_specs=(placed,) * 4,
        check_vma=False,
    )
```

```python
import functools
import math

import jax
import jax.numpy as jnp
import ml_dtypes
import numpy as np
from jax import lax
from jax.experimental import pallas as pl
from jax.experimental.pallas import tpu as pltpu
from jax.sharding import PartitionSpec as P

RMAX = 2
FAR = 99.0
LOG2E = math.log2(math.e)
LANES = 128


def round_up(value, unit):
    return (value + unit - 1) // unit * unit


def dot_nt(a, b):
    return lax.dot_general(a, b, (((1,), (1,)), ((), ())), preferred_element_type=jnp.float32)


def dot_nn(a, b):
    return lax.dot_general(a, b, (((1,), (0,)), ((), ())), preferred_element_type=jnp.float32)


class Side:
    def __init__(self, kind, count, tile, variant):
        self.count = count
        self.swap = kind == "swap"
        if kind == "same":
            self.delta, self.start, self.length, self.send_start = 0, 0, tile, 0
        else:
            self.delta = 1 - 2 * variant if self.swap else kind
            send_up = (variant == 0) if self.swap else (kind < 0)
            self.length = RMAX
            self.start = tile if self.delta > 0 else -RMAX
            self.send_start = tile - RMAX if send_up else 0
        shift = 1 if self.swap else self.delta
        self.pairs = [((i + shift) % count, i) for i in range(count)]

    def place(self, index):
        delta = 1 - 2 * index if self.swap else self.delta
        other = index + delta
        inside = (other >= 0) & (other < self.count)
        return jnp.where(inside, other, index), inside


def sides(count, tile, variant):
    kinds = [] if count == 1 else ["swap"] if count == 2 else [-1, 1]
    return [Side(kind, count, tile, variant) for kind in ["same"] + kinds]


class Geometry:
    def __init__(self, frames, tile_h, tile_w, count_h, count_w):
        self.frames, self.tile_h, self.tile_w = frames, tile_h, tile_w
        self.count_h, self.count_w = count_h, count_w
        self.tokens = frames * tile_h * tile_w
        self.groups = frames * tile_w
        self.variants_h = 2 if count_h == 2 else 1
        self.variants_w = 2 if count_w == 2 else 1
        found = [
            self.variant(variant_h, variant_w)
            for variant_h in range(self.variants_h)
            for variant_w in range(self.variants_w)
        ]
        direct, tall, gap = (np.stack(arrays) for arrays in zip(*found))
        own = np.arange(self.tokens)
        starts = [start for start, *_ in self.ranges] + [self.used]
        self.places = [(a, b - a) for a, b in zip(starts, starts[1:])][1:]
        self.all_select = self.one_hot(direct[:, self.tokens : self.used], self.tokens)
        self.row_select = self.one_hot(direct[:, self.tokens : self.tall], self.tokens)
        self.col_select = self.one_hot(tall[:, self.tall : self.used], self.tall)
        self.select = self.one_hot(direct, self.tokens)
        self.gap = gap.astype(np.float32)
        assert (direct[:, : self.tokens] == own).all()

    def one_hot(self, index, count):
        return (index[..., None] == np.arange(count)).astype(ml_dtypes.bfloat16)

    def variant(self, variant_h, variant_w):
        row_own, *rows_of = sides(self.count_h, self.tile_h, variant_h)
        col_own, *cols_of = sides(self.count_w, self.tile_w, variant_w)
        self.row_sides, self.col_sides = rows_of, cols_of
        direct, tall, rows, cols, frame = [], [], [], [], []
        self.ranges = []

        def add(row, col, base):
            ff, xx, yy = np.unravel_index(
                np.arange(self.frames * col.length * row.length),
                (self.frames, col.length, row.length),
            )
            start = len(direct)
            own_x, own_y = col.send_start + xx, row.send_start + yy
            direct.extend((ff * self.tile_w + own_x) * self.tile_h + own_y)
            tall.extend(base + (ff * self.tile_w + own_x) * row.length + yy)
            rows.extend(row.start + yy)
            cols.extend(col.start + xx)
            frame.extend(ff)
            self.ranges.append((start, len(direct), row, col))

        def pad(unit):
            count = round_up(len(direct), unit) - len(direct)
            for array, value in zip((direct, tall, rows, cols, frame), (-1, -1, 1000, 1000, 0)):
                array.extend([value] * count)

        add(row_own, col_own, 0)
        bases = []
        self.row_places, self.col_places = [], []
        for row in rows_of:
            bases.append(len(direct))
            add(row, col_own, bases[-1])
            pad(16)
            self.row_places.append((bases[-1], len(direct) - bases[-1]))
        self.tall = len(direct)
        for col in cols_of:
            start = len(direct)
            for row, base in zip([row_own] + rows_of, [0] + bases):
                add(row, col, base)
                pad(16)
            self.col_places.append((start, len(direct) - start))
        self.used = len(direct)
        pad(LANES)
        self.wide = len(direct)
        self.frame = np.array(frame, np.int32)
        rows, cols = np.array(rows), np.array(cols)
        mine = slice(0, self.tokens)
        gap = np.maximum(
            np.abs(rows[mine][:, None] - rows[None, :]), np.abs(cols[mine][:, None] - cols[None, :])
        )
        return np.array(direct), np.array(tall), np.minimum(gap, FAR)

    def which(self):
        at_h = lax.axis_index("ha") if self.variants_h == 2 else 0
        at_w = lax.axis_index("wa") if self.variants_w == 2 else 0
        return at_h * self.variants_w + at_w

    def near(self, gap_ref):
        lane = lax.broadcasted_iota(jnp.int32, (1, self.wide), 1)
        far = jnp.zeros((1, self.wide), jnp.float32)
        for start, end, row, col in self.ranges[1:]:
            inside = row.place(lax.axis_index("ha"))[1] & col.place(lax.axis_index("wa"))[1]
            cost = jnp.where(inside, 0.0, FAR)
            far = jnp.where((lane >= start) & (lane < end), cost, far)
        return gap_ref[self.which()] + far

    def permute(self, row, col, x):
        pairs = [
            (a * self.count_w + c, b * self.count_w + d)
            for a, b in row.pairs
            for c, d in col.pairs
        ]
        return lax.ppermute(x, ("ha", "wa"), pairs)

    def exchange_rows(self, messages):
        own = self.ranges[0][3]
        return [self.permute(row, own, x) for row, x in zip(self.row_sides, messages)]

    def exchange_cols(self, messages):
        own = self.ranges[0][2]
        return [self.permute(own, col, x) for col, x in zip(self.col_sides, messages)]

    def exchange_all(self, messages):
        return [self.permute(row, col, x) for x, (_, _, row, col) in zip(messages, self.ranges[1:])]


def whole(memory=pltpu.VMEM):
    return pl.BlockSpec(memory_space=memory)


def call(kernel, name, in_specs, out_specs, out_shape, scratch, mib, cost, aliases=None):
    return pl.pallas_call(
        kernel,
        in_specs=in_specs,
        out_specs=out_specs,
        out_shape=out_shape,
        scratch_shapes=scratch,
        compiler_params=pltpu.CompilerParams(vmem_limit_bytes=mib * 1024 * 1024),
        cost_estimate=pl.CostEstimate(
            flops=int(cost * 1e9), bytes_accessed=int(cost * 2e6), transcendentals=0
        ),
        input_output_aliases=aliases or {},
        name=name,
    )


def pick(table, place):
    value = jnp.int32(table[0])
    for index, entry in enumerate(table[1:], 1):
        if entry != table[0]:
            value = jnp.where(place == index, entry, value)
    return value


def relay(blocks):
    held = [[(s, (s % 2 == 0) != bool(chain)) for s in range(blocks)] for chain in range(2)]
    fresh = [[] for _ in range(blocks)]
    for number in range(1, blocks):
        for chain in range(2):
            moved = [held[chain][a] for a in swap(blocks, chain, number)]
            held[chain] = moved
            for s, (block, keys) in enumerate(moved):
                if block != s and keys == (block < s) and block not in [b for _, b in fresh[s]]:
                    fresh[s].append(((chain, number), block))
    batches = []
    for n in range(blocks - 1):
        steps = sorted({fresh[s][n][0] for s in range(blocks)}, key=lambda step: step[::-1])
        which = [steps.index(fresh[s][n][0]) for s in range(blocks)]
        batches.append((steps, which, [fresh[s][n][1] for s in range(blocks)]))
    return batches


def swap(blocks, chain, number):
    start = (chain + number + 1) % 2
    partner = list(range(blocks))
    for low in range(start, blocks - 1, 2):
        partner[low], partner[low + 1] = low + 1, low
    return partner


def tidy(geo, arrays, blocks):
    width = arrays[0].shape[-1]
    tokens, tile_h = geo.tokens, geo.tile_h

    def kernel(*refs):
        ins, (own_ref, even_ref, odd_ref, stage, sems) = refs[:4], refs[4:]
        copies = [
            pltpu.make_async_copy(ref, stage.at[number], sems.at[number])
            for number, ref in enumerate(ins)
        ]
        for copy in copies:
            copy.start()
        for number, copy in enumerate(copies):
            copy.wait()
            for group in range(geo.groups):
                own_ref[number, group * tile_h : (group + 1) * tile_h, :] = stage[number, group]
        odd = lax.rem(lax.axis_index("span"), 2)
        even_ref[...] = own_ref[pl.ds(2 * odd, 2)]
        odd_ref[...] = own_ref[pl.ds(2 - 2 * odd, 2)]

    pair = jax.ShapeDtypeStruct((2, tokens, width), jnp.bfloat16)
    return call(
        kernel,
        "tidy",
        [whole(pltpu.HBM)] * 4,
        [whole()] * 3,
        [jax.ShapeDtypeStruct((4, tokens, width), jnp.bfloat16), pair, pair],
        [
            pltpu.VMEM((4, geo.groups, tile_h, width), jnp.bfloat16),
            pltpu.SemaphoreType.DMA((4,)),
        ],
        60,
        2,
    )(*arrays)


def pack_rows(geo, which, candidates, after, every=False):
    places = geo.places if every else geo.row_places
    select = geo.all_select if every else geo.row_select
    count, tokens, width = candidates[0].shape
    several = len(candidates) > 1
    sides = len(places)

    def kernel(select_ref, *refs):
        ins, outs = refs[: len(candidates)], refs[len(candidates) + len(after) :]
        chosen = select_ref[geo.which()]
        pieces = outs[1:] if several else outs
        number = pick(which, lax.axis_index("span"))

        def work(x_ref):
            for a in range(count):
                x = x_ref[a]
                if several:
                    outs[0][a] = x
                picked = dot_nn(chosen, x).astype(jnp.bfloat16)
                for out, (start, size) in zip(pieces[a // 2 * sides :], places):
                    out[a % 2] = picked[start - tokens : start - tokens + size]

        if not several:
            work(ins[0])
            return
        for index, ref in enumerate(ins):
            pl.when(number == index)(functools.partial(work, ref))

    sizes = [tokens] if several else []
    sizes += [size for _, size in places] * (count // 2)
    out = call(
        kernel,
        "pack_rows",
        [whole()] * (1 + len(candidates)) + [whole(pl.ANY)] * len(after),
        [whole()] * len(sizes),
        [jax.ShapeDtypeStruct((2, size, width), jnp.bfloat16) for size in sizes],
        [],
        12,
        0.2,
    )(select, *candidates, *after)
    return (out[0], out[1:]) if several else (candidates[0], out)


def pack_cols(geo, x, base, rows, after):
    count, tokens, width = 2, *x.shape[1:]

    def kernel(select_ref, x_ref, *refs):
        row_refs, refs = refs[: len(rows)], refs[len(rows) + len(after) :]
        outs, tall = refs[:-1], refs[-1]
        chosen = select_ref[geo.which()]
        for a in range(count):
            tall[a, :tokens] = x_ref[base + a]
            for ref, (start, size) in zip(row_refs, geo.row_places):
                tall[a, start : start + size] = ref[a]
            picked = dot_nn(chosen, tall[a]).astype(jnp.bfloat16)
            for out, (start, size) in zip(outs, geo.col_places):
                out[a] = picked[start - geo.tall : start - geo.tall + size]

    return call(
        kernel,
        "pack_cols",
        [whole()] * (2 + len(rows)) + [whole(pl.ANY)] * len(after),
        [whole()] * len(geo.col_places),
        [jax.ShapeDtypeStruct((count, size, width), jnp.bfloat16) for _, size in geo.col_places],
        [pltpu.VMEM((count, geo.tall, width), jnp.bfloat16)],
        12,
        0.2,
    )(geo.col_select, x, *rows, *after)


def set_bias(bias_ref, gap):
    for reach in range(1, RMAX + 1):
        bias_ref[reach - 1] = jnp.where(gap <= reach, 0.0, -jnp.inf)


def fit(x, lanes):
    return x if x.shape[1] == lanes else jnp.broadcast_to(x[:, :1], (x.shape[0], lanes))


def repeat(x, lanes):
    return jnp.concatenate([x] * (lanes // LANES), axis=1)


def spread(geo, base, parts, wide):
    for a in range(2):
        wide[a, : geo.tokens] = parts[0][base + a]
        places = geo.row_places + geo.col_places
        if len(parts) > 1 + len(places):
            places = geo.places
        for ref, (start, size) in zip(parts[1:], places):
            wide[a, start : start + size] = ref[a]
        if geo.wide > geo.used:
            wide[a, geo.used :] = jnp.zeros((geo.wide - geo.used, wide.shape[-1]), jnp.bfloat16)


def lay_out(geo, parts):
    def kernel(*refs):
        spread(geo, 2, refs[:-1], refs[-1])

    return call(
        kernel,
        "lay_out",
        [whole()] * len(parts),
        whole(),
        jax.ShapeDtypeStruct((2, geo.wide, parts[0].shape[-1]), jnp.bfloat16),
        [],
        12,
        0.1,
    )(*parts)


def forward(geo, blocks, heads, small, own, sources, parts, state, last, after):
    tokens, wide_rows = geo.tokens, geo.wide
    count, width = 2, own.shape[-1]
    depth = width // heads
    scale = LOG2E / math.sqrt(depth)
    per = len(parts)
    stat_rows = round_up(2 * heads, 8)
    first = state is None
    lanes = [slice(h * depth, (h + 1) * depth) for h in range(heads)]

    def kernel(radius_ref, live_ref, gap_ref, frame_ref, select_ref, own_ref, *refs):
        parts_refs, refs = refs[:per], refs[per:]
        state_in, refs = (None, refs) if first else (refs[:3], refs[3:])
        wide, *refs = refs[len(after) :]
        if last:
            outs, (accum, top, total, bias_ref) = refs[:4], refs[4:]
        else:
            accum, top, total, bias_ref = refs
        place = lax.axis_index("span")
        source = place if first else pick(sources, place)
        active = source <= place

        spread(geo, 0, parts_refs, wide)
        if first:
            accum[...] = jnp.zeros(accum.shape, jnp.float32)
            top[...] = jnp.full(top.shape, -jnp.inf, jnp.float32)
            total[...] = jnp.zeros(total.shape, jnp.float32)
        else:
            for old, new in zip(state_in, (accum, top, total)):
                new[...] = old[...]

        def attend():
            live = live_ref[source]
            set_bias(bias_ref, jnp.where(frame_ref[...] < live, geo.near(gap_ref), FAR))
            ones = jnp.ones((wide_rows, LANES), jnp.bfloat16)
            ahead = dot_nt(own_ref[2, :, lanes[0]], wide[0, :, lanes[0]])
            for h in range(heads):
                score = ahead
                if h + 1 < heads:
                    ahead = dot_nt(own_ref[2, :, lanes[h + 1]], wide[0, :, lanes[h + 1]])
                score = score * scale + bias_ref[radius_ref[h] - 1]
                best = jnp.max(score, axis=1, keepdims=True)
                new_top = jnp.maximum(top[h], best)
                fading = jnp.exp2(top[h] - new_top)
                top[h] = new_top
                weight = jnp.exp2(score - repeat(new_top, wide_rows)).astype(jnp.bfloat16)
                value = jnp.concatenate([wide[1, :, lanes[h]], ones], axis=1)
                both = dot_nn(weight, value)
                accum[:, lanes[h]] = accum[:, lanes[h]] * fit(fading, depth) + both[:, :depth]
                total[h] = total[h] * fading + both[:, depth:]

        def finish():
            attended_ref, lse_ref, delta_ref, packed_ref = outs
            lane = lax.broadcasted_iota(jnp.int32, (tokens, LANES), 1)
            column = jnp.zeros((tokens, LANES), jnp.float32)
            for h in range(heads):
                rounded = (accum[:, lanes[h]] / fit(total[h], depth)).astype(jnp.bfloat16)
                rounded = rounded.astype(jnp.float32)
                accum[:, lanes[h]] = rounded
                lse = top[h] + jnp.log2(total[h])
                grad = own_ref[3, :, lanes[h]].astype(jnp.float32)
                delta = jnp.sum(rounded * grad, axis=1, keepdims=True)
                delta = jnp.broadcast_to(delta, (tokens, LANES))
                lse_ref[h] = lse
                delta_ref[h] = delta
                column = jnp.where(lane == h, lse, column)
                column = jnp.where(lane == heads + h, delta, column)
            packed = jnp.zeros((wide_rows, LANES), jnp.float32)
            rest = column
            chosen = select_ref[geo.which()]
            for _ in range(3):
                part = rest.astype(jnp.bfloat16)
                rest = rest - part.astype(jnp.float32)
                packed = packed + dot_nn(chosen, part)
            packed_ref[...] = jnp.transpose(packed)[:stat_rows]
            for group in range(geo.groups):
                at = slice(group * geo.tile_h, (group + 1) * geo.tile_h)
                attended_ref[group] = accum[at, :].astype(jnp.bfloat16)

        if first:
            attend()
        else:
            pl.when(active)(attend)
        if last:
            finish()

    ins = [*small, geo.gap, geo.frame[None, :], geo.select, own, *parts]
    ins += [] if first else list(state)
    stat = (heads, tokens, LANES)
    running = [(tokens, width), stat, stat]
    shapes = [jax.ShapeDtypeStruct((count, wide_rows, width), jnp.bfloat16)]
    scratch = []
    if last:
        shapes += [
            jax.ShapeDtypeStruct((geo.groups, geo.tile_h, width), jnp.bfloat16),
            jax.ShapeDtypeStruct(stat, jnp.float32),
            jax.ShapeDtypeStruct(stat, jnp.float32),
            jax.ShapeDtypeStruct((stat_rows, wide_rows), jnp.float32),
        ]
        scratch += [pltpu.VMEM(shape, jnp.float32) for shape in running]
    else:
        shapes += [jax.ShapeDtypeStruct(shape, jnp.float32) for shape in running]
    return call(
        kernel,
        "forward",
        [whole(pltpu.SMEM)] * 2 + [whole()] * (len(ins) - 2) + [whole(pl.ANY)] * len(after),
        [whole()] * len(shapes),
        shapes,
        scratch + [pltpu.VMEM((RMAX, tokens, wide_rows), jnp.float32)],
        20,
        1.5,
    )(*ins, *after)


def merge(geo, pieces, after):
    def kernel(*refs):
        out = refs[-1]
        row = refs[0][...]
        lane = lax.broadcasted_iota(jnp.int32, row.shape, 1)
        for ref, (start, *_) in zip(refs[1:], geo.ranges[1:]):
            row = jnp.where(lane >= start, ref[...], row)
        out[...] = row

    return call(
        kernel,
        "merge",
        [whole()] * len(pieces) + [whole(pl.ANY)] * len(after),
        whole(),
        jax.ShapeDtypeStruct(pieces[0].shape, jnp.float32),
        [],
        4,
        0.1,
    )(*pieces, *after)


def query_grads(geo, heads, small, own, lse, delta, sources, wides, state, last, after):
    tokens, wide_rows = geo.tokens, geo.wide
    width = own.shape[-1]
    depth = width // heads
    natural = 1.0 / math.sqrt(depth)
    scale = LOG2E * natural
    lanes = [slice(h * depth, (h + 1) * depth) for h in range(heads)]

    def kernel(radius_ref, live_ref, gap_ref, frame_ref, lse_ref, delta_ref, own_ref, *refs):
        wide_refs, refs = refs[: len(wides)], refs[len(wides) :]
        state_in, refs = (None, refs) if state is None else (refs[0], refs[1:])
        refs = refs[len(after) :]
        out, accum, bias_ref = refs if last else (None, *refs)
        place = lax.axis_index("span")
        accum[...] = jnp.zeros(accum.shape, jnp.float32) if state is None else state_in[...]

        def step(wide, source):
            live = live_ref[source]
            set_bias(bias_ref, jnp.where(frame_ref[...] < live, geo.near(gap_ref), FAR))

            def products(h):
                return (
                    dot_nt(own_ref[2, :, lanes[h]], wide[0, :, lanes[h]]),
                    dot_nt(own_ref[3, :, lanes[h]], wide[1, :, lanes[h]]),
                )

            ahead = products(0)
            for h in range(heads):
                score, push = ahead
                if h + 1 < heads:
                    ahead = products(h + 1)
                score = score * scale + bias_ref[radius_ref[h] - 1]
                prob = jnp.exp2(score - repeat(lse_ref[h], wide_rows))
                slope = prob * (push - repeat(delta_ref[h], wide_rows))
                accum[:, lanes[h]] += dot_nn(slope.astype(jnp.bfloat16), wide[0, :, lanes[h]])

        for wide, table in zip(wide_refs, sources):
            if table == list(range(len(table))):
                step(wide, place)
            else:
                source = pick(table, place)
                pl.when(source < place)(functools.partial(step, wide, source))
        if last:
            for group in range(geo.groups):
                at = slice(group * geo.tile_h, (group + 1) * geo.tile_h)
                out[group] = (accum[at, :] * natural).astype(jnp.bfloat16)

    ins = [*small, geo.gap, geo.frame[None, :], lse, delta, own, *wides]
    ins += [] if state is None else [state]
    running = (tokens, width)
    shape = jax.ShapeDtypeStruct(running, jnp.float32)
    if last:
        shape = jax.ShapeDtypeStruct((geo.groups, geo.tile_h, width), jnp.bfloat16)
    return call(
        kernel,
        "query_grads",
        [whole(pltpu.SMEM)] * 2 + [whole()] * (len(ins) - 2) + [whole(pl.ANY)] * len(after),
        whole(),
        shape,
        ([pltpu.VMEM(running, jnp.float32)] if last else [])
        + [pltpu.VMEM((RMAX, tokens, wide_rows), jnp.float32)],
        14,
        3,
    )(*ins, *after)


def key_grads(geo, blocks, heads, small, own, stats, sources, wides, state, last):
    tokens, wide_rows = geo.tokens, geo.wide
    width = own.shape[-1]
    depth = width // heads
    natural = 1.0 / math.sqrt(depth)
    scale = LOG2E * natural
    stat_rows = stats[0].shape[0]
    lanes = [slice(h * depth, (h + 1) * depth) for h in range(heads)]

    def kernel(radius_ref, live_ref, gap_ref, frame_ref, own_ref, *refs):
        wide_refs, refs = refs[: len(wides)], refs[len(wides) :]
        stat_refs, refs = refs[: len(stats)], refs[len(stats) :]
        state_in, refs = (None, refs) if state is None else (refs[0], refs[1:])
        outs, refs = (refs[:2], refs[2:]) if last else (None, refs)
        accum, rows, bias_ref = refs
        place = lax.axis_index("span")
        accum[...] = jnp.zeros(accum.shape, jnp.float32) if state is None else state_in[...]
        for n, ref in enumerate(stat_refs):
            rows[n] = ref[...]
        live = frame_ref[...] < live_ref[place]
        set_bias(bias_ref, jnp.where(live, geo.near(gap_ref), FAR))

        def step(wide, rotation):
            def products(h):
                return (
                    dot_nt(own_ref[0, :, lanes[h]], wide[0, :, lanes[h]]),
                    dot_nt(own_ref[1, :, lanes[h]], wide[1, :, lanes[h]]),
                )

            ahead = products(0)
            for h in range(heads):
                score, push = ahead
                if h + 1 < heads:
                    ahead = products(h + 1)
                score = score * scale + bias_ref[radius_ref[h] - 1]
                prob = jnp.exp2(score - rows[rotation, h : h + 1, :])
                accum[1, :, lanes[h]] += dot_nn(
                    prob.astype(jnp.bfloat16), wide[1, :, lanes[h]]
                )
                slope = prob * (push - rows[rotation, heads + h : heads + h + 1, :])
                accum[0, :, lanes[h]] += dot_nn(
                    slope.astype(jnp.bfloat16), wide[0, :, lanes[h]]
                )

        for wide, table in zip(wide_refs, sources):
            if table == list(range(blocks)):
                step(wide, 0)
            else:
                source = pick(table, place)
                rotation = lax.rem(place - source + blocks, blocks)
                pl.when(source > place)(functools.partial(step, wide, rotation - 1))
        if last:
            for group in range(geo.groups):
                at = slice(group * geo.tile_h, (group + 1) * geo.tile_h)
                outs[0][group] = (accum[0, at, :] * natural).astype(jnp.bfloat16)
                outs[1][group] = accum[1, at, :].astype(jnp.bfloat16)

    ins = [*small, geo.gap, geo.frame[:tokens, None], own, *wides, *stats]
    ins += [] if state is None else [state]
    running = (2, tokens, width)
    shapes = [jax.ShapeDtypeStruct(running, jnp.float32)]
    if last:
        shapes = [jax.ShapeDtypeStruct((geo.groups, geo.tile_h, width), jnp.bfloat16)] * 2
    return call(
        kernel,
        "key_grads",
        [whole(pltpu.SMEM)] * 2 + [whole()] * (len(ins) - 2),
        [whole()] * len(shapes),
        shapes,
        ([pltpu.VMEM(running, jnp.float32)] if last else [])
        + [
            pltpu.VMEM((len(stats), stat_rows, wide_rows), jnp.float32),
            pltpu.VMEM((RMAX, tokens, wide_rows), jnp.float32),
        ],
        10 + 2 * len(wides),
        3,
    )(*ins)


def rotate(x, by, blocks):
    return lax.ppermute(x, "span", [(i, (i + by) % blocks) for i in range(blocks)])


def shards(queries, cache_keys, cache_values, grad_attended, radius, frame_count, sizes):
    blocks, count_h, count_w = sizes
    frames, tile_h, tile_w, width = queries.shape[1:]
    heads = radius.shape[0]
    geo = Geometry(frames, tile_h, tile_w, count_h, count_w)
    small = (radius, frame_count)

    def grouped(x):
        return jnp.transpose(x[0], (0, 2, 1, 3)).reshape(geo.groups, tile_h, width)

    def restored(x):
        x = x.reshape(frames, tile_w, tile_h, width)
        return jnp.transpose(x, (0, 2, 1, 3))[None]

    arrays = [grouped(x) for x in (cache_keys, cache_values, queries, grad_attended)]
    own, *chains = tidy(geo, arrays, blocks)
    batches = relay(blocks)
    needed = {step for steps, _, _ in batches for step in steps}
    sources = [list(range(blocks))] + [blks for _, _, blks in batches]
    hops = [0] + [max(number for _, number in steps) for steps, _, _ in batches]
    moved = {}

    def hop(number, after):
        for chain in range(2):
            if any(c == chain and n >= number for c, n in needed):
                x = chains[chain]
                x = lax.optimization_barrier((x, *after))[0] if after else x
                pairs = list(enumerate(swap(blocks, chain, number)))
                moved[chain, number] = chains[chain] = lax.ppermute(x, "span", pairs)

    def take(n, after):
        steps, which, _ = batches[n - 1]
        after = after + [x for (_, number), x in moved.items() if number <= hops[n]]
        final = n == blocks - 1
        return pack_rows(geo, which, [moved[step] for step in steps], after, final)

    hop(1, [])
    x, messages = pack_rows(geo, [0] * blocks, [own], [])
    half = len(geo.row_places)
    asked, pieces = messages[half:], geo.exchange_rows(messages[:half])
    wides, state = [], None
    for n in range(blocks):
        last = n == blocks - 1
        ready = []
        if n == 0 or not last:
            messages = pack_cols(geo, x, 0, pieces, [state[0]] if state else [])
            ready = list(messages[:1])
            pieces = pieces + geo.exchange_cols(messages)
        parts, after = [x] + pieces, []
        if not last:
            for number in range(hops[n] + 2, hops[n + 1] + 2):
                hop(number, ready)
            x, messages = take(n + 1, pieces[-1:] if n + 2 < blocks else ready)
            after = list(messages[:1])
            if n == 0:
                asked = lax.optimization_barrier((*asked, *after))[:half]
                asked = geo.exchange_rows(asked)
            if n == 1:
                cols = geo.exchange_cols(pack_cols(geo, own, 2, asked, after))
                asked = lay_out(geo, [own] + asked + cols)
            if n == blocks - 2:
                after = after + [asked] if n > 1 else after
                pieces = geo.exchange_all(messages)
            else:
                pieces = geo.exchange_rows(messages)
        wide, *state = forward(
            geo, blocks, heads, small, own, sources[n], parts, state, last, after
        )
        wides.append(wide)
    if blocks < 3:
        cols = geo.exchange_cols(pack_cols(geo, own, 2, asked, [state[0]]))
        asked = lay_out(geo, [own] + asked + cols)
    attended, lse, delta, packed = state
    cut = (blocks + 1) // 2

    def query_part(first, end, begun, after):
        return query_grads(
            geo, heads, small, own, lse, delta, sources[first:end], wides[first:end], begun,
            end == blocks, after,
        )

    def key_part(first, end, brought, begun):
        return key_grads(
            geo, blocks, heads, small, own, brought, sources[first:end], ([asked] + wides[1:])[first:end],
            begun, end == blocks,
        )

    begun = query_part(0, cut, None, [])
    own_stats = merge(geo, [packed] + geo.exchange_all([packed] * len(geo.places)), [begun])
    stats = [rotate(own_stats, n, blocks) for n in range(1, blocks)]
    grad_q = query_part(cut, blocks, begun, [own_stats])
    begun = key_part(0, 1, [own_stats], None)[0]
    grad_k, grad_v = key_part(1, blocks, stats, begun)
    return tuple(restored(x) for x in (attended, grad_q, grad_k, grad_v))


def solution(mesh):
    placed = P("span", None, "ha", "wa", None)
    sizes = tuple(mesh.shape[name] for name in ("span", "ha", "wa"))
    return jax.shard_map(
        functools.partial(shards, sizes=sizes),
        mesh=mesh,
        in_specs=(placed,) * 4 + (P(), P()),
        out_specs=(placed,) * 4,
        check_vma=False,
    )
```

```python
import functools
import math

import jax
import jax.numpy as jnp
import ml_dtypes
import numpy as np
from jax import lax
from jax.experimental import pallas as pl
from jax.experimental.pallas import tpu as pltpu
from jax.sharding import PartitionSpec as P

RMAX = 2
FAR = 99.0
LOG2E = math.log2(math.e)
LANES = 128


def round_up(value, unit):
    return (value + unit - 1) // unit * unit


def dot_nt(a, b):
    return lax.dot_general(a, b, (((1,), (1,)), ((), ())), preferred_element_type=jnp.float32)


def dot_nn(a, b):
    return lax.dot_general(a, b, (((1,), (0,)), ((), ())), preferred_element_type=jnp.float32)


class Side:
    def __init__(self, kind, count, tile, variant):
        self.count = count
        self.swap = kind == "swap"
        if kind == "same":
            self.delta, self.start, self.length, self.send_start = 0, 0, tile, 0
        else:
            self.delta = 1 - 2 * variant if self.swap else kind
            send_up = (variant == 0) if self.swap else (kind < 0)
            self.length = RMAX
            self.start = tile if self.delta > 0 else -RMAX
            self.send_start = tile - RMAX if send_up else 0
        shift = 1 if self.swap else self.delta
        self.pairs = [((i + shift) % count, i) for i in range(count)]

    def place(self, index):
        delta = 1 - 2 * index if self.swap else self.delta
        other = index + delta
        inside = (other >= 0) & (other < self.count)
        return jnp.where(inside, other, index), inside


def sides(count, tile, variant):
    kinds = [] if count == 1 else ["swap"] if count == 2 else [-1, 1]
    return [Side(kind, count, tile, variant) for kind in ["same"] + kinds]


class Geometry:
    def __init__(self, frames, tile_h, tile_w, count_h, count_w):
        self.frames, self.tile_h, self.tile_w = frames, tile_h, tile_w
        self.count_h, self.count_w = count_h, count_w
        self.tokens = frames * tile_h * tile_w
        self.groups = frames * tile_w
        self.variants_h = 2 if count_h == 2 else 1
        self.variants_w = 2 if count_w == 2 else 1
        found = [
            self.variant(variant_h, variant_w)
            for variant_h in range(self.variants_h)
            for variant_w in range(self.variants_w)
        ]
        direct, tall, gap = (np.stack(arrays) for arrays in zip(*found))
        own = np.arange(self.tokens)
        starts = [start for start, *_ in self.ranges] + [self.used]
        self.places = [(a, b - a) for a, b in zip(starts, starts[1:])][1:]
        self.all_select = self.one_hot(direct[:, self.tokens : self.used], self.tokens)
        self.row_select = self.one_hot(direct[:, self.tokens : self.tall], self.tokens)
        self.col_select = self.one_hot(tall[:, self.tall : self.used], self.tall)
        self.select = self.one_hot(direct, self.tokens)
        self.gap = gap.astype(np.float32)
        assert (direct[:, : self.tokens] == own).all()

    def one_hot(self, index, count):
        return (index[..., None] == np.arange(count)).astype(ml_dtypes.bfloat16)

    def variant(self, variant_h, variant_w):
        row_own, *rows_of = sides(self.count_h, self.tile_h, variant_h)
        col_own, *cols_of = sides(self.count_w, self.tile_w, variant_w)
        self.row_sides, self.col_sides = rows_of, cols_of
        direct, tall, rows, cols, frame = [], [], [], [], []
        self.ranges = []

        def add(row, col, base):
            ff, xx, yy = np.unravel_index(
                np.arange(self.frames * col.length * row.length),
                (self.frames, col.length, row.length),
            )
            start = len(direct)
            own_x, own_y = col.send_start + xx, row.send_start + yy
            direct.extend((ff * self.tile_w + own_x) * self.tile_h + own_y)
            tall.extend(base + (ff * self.tile_w + own_x) * row.length + yy)
            rows.extend(row.start + yy)
            cols.extend(col.start + xx)
            frame.extend(ff)
            self.ranges.append((start, len(direct), row, col))

        def pad(unit):
            count = round_up(len(direct), unit) - len(direct)
            for array, value in zip((direct, tall, rows, cols, frame), (-1, -1, 1000, 1000, 0)):
                array.extend([value] * count)

        add(row_own, col_own, 0)
        bases = []
        self.row_places, self.col_places = [], []
        for row in rows_of:
            bases.append(len(direct))
            add(row, col_own, bases[-1])
            pad(16)
            self.row_places.append((bases[-1], len(direct) - bases[-1]))
        self.tall = len(direct)
        for col in cols_of:
            start = len(direct)
            for row, base in zip([row_own] + rows_of, [0] + bases):
                add(row, col, base)
                pad(16)
            self.col_places.append((start, len(direct) - start))
        self.used = len(direct)
        pad(LANES)
        self.wide = len(direct)
        self.frame = np.array(frame, np.int32)
        rows, cols = np.array(rows), np.array(cols)
        mine = slice(0, self.tokens)
        gap = np.maximum(
            np.abs(rows[mine][:, None] - rows[None, :]), np.abs(cols[mine][:, None] - cols[None, :])
        )
        return np.array(direct), np.array(tall), np.minimum(gap, FAR)

    def which(self):
        at_h = lax.axis_index("ha") if self.variants_h == 2 else 0
        at_w = lax.axis_index("wa") if self.variants_w == 2 else 0
        return at_h * self.variants_w + at_w

    def near(self, gap_ref):
        lane = lax.broadcasted_iota(jnp.int32, (1, self.wide), 1)
        far = jnp.zeros((1, self.wide), jnp.float32)
        for start, end, row, col in self.ranges[1:]:
            inside = row.place(lax.axis_index("ha"))[1] & col.place(lax.axis_index("wa"))[1]
            cost = jnp.where(inside, 0.0, FAR)
            far = jnp.where((lane >= start) & (lane < end), cost, far)
        return gap_ref[self.which()] + far

    def permute(self, row, col, x):
        pairs = [
            (a * self.count_w + c, b * self.count_w + d)
            for a, b in row.pairs
            for c, d in col.pairs
        ]
        return lax.ppermute(x, ("ha", "wa"), pairs)

    def exchange_rows(self, messages):
        own = self.ranges[0][3]
        return [self.permute(row, own, x) for row, x in zip(self.row_sides, messages)]

    def exchange_cols(self, messages):
        own = self.ranges[0][2]
        return [self.permute(own, col, x) for col, x in zip(self.col_sides, messages)]

    def exchange_all(self, messages):
        return [self.permute(row, col, x) for x, (_, _, row, col) in zip(messages, self.ranges[1:])]


def whole(memory=pltpu.VMEM):
    return pl.BlockSpec(memory_space=memory)


def call(kernel, name, in_specs, out_specs, out_shape, scratch, mib, cost, aliases=None):
    return pl.pallas_call(
        kernel,
        in_specs=in_specs,
        out_specs=out_specs,
        out_shape=out_shape,
        scratch_shapes=scratch,
        compiler_params=pltpu.CompilerParams(vmem_limit_bytes=mib * 1024 * 1024),
        cost_estimate=pl.CostEstimate(
            flops=int(cost * 1e9), bytes_accessed=int(cost * 2e6), transcendentals=0
        ),
        input_output_aliases=aliases or {},
        name=name,
    )


def pick(table, place):
    value = jnp.int32(table[0])
    for index, entry in enumerate(table[1:], 1):
        if entry != table[0]:
            value = jnp.where(place == index, entry, value)
    return value


def relay(blocks):
    held = [[(s, (s % 2 == 0) != bool(chain)) for s in range(blocks)] for chain in range(2)]
    fresh = [[] for _ in range(blocks)]
    for number in range(1, blocks):
        for chain in range(2):
            moved = [held[chain][a] for a in swap(blocks, chain, number)]
            held[chain] = moved
            for s, (block, keys) in enumerate(moved):
                if block != s and keys == (block < s) and block not in [b for _, b in fresh[s]]:
                    fresh[s].append(((chain, number), block))
    batches = []
    for n in range(blocks - 1):
        steps = sorted({fresh[s][n][0] for s in range(blocks)}, key=lambda step: step[::-1])
        which = [steps.index(fresh[s][n][0]) for s in range(blocks)]
        batches.append((steps, which, [fresh[s][n][1] for s in range(blocks)]))
    return batches


def swap(blocks, chain, number):
    start = (chain + number + 1) % 2
    partner = list(range(blocks))
    for low in range(start, blocks - 1, 2):
        partner[low], partner[low + 1] = low + 1, low
    return partner


def tidy(geo, arrays, blocks):
    width = arrays[0].shape[-1]
    tokens, tile_h = geo.tokens, geo.tile_h

    def kernel(*refs):
        ins, (own_ref, even_ref, odd_ref, stage, sems) = refs[:4], refs[4:]
        copies = [
            pltpu.make_async_copy(ref, stage.at[number], sems.at[number])
            for number, ref in enumerate(ins)
        ]
        for copy in copies:
            copy.start()
        for number, copy in enumerate(copies):
            copy.wait()
            for group in range(geo.groups):
                own_ref[number, group * tile_h : (group + 1) * tile_h, :] = stage[number, group]
        odd = lax.rem(lax.axis_index("span"), 2)
        even_ref[...] = own_ref[pl.ds(2 * odd, 2)]
        odd_ref[...] = own_ref[pl.ds(2 - 2 * odd, 2)]

    pair = jax.ShapeDtypeStruct((2, tokens, width), jnp.bfloat16)
    return call(
        kernel,
        "tidy",
        [whole(pltpu.HBM)] * 4,
        [whole()] * 3,
        [jax.ShapeDtypeStruct((4, tokens, width), jnp.bfloat16), pair, pair],
        [
            pltpu.VMEM((4, geo.groups, tile_h, width), jnp.bfloat16),
            pltpu.SemaphoreType.DMA((4,)),
        ],
        60,
        2,
    )(*arrays)


def pack_rows(geo, which, candidates, after, every=False):
    places = geo.places if every else geo.row_places
    select = geo.all_select if every else geo.row_select
    count, tokens, width = candidates[0].shape
    several = len(candidates) > 1
    sides = len(places)

    def kernel(select_ref, *refs):
        ins, outs = refs[: len(candidates)], refs[len(candidates) + len(after) :]
        chosen = select_ref[geo.which()]
        pieces = outs[1:] if several else outs
        number = pick(which, lax.axis_index("span"))

        def work(x_ref):
            for a in range(count):
                x = x_ref[a]
                if several:
                    outs[0][a] = x
                picked = dot_nn(chosen, x).astype(jnp.bfloat16)
                for out, (start, size) in zip(pieces[a // 2 * sides :], places):
                    out[a % 2] = picked[start - tokens : start - tokens + size]

        if not several:
            work(ins[0])
            return
        for index, ref in enumerate(ins):
            pl.when(number == index)(functools.partial(work, ref))

    sizes = [tokens] if several else []
    sizes += [size for _, size in places] * (count // 2)
    out = call(
        kernel,
        "pack_rows",
        [whole()] * (1 + len(candidates)) + [whole(pl.ANY)] * len(after),
        [whole()] * len(sizes),
        [jax.ShapeDtypeStruct((2, size, width), jnp.bfloat16) for size in sizes],
        [],
        12,
        0.2,
    )(select, *candidates, *after)
    return (out[0], out[1:]) if several else (candidates[0], out)


def pack_cols(geo, x, base, rows, after):
    count, tokens, width = 2, *x.shape[1:]

    def kernel(select_ref, x_ref, *refs):
        row_refs, refs = refs[: len(rows)], refs[len(rows) + len(after) :]
        outs, tall = refs[:-1], refs[-1]
        chosen = select_ref[geo.which()]
        for a in range(count):
            tall[a, :tokens] = x_ref[base + a]
            for ref, (start, size) in zip(row_refs, geo.row_places):
                tall[a, start : start + size] = ref[a]
            picked = dot_nn(chosen, tall[a]).astype(jnp.bfloat16)
            for out, (start, size) in zip(outs, geo.col_places):
                out[a] = picked[start - geo.tall : start - geo.tall + size]

    return call(
        kernel,
        "pack_cols",
        [whole()] * (2 + len(rows)) + [whole(pl.ANY)] * len(after),
        [whole()] * len(geo.col_places),
        [jax.ShapeDtypeStruct((count, size, width), jnp.bfloat16) for _, size in geo.col_places],
        [pltpu.VMEM((count, geo.tall, width), jnp.bfloat16)],
        12,
        0.2,
    )(geo.col_select, x, *rows, *after)


def set_bias(bias_ref, gap):
    for reach in range(1, RMAX + 1):
        bias_ref[reach - 1] = jnp.where(gap <= reach, 0.0, -jnp.inf)


def fit(x, lanes):
    return x if x.shape[1] == lanes else jnp.broadcast_to(x[:, :1], (x.shape[0], lanes))


def repeat(x, lanes):
    return jnp.concatenate([x] * (lanes // LANES), axis=1)


def spread(geo, base, parts, wide):
    for a in range(2):
        wide[a, : geo.tokens] = parts[0][base + a]
        places = geo.row_places + geo.col_places
        if len(parts) > 1 + len(places):
            places = geo.places
        for ref, (start, size) in zip(parts[1:], places):
            wide[a, start : start + size] = ref[a]
        if geo.wide > geo.used:
            wide[a, geo.used :] = jnp.zeros((geo.wide - geo.used, wide.shape[-1]), jnp.bfloat16)


def lay_out(geo, parts):
    def kernel(*refs):
        spread(geo, 2, refs[:-1], refs[-1])

    return call(
        kernel,
        "lay_out",
        [whole()] * len(parts),
        whole(),
        jax.ShapeDtypeStruct((2, geo.wide, parts[0].shape[-1]), jnp.bfloat16),
        [],
        12,
        0.1,
    )(*parts)


def forward(geo, blocks, heads, small, own, sources, parts, state, last, after):
    tokens, wide_rows = geo.tokens, geo.wide
    count, width = 2, own.shape[-1]
    depth = width // heads
    scale = LOG2E / math.sqrt(depth)
    per = len(parts)
    stat_rows = round_up(2 * heads, 8)
    first = state is None
    lanes = [slice(h * depth, (h + 1) * depth) for h in range(heads)]

    def kernel(radius_ref, live_ref, gap_ref, frame_ref, select_ref, own_ref, *refs):
        parts_refs, refs = refs[:per], refs[per:]
        state_in, refs = (None, refs) if first else (refs[:3], refs[3:])
        wide, *refs = refs[len(after) :]
        if last:
            outs, (accum, top, total, bias_ref) = refs[:4], refs[4:]
        else:
            accum, top, total, bias_ref = refs
        place = lax.axis_index("span")
        source = place if first else pick(sources, place)
        active = source <= place

        spread(geo, 0, parts_refs, wide)
        if first:
            accum[...] = jnp.zeros(accum.shape, jnp.float32)
            top[...] = jnp.full(top.shape, -jnp.inf, jnp.float32)
            total[...] = jnp.zeros(total.shape, jnp.float32)
        else:
            for old, new in zip(state_in, (accum, top, total)):
                new[...] = old[...]

        def attend():
            live = live_ref[source]
            set_bias(bias_ref, jnp.where(frame_ref[...] < live, geo.near(gap_ref), FAR))
            ones = jnp.ones((wide_rows, LANES), jnp.bfloat16)
            ahead = dot_nt(own_ref[2, :, lanes[0]], wide[0, :, lanes[0]])
            for h in range(heads):
                score = ahead
                if h + 1 < heads:
                    ahead = dot_nt(own_ref[2, :, lanes[h + 1]], wide[0, :, lanes[h + 1]])
                score = score * scale + bias_ref[radius_ref[h] - 1]
                best = jnp.max(score, axis=1, keepdims=True)
                new_top = jnp.maximum(top[h], best)
                fading = jnp.exp2(top[h] - new_top)
                top[h] = new_top
                weight = jnp.exp2(score - repeat(new_top, wide_rows)).astype(jnp.bfloat16)
                value = jnp.concatenate([wide[1, :, lanes[h]], ones], axis=1)
                both = dot_nn(weight, value)
                accum[:, lanes[h]] = accum[:, lanes[h]] * fit(fading, depth) + both[:, :depth]
                total[h] = total[h] * fading + both[:, depth:]

        def finish():
            attended_ref, lse_ref, delta_ref, packed_ref = outs
            lane = lax.broadcasted_iota(jnp.int32, (tokens, LANES), 1)
            column = jnp.zeros((tokens, LANES), jnp.float32)
            for h in range(heads):
                rounded = (accum[:, lanes[h]] / fit(total[h], depth)).astype(jnp.bfloat16)
                rounded = rounded.astype(jnp.float32)
                accum[:, lanes[h]] = rounded
                lse = top[h] + jnp.log2(total[h])
                grad = own_ref[3, :, lanes[h]].astype(jnp.float32)
                delta = jnp.sum(rounded * grad, axis=1, keepdims=True)
                delta = jnp.broadcast_to(delta, (tokens, LANES))
                lse_ref[h] = lse
                delta_ref[h] = delta
                column = jnp.where(lane == h, lse, column)
                column = jnp.where(lane == heads + h, delta, column)
            packed = jnp.zeros((wide_rows, LANES), jnp.float32)
            rest = column
            chosen = select_ref[geo.which()]
            for _ in range(3):
                part = rest.astype(jnp.bfloat16)
                rest = rest - part.astype(jnp.float32)
                packed = packed + dot_nn(chosen, part)
            packed_ref[...] = jnp.transpose(packed)[:stat_rows]
            for group in range(geo.groups):
                at = slice(group * geo.tile_h, (group + 1) * geo.tile_h)
                attended_ref[group] = accum[at, :].astype(jnp.bfloat16)

        if first:
            attend()
        else:
            pl.when(active)(attend)
        if last:
            finish()

    ins = [*small, geo.gap, geo.frame[None, :], geo.select, own, *parts]
    ins += [] if first else list(state)
    stat = (heads, tokens, LANES)
    running = [(tokens, width), stat, stat]
    shapes = [jax.ShapeDtypeStruct((count, wide_rows, width), jnp.bfloat16)]
    scratch = []
    if last:
        shapes += [
            jax.ShapeDtypeStruct((geo.groups, geo.tile_h, width), jnp.bfloat16),
            jax.ShapeDtypeStruct(stat, jnp.float32),
            jax.ShapeDtypeStruct(stat, jnp.float32),
            jax.ShapeDtypeStruct((stat_rows, wide_rows), jnp.float32),
        ]
        scratch += [pltpu.VMEM(shape, jnp.float32) for shape in running]
    else:
        shapes += [jax.ShapeDtypeStruct(shape, jnp.float32) for shape in running]
    return call(
        kernel,
        "forward",
        [whole(pltpu.SMEM)] * 2 + [whole()] * (len(ins) - 2) + [whole(pl.ANY)] * len(after),
        [whole()] * len(shapes),
        shapes,
        scratch + [pltpu.VMEM((RMAX, tokens, wide_rows), jnp.float32)],
        20,
        1.5,
    )(*ins, *after)


def merge(geo, pieces, after):
    def kernel(*refs):
        out = refs[-1]
        row = refs[0][...]
        lane = lax.broadcasted_iota(jnp.int32, row.shape, 1)
        for ref, (start, *_) in zip(refs[1:], geo.ranges[1:]):
            row = jnp.where(lane >= start, ref[...], row)
        out[...] = row

    return call(
        kernel,
        "merge",
        [whole()] * len(pieces) + [whole(pl.ANY)] * len(after),
        whole(),
        jax.ShapeDtypeStruct(pieces[0].shape, jnp.float32),
        [],
        4,
        0.1,
    )(*pieces, *after)


def query_grads(geo, heads, small, own, lse, delta, sources, wides, state, last, after):
    tokens, wide_rows = geo.tokens, geo.wide
    width = own.shape[-1]
    depth = width // heads
    natural = 1.0 / math.sqrt(depth)
    scale = LOG2E * natural
    lanes = [slice(h * depth, (h + 1) * depth) for h in range(heads)]

    def kernel(radius_ref, live_ref, gap_ref, frame_ref, lse_ref, delta_ref, own_ref, *refs):
        wide_refs, refs = refs[: len(wides)], refs[len(wides) :]
        state_in, refs = (None, refs) if state is None else (refs[0], refs[1:])
        refs = refs[len(after) :]
        out, accum, bias_ref = refs if last else (None, *refs)
        place = lax.axis_index("span")
        accum[...] = jnp.zeros(accum.shape, jnp.float32) if state is None else state_in[...]

        def step(wide, source):
            live = live_ref[source]
            set_bias(bias_ref, jnp.where(frame_ref[...] < live, geo.near(gap_ref), FAR))

            def products(h):
                return (
                    dot_nt(own_ref[2, :, lanes[h]], wide[0, :, lanes[h]]),
                    dot_nt(own_ref[3, :, lanes[h]], wide[1, :, lanes[h]]),
                )

            ahead = products(0)
            for h in range(heads):
                score, push = ahead
                if h + 1 < heads:
                    ahead = products(h + 1)
                score = score * scale + bias_ref[radius_ref[h] - 1]
                prob = jnp.exp2(score - repeat(lse_ref[h], wide_rows))
                slope = prob * (push - repeat(delta_ref[h], wide_rows))
                accum[:, lanes[h]] += dot_nn(slope.astype(jnp.bfloat16), wide[0, :, lanes[h]])

        for wide, table in zip(wide_refs, sources):
            if table == list(range(len(table))):
                step(wide, place)
            else:
                source = pick(table, place)
                pl.when(source < place)(functools.partial(step, wide, source))
        if last:
            for group in range(geo.groups):
                at = slice(group * geo.tile_h, (group + 1) * geo.tile_h)
                out[group] = (accum[at, :] * natural).astype(jnp.bfloat16)

    ins = [*small, geo.gap, geo.frame[None, :], lse, delta, own, *wides]
    ins += [] if state is None else [state]
    running = (tokens, width)
    shape = jax.ShapeDtypeStruct(running, jnp.float32)
    if last:
        shape = jax.ShapeDtypeStruct((geo.groups, geo.tile_h, width), jnp.bfloat16)
    return call(
        kernel,
        "query_grads",
        [whole(pltpu.SMEM)] * 2 + [whole()] * (len(ins) - 2) + [whole(pl.ANY)] * len(after),
        whole(),
        shape,
        ([pltpu.VMEM(running, jnp.float32)] if last else [])
        + [pltpu.VMEM((RMAX, tokens, wide_rows), jnp.float32)],
        14,
        3,
    )(*ins, *after)


def key_grads(geo, blocks, heads, small, own, stats, sources, wides, state, last):
    tokens, wide_rows = geo.tokens, geo.wide
    width = own.shape[-1]
    depth = width // heads
    natural = 1.0 / math.sqrt(depth)
    scale = LOG2E * natural
    stat_rows = stats[0].shape[0]
    lanes = [slice(h * depth, (h + 1) * depth) for h in range(heads)]

    def kernel(radius_ref, live_ref, gap_ref, frame_ref, own_ref, *refs):
        wide_refs, refs = refs[: len(wides)], refs[len(wides) :]
        stat_refs, refs = refs[: len(stats)], refs[len(stats) :]
        state_in, refs = (None, refs) if state is None else (refs[0], refs[1:])
        outs, refs = (refs[:2], refs[2:]) if last else (None, refs)
        accum, rows, bias_ref = refs
        place = lax.axis_index("span")
        accum[...] = jnp.zeros(accum.shape, jnp.float32) if state is None else state_in[...]
        for n, ref in enumerate(stat_refs):
            rows[n] = ref[...]
        live = frame_ref[...] < live_ref[place]
        set_bias(bias_ref, jnp.where(live, geo.near(gap_ref), FAR))

        def step(wide, rotation):
            def products(h):
                return (
                    dot_nt(own_ref[0, :, lanes[h]], wide[0, :, lanes[h]]),
                    dot_nt(own_ref[1, :, lanes[h]], wide[1, :, lanes[h]]),
                )

            ahead = products(0)
            for h in range(heads):
                score, push = ahead
                if h + 1 < heads:
                    ahead = products(h + 1)
                score = score * scale + bias_ref[radius_ref[h] - 1]
                prob = jnp.exp2(score - rows[rotation, h : h + 1, :])
                accum[1, :, lanes[h]] += dot_nn(
                    prob.astype(jnp.bfloat16), wide[1, :, lanes[h]]
                )
                slope = prob * (push - rows[rotation, heads + h : heads + h + 1, :])
                accum[0, :, lanes[h]] += dot_nn(
                    slope.astype(jnp.bfloat16), wide[0, :, lanes[h]]
                )

        for wide, table in zip(wide_refs, sources):
            if table == list(range(blocks)):
                step(wide, 0)
            else:
                source = pick(table, place)
                rotation = lax.rem(place - source + blocks, blocks)
                pl.when(source > place)(functools.partial(step, wide, rotation - 1))
        if last:
            for group in range(geo.groups):
                at = slice(group * geo.tile_h, (group + 1) * geo.tile_h)
                outs[0][group] = (accum[0, at, :] * natural).astype(jnp.bfloat16)
                outs[1][group] = accum[1, at, :].astype(jnp.bfloat16)

    ins = [*small, geo.gap, geo.frame[:tokens, None], own, *wides, *stats]
    ins += [] if state is None else [state]
    running = (2, tokens, width)
    shapes = [jax.ShapeDtypeStruct(running, jnp.float32)]
    if last:
        shapes = [jax.ShapeDtypeStruct((geo.groups, geo.tile_h, width), jnp.bfloat16)] * 2
    return call(
        kernel,
        "key_grads",
        [whole(pltpu.SMEM)] * 2 + [whole()] * (len(ins) - 2),
        [whole()] * len(shapes),
        shapes,
        ([pltpu.VMEM(running, jnp.float32)] if last else [])
        + [
            pltpu.VMEM((len(stats), stat_rows, wide_rows), jnp.float32),
            pltpu.VMEM((RMAX, tokens, wide_rows), jnp.float32),
        ],
        10 + 2 * len(wides),
        3,
    )(*ins)


def rotate(x, by, blocks):
    return lax.ppermute(x, "span", [(i, (i + by) % blocks) for i in range(blocks)])


def shards(queries, cache_keys, cache_values, grad_attended, radius, frame_count, sizes):
    blocks, count_h, count_w = sizes
    frames, tile_h, tile_w, width = queries.shape[1:]
    heads = radius.shape[0]
    geo = Geometry(frames, tile_h, tile_w, count_h, count_w)
    small = (radius, frame_count)

    def grouped(x):
        return jnp.transpose(x[0], (0, 2, 1, 3)).reshape(geo.groups, tile_h, width)

    def restored(x):
        x = x.reshape(frames, tile_w, tile_h, width)
        return jnp.transpose(x, (0, 2, 1, 3))[None]

    arrays = [grouped(x) for x in (cache_keys, cache_values, queries, grad_attended)]
    own, *chains = tidy(geo, arrays, blocks)
    batches = relay(blocks)
    needed = {step for steps, _, _ in batches for step in steps}
    sources = [list(range(blocks))] + [blks for _, _, blks in batches]
    moved = {}

    def hop(chain, number, after):
        if any(c == chain and n >= number for c, n in needed):
            x = chains[chain]
            x = lax.optimization_barrier((x, *after))[0] if after else x
            pairs = list(enumerate(swap(blocks, chain, number)))
            moved[chain, number] = chains[chain] = lax.ppermute(x, "span", pairs)

    def take(n, after):
        steps, which, _ = batches[n - 1]
        final = n == blocks - 1
        return pack_rows(geo, which, [moved[step] for step in steps], after, final)

    hop(0, 1, [])
    hop(1, 1, [])
    x, messages = pack_rows(geo, [0] * blocks, [own], [])
    half = len(geo.row_places)
    asked, pieces = messages[half:], geo.exchange_rows(messages[:half])
    wides, state = [], None
    for n in range(blocks):
        last = n == blocks - 1
        ready = []
        if n == 0 or not last:
            messages = pack_cols(geo, x, 0, pieces, [state[0]] if state else [])
            ready = list(messages[:1])
            pieces = pieces + geo.exchange_cols(messages)
        parts, after = [x] + pieces, []
        if n == 0:
            asked = geo.exchange_rows(lax.optimization_barrier((*asked, *ready))[:half])
        if not last:
            hop(0, n + 2, [state[0]] if state else ready)
            x, messages = take(n + 1, ready)
            after = list(messages[:1])
            hop(1, n + 2, after)
            if n == 1:
                cols = geo.exchange_cols(pack_cols(geo, own, 2, asked, after))
                asked = lay_out(geo, [own] + asked + cols)
            if n == blocks - 2:
                after = after + [asked] if n > 1 else after
                pieces = geo.exchange_all(messages)
            else:
                pieces = geo.exchange_rows(messages)
        wide, *state = forward(
            geo, blocks, heads, small, own, sources[n], parts, state, last, after
        )
        wides.append(wide)
    if blocks < 3:
        cols = geo.exchange_cols(pack_cols(geo, own, 2, asked, [state[0]]))
        asked = lay_out(geo, [own] + asked + cols)
    attended, lse, delta, packed = state
    cut = (blocks + 1) // 2

    def query_part(first, end, begun, after):
        return query_grads(
            geo, heads, small, own, lse, delta, sources[first:end], wides[first:end], begun,
            end == blocks, after,
        )

    def key_part(first, end, brought, begun):
        return key_grads(
            geo, blocks, heads, small, own, brought, sources[first:end], ([asked] + wides[1:])[first:end],
            begun, end == blocks,
        )

    begun = query_part(0, cut, None, [])
    own_stats = merge(geo, [packed] + geo.exchange_all([packed] * len(geo.places)), [begun])
    stats = [rotate(own_stats, n, blocks) for n in range(1, blocks)]
    grad_q = query_part(cut, blocks, begun, [own_stats])
    begun = key_part(0, 1, [own_stats], None)[0]
    grad_k, grad_v = key_part(1, blocks, stats, begun)
    return tuple(restored(x) for x in (attended, grad_q, grad_k, grad_v))


def solution(mesh):
    placed = P("span", None, "ha", "wa", None)
    sizes = tuple(mesh.shape[name] for name in ("span", "ha", "wa"))
    return jax.shard_map(
        functools.partial(shards, sizes=sizes),
        mesh=mesh,
        in_specs=(placed,) * 4 + (P(), P()),
        out_specs=(placed,) * 4,
        check_vma=False,
    )
```

```python
import functools
import math

import jax
import jax.numpy as jnp
import ml_dtypes
import numpy as np
from jax import lax
from jax.experimental import pallas as pl
from jax.experimental.pallas import tpu as pltpu
from jax.sharding import PartitionSpec as P

RMAX = 2
FAR = 99.0
LOG2E = math.log2(math.e)
LANES = 128


def round_up(value, unit):
    return (value + unit - 1) // unit * unit


def dot_nt(a, b):
    return lax.dot_general(a, b, (((1,), (1,)), ((), ())), preferred_element_type=jnp.float32)


def dot_nn(a, b):
    return lax.dot_general(a, b, (((1,), (0,)), ((), ())), preferred_element_type=jnp.float32)


class Side:
    def __init__(self, kind, count, tile, variant):
        self.count = count
        self.swap = kind == "swap"
        if kind == "same":
            self.delta, self.start, self.length, self.send_start = 0, 0, tile, 0
        else:
            self.delta = 1 - 2 * variant if self.swap else kind
            send_up = (variant == 0) if self.swap else (kind < 0)
            self.length = RMAX
            self.start = tile if self.delta > 0 else -RMAX
            self.send_start = tile - RMAX if send_up else 0
        shift = 1 if self.swap else self.delta
        self.pairs = [((i + shift) % count, i) for i in range(count)]

    def place(self, index):
        delta = 1 - 2 * index if self.swap else self.delta
        other = index + delta
        inside = (other >= 0) & (other < self.count)
        return jnp.where(inside, other, index), inside


def sides(count, tile, variant):
    kinds = [] if count == 1 else ["swap"] if count == 2 else [-1, 1]
    return [Side(kind, count, tile, variant) for kind in ["same"] + kinds]


class Geometry:
    def __init__(self, frames, tile_h, tile_w, count_h, count_w):
        self.frames, self.tile_h, self.tile_w = frames, tile_h, tile_w
        self.count_h, self.count_w = count_h, count_w
        self.tokens = frames * tile_h * tile_w
        self.groups = frames * tile_w
        self.variants_h = 2 if count_h == 2 else 1
        self.variants_w = 2 if count_w == 2 else 1
        found = [
            self.variant(variant_h, variant_w)
            for variant_h in range(self.variants_h)
            for variant_w in range(self.variants_w)
        ]
        direct, tall, gap = (np.stack(arrays) for arrays in zip(*found))
        own = np.arange(self.tokens)
        starts = [start for start, *_ in self.ranges] + [self.used]
        self.places = [(a, b - a) for a, b in zip(starts, starts[1:])][1:]
        self.all_select = self.one_hot(direct[:, self.tokens : self.used], self.tokens)
        self.row_select = self.one_hot(direct[:, self.tokens : self.tall], self.tokens)
        self.col_select = self.one_hot(tall[:, self.tall : self.used], self.tall)
        self.select = self.one_hot(direct, self.tokens)
        self.gap = gap.astype(np.float32)
        assert (direct[:, : self.tokens] == own).all()

    def one_hot(self, index, count):
        return (index[..., None] == np.arange(count)).astype(ml_dtypes.bfloat16)

    def variant(self, variant_h, variant_w):
        row_own, *rows_of = sides(self.count_h, self.tile_h, variant_h)
        col_own, *cols_of = sides(self.count_w, self.tile_w, variant_w)
        self.row_sides, self.col_sides = rows_of, cols_of
        direct, tall, rows, cols, frame = [], [], [], [], []
        self.ranges = []

        def add(row, col, base):
            ff, xx, yy = np.unravel_index(
                np.arange(self.frames * col.length * row.length),
                (self.frames, col.length, row.length),
            )
            start = len(direct)
            own_x, own_y = col.send_start + xx, row.send_start + yy
            direct.extend((ff * self.tile_w + own_x) * self.tile_h + own_y)
            tall.extend(base + (ff * self.tile_w + own_x) * row.length + yy)
            rows.extend(row.start + yy)
            cols.extend(col.start + xx)
            frame.extend(ff)
            self.ranges.append((start, len(direct), row, col))

        def pad(unit):
            count = round_up(len(direct), unit) - len(direct)
            for array, value in zip((direct, tall, rows, cols, frame), (-1, -1, 1000, 1000, 0)):
                array.extend([value] * count)

        add(row_own, col_own, 0)
        bases = []
        self.row_places, self.col_places = [], []
        for row in rows_of:
            bases.append(len(direct))
            add(row, col_own, bases[-1])
            pad(16)
            self.row_places.append((bases[-1], len(direct) - bases[-1]))
        self.tall = len(direct)
        for col in cols_of:
            start = len(direct)
            for row, base in zip([row_own] + rows_of, [0] + bases):
                add(row, col, base)
                pad(16)
            self.col_places.append((start, len(direct) - start))
        self.used = len(direct)
        pad(LANES)
        self.wide = len(direct)
        self.frame = np.array(frame, np.int32)
        rows, cols = np.array(rows), np.array(cols)
        mine = slice(0, self.tokens)
        gap = np.maximum(
            np.abs(rows[mine][:, None] - rows[None, :]), np.abs(cols[mine][:, None] - cols[None, :])
        )
        return np.array(direct), np.array(tall), np.minimum(gap, FAR)

    def which(self):
        at_h = lax.axis_index("ha") if self.variants_h == 2 else 0
        at_w = lax.axis_index("wa") if self.variants_w == 2 else 0
        return at_h * self.variants_w + at_w

    def near(self, gap_ref):
        lane = lax.broadcasted_iota(jnp.int32, (1, self.wide), 1)
        far = jnp.zeros((1, self.wide), jnp.float32)
        for start, end, row, col in self.ranges[1:]:
            inside = row.place(lax.axis_index("ha"))[1] & col.place(lax.axis_index("wa"))[1]
            cost = jnp.where(inside, 0.0, FAR)
            far = jnp.where((lane >= start) & (lane < end), cost, far)
        return gap_ref[self.which()] + far

    def permute(self, row, col, x):
        pairs = [
            (a * self.count_w + c, b * self.count_w + d)
            for a, b in row.pairs
            for c, d in col.pairs
        ]
        return lax.ppermute(x, ("ha", "wa"), pairs)

    def exchange_rows(self, messages):
        own = self.ranges[0][3]
        return [self.permute(row, own, x) for row, x in zip(self.row_sides, messages)]

    def exchange_cols(self, messages):
        own = self.ranges[0][2]
        return [self.permute(own, col, x) for col, x in zip(self.col_sides, messages)]

    def exchange_all(self, messages):
        return [self.permute(row, col, x) for x, (_, _, row, col) in zip(messages, self.ranges[1:])]


def whole(memory=pltpu.VMEM):
    return pl.BlockSpec(memory_space=memory)


def call(kernel, name, in_specs, out_specs, out_shape, scratch, mib, cost, aliases=None):
    return pl.pallas_call(
        kernel,
        in_specs=in_specs,
        out_specs=out_specs,
        out_shape=out_shape,
        scratch_shapes=scratch,
        compiler_params=pltpu.CompilerParams(vmem_limit_bytes=mib * 1024 * 1024),
        cost_estimate=pl.CostEstimate(
            flops=int(cost * 1e9), bytes_accessed=int(cost * 2e6), transcendentals=0
        ),
        input_output_aliases=aliases or {},
        name=name,
    )


def pick(table, place):
    value = jnp.int32(table[0])
    for index, entry in enumerate(table[1:], 1):
        if entry != table[0]:
            value = jnp.where(place == index, entry, value)
    return value


def relay(blocks):
    held = [[(s, (s % 2 == 0) != bool(chain)) for s in range(blocks)] for chain in range(2)]
    fresh = [[] for _ in range(blocks)]
    for number in range(1, blocks):
        for chain in range(2):
            moved = [held[chain][a] for a in swap(blocks, chain, number)]
            held[chain] = moved
            for s, (block, keys) in enumerate(moved):
                if block != s and keys == (block < s) and block not in [b for _, b in fresh[s]]:
                    fresh[s].append(((chain, number), block))
    batches = []
    for n in range(blocks - 1):
        steps = sorted({fresh[s][n][0] for s in range(blocks)}, key=lambda step: step[::-1])
        which = [steps.index(fresh[s][n][0]) for s in range(blocks)]
        batches.append((steps, which, [fresh[s][n][1] for s in range(blocks)]))
    return batches


def swap(blocks, chain, number):
    start = (chain + number + 1) % 2
    partner = list(range(blocks))
    for low in range(start, blocks - 1, 2):
        partner[low], partner[low + 1] = low + 1, low
    return partner


def tidy(geo, arrays, blocks):
    width = arrays[0].shape[-1]
    tokens, tile_h = geo.tokens, geo.tile_h

    def kernel(*refs):
        ins, (own_ref, even_ref, odd_ref, stage, sems) = refs[:4], refs[4:]
        copies = [
            pltpu.make_async_copy(ref, stage.at[number], sems.at[number])
            for number, ref in enumerate(ins)
        ]
        for copy in copies:
            copy.start()
        for number, copy in enumerate(copies):
            copy.wait()
            for group in range(geo.groups):
                own_ref[number, group * tile_h : (group + 1) * tile_h, :] = stage[number, group]
        odd = lax.rem(lax.axis_index("span"), 2)
        even_ref[...] = own_ref[pl.ds(2 * odd, 2)]
        odd_ref[...] = own_ref[pl.ds(2 - 2 * odd, 2)]

    pair = jax.ShapeDtypeStruct((2, tokens, width), jnp.bfloat16)
    return call(
        kernel,
        "tidy",
        [whole(pltpu.HBM)] * 4,
        [whole()] * 3,
        [jax.ShapeDtypeStruct((4, tokens, width), jnp.bfloat16), pair, pair],
        [
            pltpu.VMEM((4, geo.groups, tile_h, width), jnp.bfloat16),
            pltpu.SemaphoreType.DMA((4,)),
        ],
        60,
        2,
    )(*arrays)


def pack_rows(geo, which, candidates, extra, after, every=False):
    places = geo.places if every else geo.row_places
    select = geo.all_select if every else geo.row_select
    _, tokens, width = candidates[0].shape
    several = len(candidates) > 1
    ins = candidates + extra

    def kernel(select_ref, *refs):
        refs, outs = refs[: len(ins)], refs[len(ins) + len(after) :]
        chosen = select_ref[geo.which()]
        pieces = outs[1:] if several else outs
        number = pick(which, lax.axis_index("span"))

        def send(x, a):
            picked = dot_nn(chosen, x).astype(jnp.bfloat16)
            for out, (start, size) in zip(pieces, places):
                out[a] = picked[start - tokens : start - tokens + size]

        def work(x_ref):
            for a in range(2):
                x = x_ref[a]
                if several:
                    outs[0][a] = x
                send(x, a)

        if several:
            for index in range(len(candidates)):
                pl.when(number == index)(functools.partial(work, refs[index]))
        else:
            work(refs[0])
        for ref in refs[len(candidates) :]:
            for a in range(2):
                send(ref[2 + a], 2 + a)

    count = 2 + 2 * len(extra)
    shapes = [jax.ShapeDtypeStruct((2, tokens, width), jnp.bfloat16)] if several else []
    shapes += [jax.ShapeDtypeStruct((count, size, width), jnp.bfloat16) for _, size in places]
    out = call(
        kernel,
        "pack_rows",
        [whole()] * (1 + len(ins)) + [whole(pl.ANY)] * len(after),
        [whole()] * len(shapes),
        shapes,
        [],
        12,
        0.2,
    )(select, *ins, *after)
    return (out[0], out[1:]) if several else (candidates[0], out)


def pack_cols(geo, x, extra, rows, after):
    count = 2 + 2 * len(extra)
    _, tokens, width = x.shape

    def kernel(select_ref, *refs):
        xs, refs = refs[: 1 + len(extra)], refs[1 + len(extra) :]
        row_refs, refs = refs[: len(rows)], refs[len(rows) + len(after) :]
        outs, tall = refs[:-1], refs[-1]
        chosen = select_ref[geo.which()]
        for a in range(count):
            tall[a, :tokens] = xs[a // 2][a]
            for ref, (start, size) in zip(row_refs, geo.row_places):
                tall[a, start : start + size] = ref[a]
            picked = dot_nn(chosen, tall[a]).astype(jnp.bfloat16)
            for out, (start, size) in zip(outs, geo.col_places):
                out[a] = picked[start - geo.tall : start - geo.tall + size]

    return call(
        kernel,
        "pack_cols",
        [whole()] * (2 + len(extra) + len(rows)) + [whole(pl.ANY)] * len(after),
        [whole()] * len(geo.col_places),
        [jax.ShapeDtypeStruct((count, size, width), jnp.bfloat16) for _, size in geo.col_places],
        [pltpu.VMEM((count, geo.tall, width), jnp.bfloat16)],
        12,
        0.2,
    )(geo.col_select, x, *extra, *rows, *after)


def set_bias(bias_ref, gap):
    for reach in range(1, RMAX + 1):
        bias_ref[reach - 1] = jnp.where(gap <= reach, 0.0, -jnp.inf)


def fit(x, lanes):
    return x if x.shape[1] == lanes else jnp.broadcast_to(x[:, :1], (x.shape[0], lanes))


def repeat(x, lanes):
    return jnp.concatenate([x] * (lanes // LANES), axis=1)


def spread(geo, base, parts, wide):
    places = geo.row_places + geo.col_places
    if len(parts) > 1 + len(places):
        places = geo.places
    for a in range(2):
        wide[a, : geo.tokens] = parts[0][base + a]
        for ref, (start, size) in zip(parts[1:], places):
            wide[a, start : start + size] = ref[base + a]
        if geo.wide > geo.used:
            wide[a, geo.used :] = jnp.zeros((geo.wide - geo.used, wide.shape[-1]), jnp.bfloat16)


def lay_out(geo, heads, small, own, parts):
    tokens, wide_rows = geo.tokens, geo.wide
    width = own.shape[-1]
    depth = width // heads
    scale = LOG2E / math.sqrt(depth)

    def kernel(radius_ref, live_ref, gap_ref, row_frame_ref, own_ref, *refs):
        parts_refs, (wide, products, bias_ref) = refs[: len(parts)], refs[len(parts) :]
        spread(geo, 2, parts_refs, wide)
        live = row_frame_ref[...] < live_ref[lax.axis_index("span")]
        set_bias(bias_ref, jnp.where(live, geo.near(gap_ref), FAR))
        for h in range(heads):
            lanes = slice(h * depth, (h + 1) * depth)
            score = dot_nt(own_ref[0, :, lanes], wide[0, :, lanes])
            products[0, h] = score * scale + bias_ref[radius_ref[h] - 1]
            products[1, h] = dot_nt(own_ref[1, :, lanes], wide[1, :, lanes])

    return call(
        kernel,
        "lay_out",
        [whole(pltpu.SMEM)] * 2 + [whole()] * (3 + len(parts)),
        [whole()] * 2,
        [
            jax.ShapeDtypeStruct((2, wide_rows, width), jnp.bfloat16),
            jax.ShapeDtypeStruct((2, heads, tokens, wide_rows), jnp.float32),
        ],
        [pltpu.VMEM((RMAX, tokens, wide_rows), jnp.float32)],
        16,
        0.5,
    )(*small, geo.gap, geo.frame[:tokens, None], own, *parts)


def forward(geo, blocks, heads, small, own, sources, parts, state, last, after):
    tokens, wide_rows = geo.tokens, geo.wide
    width = own.shape[-1]
    depth = width // heads
    scale = LOG2E / math.sqrt(depth)
    per = len(parts)
    stat_rows = round_up(2 * heads, 8)
    first = state is None
    lanes = [slice(h * depth, (h + 1) * depth) for h in range(heads)]

    def kernel(
        radius_ref, live_ref, gap_ref, frame_ref, row_frame_ref, select_ref, own_ref, *refs
    ):
        parts_refs, refs = refs[:per], refs[per:]
        state_in, refs = (None, refs) if first else (refs[:3], refs[3:])
        wide, products, *refs = refs[len(after) :]
        if last:
            outs, (accum, top, total, bias_ref) = refs[:4], refs[4:]
        else:
            accum, top, total, bias_ref = refs
        place = lax.axis_index("span")
        source = place if first else pick(sources, place)
        active = source <= place

        spread(geo, 0, parts_refs, wide)
        if first:
            accum[...] = jnp.zeros(accum.shape, jnp.float32)
            top[...] = jnp.full(top.shape, -jnp.inf, jnp.float32)
            total[...] = jnp.zeros(total.shape, jnp.float32)
        else:
            for old, new in zip(state_in, (accum, top, total)):
                new[...] = old[...]

        def multiply(h, base):
            score = dot_nt(own_ref[base, :, lanes[h]], wide[0, :, lanes[h]])
            score = score * scale + bias_ref[radius_ref[h] - 1]
            products[0, h] = score
            products[1, h] = dot_nt(own_ref[base + 1, :, lanes[h]], wide[1, :, lanes[h]])
            return score

        def attend():
            live = frame_ref[...] < live_ref[source]
            set_bias(bias_ref, jnp.where(live, geo.near(gap_ref), FAR))
            ones = jnp.ones((wide_rows, LANES), jnp.bfloat16)
            ahead = multiply(0, 2)
            for h in range(heads):
                score = ahead
                if h + 1 < heads:
                    ahead = multiply(h + 1, 2)
                best = jnp.max(score, axis=1, keepdims=True)
                new_top = jnp.maximum(top[h], best)
                fading = jnp.exp2(top[h] - new_top)
                top[h] = new_top
                weight = jnp.exp2(score - repeat(new_top, wide_rows)).astype(jnp.bfloat16)
                value = jnp.concatenate([wide[1, :, lanes[h]], ones], axis=1)
                both = dot_nn(weight, value)
                accum[:, lanes[h]] = accum[:, lanes[h]] * fit(fading, depth) + both[:, :depth]
                total[h] = total[h] * fading + both[:, depth:]

        def keep():
            live = row_frame_ref[...] < live_ref[place]
            set_bias(bias_ref, jnp.where(live, geo.near(gap_ref), FAR))
            for h in range(heads):
                multiply(h, 0)

        def finish():
            attended_ref, lse_ref, delta_ref, packed_ref = outs
            lane = lax.broadcasted_iota(jnp.int32, (tokens, LANES), 1)
            column = jnp.zeros((tokens, LANES), jnp.float32)
            for h in range(heads):
                rounded = (accum[:, lanes[h]] / fit(total[h], depth)).astype(jnp.bfloat16)
                rounded = rounded.astype(jnp.float32)
                accum[:, lanes[h]] = rounded
                lse = top[h] + jnp.log2(total[h])
                grad = own_ref[3, :, lanes[h]].astype(jnp.float32)
                delta = jnp.sum(rounded * grad, axis=1, keepdims=True)
                delta = jnp.broadcast_to(delta, (tokens, LANES))
                lse_ref[h] = lse
                delta_ref[h] = delta
                column = jnp.where(lane == h, lse, column)
                column = jnp.where(lane == heads + h, delta, column)
            packed = jnp.zeros((wide_rows, LANES), jnp.float32)
            rest = column
            chosen = select_ref[geo.which()]
            for _ in range(3):
                part = rest.astype(jnp.bfloat16)
                rest = rest - part.astype(jnp.float32)
                packed = packed + dot_nn(chosen, part)
            packed_ref[...] = jnp.transpose(packed)[:stat_rows]
            for group in range(geo.groups):
                at = slice(group * geo.tile_h, (group + 1) * geo.tile_h)
                attended_ref[group] = accum[at, :].astype(jnp.bfloat16)

        if first:
            attend()
        else:
            pl.when(active)(attend)
            pl.when(jnp.logical_not(active))(keep)
        if last:
            finish()

    ins = [*small, geo.gap, geo.frame[None, :], geo.frame[:tokens, None], geo.select, own, *parts]
    ins += [] if first else list(state)
    stat = (heads, tokens, LANES)
    running = [(tokens, width), stat, stat]
    shapes = [
        jax.ShapeDtypeStruct((2, wide_rows, width), jnp.bfloat16),
        jax.ShapeDtypeStruct((2, heads, tokens, wide_rows), jnp.float32),
    ]
    scratch = []
    if last:
        shapes += [
            jax.ShapeDtypeStruct((geo.groups, geo.tile_h, width), jnp.bfloat16),
            jax.ShapeDtypeStruct(stat, jnp.float32),
            jax.ShapeDtypeStruct(stat, jnp.float32),
            jax.ShapeDtypeStruct((stat_rows, wide_rows), jnp.float32),
        ]
        scratch += [pltpu.VMEM(shape, jnp.float32) for shape in running]
    else:
        shapes += [jax.ShapeDtypeStruct(shape, jnp.float32) for shape in running]
    return call(
        kernel,
        "forward",
        [whole(pltpu.SMEM)] * 2 + [whole()] * (len(ins) - 2) + [whole(pl.ANY)] * len(after),
        [whole()] * len(shapes),
        shapes,
        scratch + [pltpu.VMEM((RMAX, tokens, wide_rows), jnp.float32)],
        20,
        1.5,
    )(*ins, *after)


def merge(geo, pieces, after):
    def kernel(*refs):
        out = refs[-1]
        row = refs[0][...]
        lane = lax.broadcasted_iota(jnp.int32, row.shape, 1)
        for ref, (start, *_) in zip(refs[1:], geo.ranges[1:]):
            row = jnp.where(lane >= start, ref[...], row)
        out[...] = row

    return call(
        kernel,
        "merge",
        [whole()] * len(pieces) + [whole(pl.ANY)] * len(after),
        whole(),
        jax.ShapeDtypeStruct(pieces[0].shape, jnp.float32),
        [],
        4,
        0.1,
    )(*pieces, *after)


def query_grads(geo, heads, lse, delta, sources, slots):
    tokens, wide_rows = geo.tokens, geo.wide
    width = slots[0][0].shape[-1]
    depth = width // heads
    natural = 1.0 / math.sqrt(depth)
    lanes = [slice(h * depth, (h + 1) * depth) for h in range(heads)]

    def kernel(lse_ref, delta_ref, *refs):
        slot_refs, (out, accum) = refs[: 2 * len(slots)], refs[2 * len(slots) :]
        place = lax.axis_index("span")

        def step(wide, products, first):
            for h in range(heads):
                prob = jnp.exp2(products[0, h] - repeat(lse_ref[h], wide_rows))
                slope = prob * (products[1, h] - repeat(delta_ref[h], wide_rows))
                part = dot_nn(slope.astype(jnp.bfloat16), wide[0, :, lanes[h]])
                accum[:, lanes[h]] = part if first else accum[:, lanes[h]] + part

        for n, table in enumerate(sources):
            work = functools.partial(step, slot_refs[2 * n], slot_refs[2 * n + 1], n == 0)
            if n == 0:
                work()
            else:
                pl.when(pick(table, place) < place)(work)
        for group in range(geo.groups):
            at = slice(group * geo.tile_h, (group + 1) * geo.tile_h)
            out[group] = (accum[at, :] * natural).astype(jnp.bfloat16)

    flat = [x for slot in slots for x in slot]
    return call(
        kernel,
        "query_grads",
        [whole()] * (2 + len(flat)),
        whole(),
        jax.ShapeDtypeStruct((geo.groups, geo.tile_h, width), jnp.bfloat16),
        [pltpu.VMEM((tokens, width), jnp.float32)],
        8,
        2,
    )(lse, delta, *flat)


def key_grads(geo, blocks, heads, stats, sources, slots, state, last):
    tokens, wide_rows = geo.tokens, geo.wide
    width = slots[0][0].shape[-1]
    depth = width // heads
    natural = 1.0 / math.sqrt(depth)
    stat_rows = stats[0].shape[0]
    lanes = [slice(h * depth, (h + 1) * depth) for h in range(heads)]

    def kernel(*refs):
        slot_refs, refs = refs[: 2 * len(slots)], refs[2 * len(slots) :]
        stat_refs, refs = refs[: len(stats)], refs[len(stats) :]
        state_in, refs = (None, refs) if state is None else (refs[0], refs[1:])
        outs, refs = (refs[:2], refs[2:]) if last else (None, refs)
        accum, rows = refs
        place = lax.axis_index("span")
        accum[...] = jnp.zeros(accum.shape, jnp.float32) if state is None else state_in[...]
        for n, ref in enumerate(stat_refs):
            rows[n] = ref[...]

        def step(wide, products, rotation):
            for h in range(heads):
                prob = jnp.exp2(products[0, h] - rows[rotation, h : h + 1, :])
                accum[1, :, lanes[h]] += dot_nn(prob.astype(jnp.bfloat16), wide[1, :, lanes[h]])
                slope = prob * (products[1, h] - rows[rotation, heads + h : heads + h + 1, :])
                accum[0, :, lanes[h]] += dot_nn(slope.astype(jnp.bfloat16), wide[0, :, lanes[h]])

        for n, table in enumerate(sources):
            wide, products = slot_refs[2 * n : 2 * n + 2]
            if table == list(range(blocks)):
                step(wide, products, 0)
            else:
                source = pick(table, place)
                rotation = lax.rem(place - source + blocks, blocks) - 1
                pl.when(source > place)(functools.partial(step, wide, products, rotation))
        if last:
            for group in range(geo.groups):
                at = slice(group * geo.tile_h, (group + 1) * geo.tile_h)
                outs[0][group] = (accum[0, at, :] * natural).astype(jnp.bfloat16)
                outs[1][group] = accum[1, at, :].astype(jnp.bfloat16)

    ins = [x for slot in slots for x in slot] + list(stats)
    ins += [] if state is None else [state]
    running = (2, tokens, width)
    shapes = [jax.ShapeDtypeStruct(running, jnp.float32)]
    if last:
        shapes = [jax.ShapeDtypeStruct((geo.groups, geo.tile_h, width), jnp.bfloat16)] * 2
    return call(
        kernel,
        "key_grads",
        [whole()] * len(ins),
        [whole()] * len(shapes),
        shapes,
        ([pltpu.VMEM(running, jnp.float32)] if last else [])
        + [pltpu.VMEM((len(stats), stat_rows, wide_rows), jnp.float32)],
        8,
        2,
    )(*ins)


def rotate(x, by, blocks):
    return lax.ppermute(x, "span", [(i, (i + by) % blocks) for i in range(blocks)])


def shards(queries, cache_keys, cache_values, grad_attended, radius, frame_count, sizes):
    blocks, count_h, count_w = sizes
    frames, tile_h, tile_w, width = queries.shape[1:]
    heads = radius.shape[0]
    geo = Geometry(frames, tile_h, tile_w, count_h, count_w)
    small = (radius, frame_count)

    def grouped(x):
        return jnp.transpose(x[0], (0, 2, 1, 3)).reshape(geo.groups, tile_h, width)

    def restored(x):
        x = x.reshape(frames, tile_w, tile_h, width)
        return jnp.transpose(x, (0, 2, 1, 3))[None]

    arrays = [grouped(x) for x in (cache_keys, cache_values, queries, grad_attended)]
    own, *chains = tidy(geo, arrays, blocks)
    batches = relay(blocks)
    needed = {step for steps, _, _ in batches for step in steps}
    sources = [list(range(blocks))] + [blks for _, _, blks in batches]
    moved = {}

    def hop(chain, number, after):
        if any(c == chain and n >= number for c, n in needed):
            x = chains[chain]
            x = lax.optimization_barrier((x, *after))[0] if after else x
            pairs = list(enumerate(swap(blocks, chain, number)))
            moved[chain, number] = chains[chain] = lax.ppermute(x, "span", pairs)

    def take(n, after):
        steps, which, _ = batches[n - 1]
        extra = [own] if n == 1 else []
        candidates = [moved[step] for step in steps]
        return pack_rows(geo, which, candidates, extra, after, n == blocks - 1)

    hop(0, 1, [])
    hop(1, 1, [])
    x, messages = pack_rows(geo, [0] * blocks, [own], [], [])
    pieces = geo.exchange_rows(messages)
    slots, state, asked = [], None, None
    for n in range(blocks):
        last = n == blocks - 1
        ready = []
        if n == 0 or not last:
            extra = [own] if n == 1 else []
            messages = pack_cols(geo, x, extra, pieces, [state[0]] if state else [])
            ready = list(messages[:1])
            pieces = pieces + geo.exchange_cols(messages)
        parts, after = [x] + pieces, []
        if n == 1:
            asked = lay_out(geo, heads, small, own, [own] + pieces)
        if not last:
            hop(0, n + 2, [state[0]] if state else ready)
            x, messages = take(n + 1, ready)
            after = list(messages[:1])
            hop(1, n + 2, after)
            if n == blocks - 2:
                after = after + ([asked[0]] if n > 1 else [])
                pieces = geo.exchange_all(messages)
            else:
                pieces = geo.exchange_rows(messages)
        wide, products, *state = forward(
            geo, blocks, heads, small, own, sources[n], parts, state, last, after
        )
        slots.append([wide, products])
    attended, lse, delta, packed = state

    grad_q = query_grads(geo, heads, lse, delta, sources, slots)
    brought = geo.exchange_all([packed] * len(geo.places))
    own_stats = merge(geo, [packed] + brought, [grad_q])
    stats = [rotate(own_stats, n, blocks) for n in range(1, blocks)]
    begun = key_grads(geo, blocks, heads, [own_stats], sources[:1], [asked], None, False)[0]
    grad_k, grad_v = key_grads(
        geo, blocks, heads, stats, sources[1:], slots[1:], begun, True
    )
    return tuple(restored(x) for x in (attended, grad_q, grad_k, grad_v))


def solution(mesh):
    placed = P("span", None, "ha", "wa", None)
    sizes = tuple(mesh.shape[name] for name in ("span", "ha", "wa"))
    return jax.shard_map(
        functools.partial(shards, sizes=sizes),
        mesh=mesh,
        in_specs=(placed,) * 4 + (P(), P()),
        out_specs=(placed,) * 4,
        check_vma=False,
    )
```

```python
import functools
import math

import jax
import jax.numpy as jnp
import ml_dtypes
import numpy as np
from jax import lax
from jax.experimental import pallas as pl
from jax.experimental.pallas import tpu as pltpu
from jax.sharding import PartitionSpec as P

RMAX = 2
FAR = 99.0
LOG2E = math.log2(math.e)
LANES = 128


def round_up(value, unit):
    return (value + unit - 1) // unit * unit


def dot_nt(a, b):
    return lax.dot_general(a, b, (((1,), (1,)), ((), ())), preferred_element_type=jnp.float32)


def dot_nn(a, b):
    return lax.dot_general(a, b, (((1,), (0,)), ((), ())), preferred_element_type=jnp.float32)


class Side:
    def __init__(self, kind, count, tile, variant):
        self.count = count
        self.swap = kind == "swap"
        if kind == "same":
            self.delta, self.start, self.length, self.send_start = 0, 0, tile, 0
        else:
            self.delta = 1 - 2 * variant if self.swap else kind
            send_up = (variant == 0) if self.swap else (kind < 0)
            self.length = RMAX
            self.start = tile if self.delta > 0 else -RMAX
            self.send_start = tile - RMAX if send_up else 0
        shift = 1 if self.swap else self.delta
        self.pairs = [((i + shift) % count, i) for i in range(count)]

    def place(self, index):
        delta = 1 - 2 * index if self.swap else self.delta
        other = index + delta
        inside = (other >= 0) & (other < self.count)
        return jnp.where(inside, other, index), inside


def sides(count, tile, variant):
    kinds = [] if count == 1 else ["swap"] if count == 2 else [-1, 1]
    return [Side(kind, count, tile, variant) for kind in ["same"] + kinds]


class Geometry:
    def __init__(self, frames, tile_h, tile_w, count_h, count_w):
        self.frames, self.tile_h, self.tile_w = frames, tile_h, tile_w
        self.count_h, self.count_w = count_h, count_w
        self.tokens = frames * tile_h * tile_w
        self.groups = frames * tile_w
        self.variants_h = 2 if count_h == 2 else 1
        self.variants_w = 2 if count_w == 2 else 1
        found = [
            self.variant(variant_h, variant_w)
            for variant_h in range(self.variants_h)
            for variant_w in range(self.variants_w)
        ]
        direct, tall, gap = (np.stack(arrays) for arrays in zip(*found))
        own = np.arange(self.tokens)
        starts = [start for start, *_ in self.ranges] + [self.used]
        self.places = [(a, b - a) for a, b in zip(starts, starts[1:])][1:]
        self.all_select = self.one_hot(direct[:, self.tokens : self.used], self.tokens)
        self.row_select = self.one_hot(direct[:, self.tokens : self.tall], self.tokens)
        self.col_select = self.one_hot(tall[:, self.tall : self.used], self.tall)
        self.select = self.one_hot(direct, self.tokens)
        self.gap = gap.astype(np.float32)
        assert (direct[:, : self.tokens] == own).all()

    def one_hot(self, index, count):
        return (index[..., None] == np.arange(count)).astype(ml_dtypes.bfloat16)

    def variant(self, variant_h, variant_w):
        row_own, *rows_of = sides(self.count_h, self.tile_h, variant_h)
        col_own, *cols_of = sides(self.count_w, self.tile_w, variant_w)
        self.row_sides, self.col_sides = rows_of, cols_of
        direct, tall, rows, cols, frame = [], [], [], [], []
        self.ranges = []

        def add(row, col, base):
            ff, xx, yy = np.unravel_index(
                np.arange(self.frames * col.length * row.length),
                (self.frames, col.length, row.length),
            )
            start = len(direct)
            own_x, own_y = col.send_start + xx, row.send_start + yy
            direct.extend((ff * self.tile_w + own_x) * self.tile_h + own_y)
            tall.extend(base + (ff * self.tile_w + own_x) * row.length + yy)
            rows.extend(row.start + yy)
            cols.extend(col.start + xx)
            frame.extend(ff)
            self.ranges.append((start, len(direct), row, col))

        def pad(unit):
            count = round_up(len(direct), unit) - len(direct)
            for array, value in zip((direct, tall, rows, cols, frame), (-1, -1, 1000, 1000, 0)):
                array.extend([value] * count)

        add(row_own, col_own, 0)
        bases = []
        self.row_places, self.col_places = [], []
        for row in rows_of:
            bases.append(len(direct))
            add(row, col_own, bases[-1])
            pad(16)
            self.row_places.append((bases[-1], len(direct) - bases[-1]))
        self.tall = len(direct)
        for col in cols_of:
            start = len(direct)
            for row, base in zip([row_own] + rows_of, [0] + bases):
                add(row, col, base)
                pad(16)
            self.col_places.append((start, len(direct) - start))
        self.used = len(direct)
        pad(LANES)
        self.wide = len(direct)
        self.frame = np.array(frame, np.int32)
        rows, cols = np.array(rows), np.array(cols)
        mine = slice(0, self.tokens)
        gap = np.maximum(
            np.abs(rows[mine][:, None] - rows[None, :]), np.abs(cols[mine][:, None] - cols[None, :])
        )
        return np.array(direct), np.array(tall), np.minimum(gap, FAR)

    def which(self):
        at_h = lax.axis_index("ha") if self.variants_h == 2 else 0
        at_w = lax.axis_index("wa") if self.variants_w == 2 else 0
        return at_h * self.variants_w + at_w

    def near(self, gap_ref):
        lane = lax.broadcasted_iota(jnp.int32, (1, self.wide), 1)
        far = jnp.zeros((1, self.wide), jnp.float32)
        for start, end, row, col in self.ranges[1:]:
            inside = row.place(lax.axis_index("ha"))[1] & col.place(lax.axis_index("wa"))[1]
            cost = jnp.where(inside, 0.0, FAR)
            far = jnp.where((lane >= start) & (lane < end), cost, far)
        return gap_ref[self.which()] + far

    def permute(self, row, col, x):
        pairs = [
            (a * self.count_w + c, b * self.count_w + d)
            for a, b in row.pairs
            for c, d in col.pairs
        ]
        return lax.ppermute(x, ("ha", "wa"), pairs)

    def exchange_rows(self, messages):
        own = self.ranges[0][3]
        return [self.permute(row, own, x) for row, x in zip(self.row_sides, messages)]

    def exchange_cols(self, messages):
        own = self.ranges[0][2]
        return [self.permute(own, col, x) for col, x in zip(self.col_sides, messages)]

    def exchange_all(self, messages):
        return [self.permute(row, col, x) for x, (_, _, row, col) in zip(messages, self.ranges[1:])]


def whole(memory=pltpu.VMEM):
    return pl.BlockSpec(memory_space=memory)


def call(kernel, name, in_specs, out_specs, out_shape, scratch, mib, cost, aliases=None):
    return pl.pallas_call(
        kernel,
        in_specs=in_specs,
        out_specs=out_specs,
        out_shape=out_shape,
        scratch_shapes=scratch,
        compiler_params=pltpu.CompilerParams(vmem_limit_bytes=mib * 1024 * 1024),
        cost_estimate=pl.CostEstimate(
            flops=int(cost * 3e8), bytes_accessed=int(cost * 6e5), transcendentals=0
        ),
        input_output_aliases=aliases or {},
        name=name,
    )


def pick(table, place):
    value = jnp.int32(table[0])
    for index, entry in enumerate(table[1:], 1):
        if entry != table[0]:
            value = jnp.where(place == index, entry, value)
    return value


class Move:
    def __init__(self, targets, payload=None, source=None, after=()):
        self.targets, self.payload, self.source, self.after = targets, payload, source, after


def transport(blocks):
    every = range(blocks)
    if blocks == 4:
        near, far, middle = [1, 0, 3, 2], [2, 3, 0, 1], [0, 2, 1, 3]
        payloads = [[0, 2, 0, 2], [0, 0, 2, 2], [2, 0, 2, 0]]
        moves = [
            Move(near, payload=0),
            Move(far, payload=1),
            Move(near, source=1),
            Move(middle, payload=2, after=(1,)),
        ]
        return payloads, moves, [
            ([0], [0] * 4, near),
            ([1], [0] * 4, far),
            ([2, 3], [0, 1, 1, 0], [3, 2, 1, 0]),
        ]
    payloads, moves, batches = [], [], []
    for r in range(1, blocks):
        targets = [(s + r) % blocks for s in every]
        payloads.append([0 if targets[s] > s else 2 for s in every])
        moves.append(Move(targets, payload=r - 1))
        batches.append(([r - 1], [0] * blocks, [(s - r) % blocks for s in every]))
    return payloads, moves, batches


def tidy(geo, arrays, payloads):
    width = arrays[0].shape[-1]
    tokens, tile_h = geo.tokens, geo.tile_h

    sides = len(geo.row_places)

    def kernel(*refs):
        ins, refs = refs[:5], refs[5:]
        own_ref, outs, rows = refs[0], refs[1 : 1 + len(payloads)], refs[1 + len(payloads) :]
        rows, (stage, select, sems) = rows[: 2 * sides], rows[2 * sides :]
        copies = [
            pltpu.make_async_copy(ref, target, sems.at[number])
            for number, (ref, target) in enumerate(zip(ins, [stage.at[n] for n in range(4)]))
        ]
        copies.append(pltpu.make_async_copy(ins[4].at[geo.which()], select, sems.at[4]))
        for copy in copies:
            copy.start()
        for number, copy in enumerate(copies[:4]):
            copy.wait()
            for group in range(geo.groups):
                own_ref[number, group * tile_h : (group + 1) * tile_h, :] = stage[number, group]
        copies[4].wait()
        chosen = select[...].astype(jnp.bfloat16)
        for a in range(4):
            picked = dot_nn(chosen, own_ref[a]).astype(jnp.bfloat16)
            for out, (start, size) in zip(rows[a // 2 * sides :], geo.row_places):
                out[a % 2] = picked[start - tokens : start - tokens + size]
        place = lax.axis_index("span")
        for out, table in zip(outs, payloads):
            out[...] = own_ref[pl.ds(pick(table, place), 2)]

    pair = jax.ShapeDtypeStruct((2, tokens, width), jnp.bfloat16)
    pieces = [
        jax.ShapeDtypeStruct((2, size, width), jnp.bfloat16) for _, size in geo.row_places * 2
    ]
    out = call(
        kernel,
        "tidy",
        [whole(pltpu.HBM)] * 5,
        [whole()] * (1 + len(payloads) + 2 * sides),
        [jax.ShapeDtypeStruct((4, tokens, width), jnp.bfloat16)]
        + [pair] * len(payloads)
        + pieces,
        [
            pltpu.VMEM((4, geo.groups, tile_h, width), jnp.bfloat16),
            pltpu.VMEM(geo.row_select.shape[1:], jnp.float32),
            pltpu.SemaphoreType.DMA((5,)),
        ],
        60,
        2,
    )(*arrays, geo.row_select.astype(np.float32))
    count = 1 + len(payloads)
    return out[0], out[1:count], out[count : count + sides], out[count + sides :]


def pack_rows(geo, groups, after, every=False):
    places = geo.places if every else geo.row_places
    select = geo.all_select if every else geo.row_select
    ins = [x for candidates, _, _ in groups for x in candidates]
    _, tokens, width = ins[0].shape
    several = [len(candidates) > 1 for candidates, _, _ in groups]

    def kernel(select_ref, *refs):
        refs, outs = refs[: len(ins)], list(refs[len(ins) + len(after) :])
        chosen = select_ref[geo.which()]
        kept = [outs.pop(0) if many else None for many in several]
        place = lax.axis_index("span")

        def work(x_ref, first, pair):
            for a in range(2):
                x = x_ref[first + a]
                if kept[pair] is not None:
                    kept[pair][a] = x
                picked = dot_nn(chosen, x).astype(jnp.bfloat16)
                for out, (start, size) in zip(outs[pair * len(places) :], places):
                    out[a] = picked[start - tokens : start - tokens + size]

        at = 0
        for pair, (candidates, which, first) in enumerate(groups):
            for index in range(len(candidates)):
                job = functools.partial(work, refs[at + index], first, pair)
                if several[pair]:
                    pl.when(pick(which, place) == index)(job)
                else:
                    job()
            at += len(candidates)

    shapes = [jax.ShapeDtypeStruct((2, tokens, width), jnp.bfloat16)] * sum(several)
    shapes += [
        jax.ShapeDtypeStruct((2, size, width), jnp.bfloat16) for _, size in places * len(groups)
    ]
    out = list(
        call(
            kernel,
            "pack_rows",
            [whole()] * (1 + len(ins)) + [whole(pl.ANY)] * len(after),
            [whole()] * len(shapes),
            shapes,
            [],
            12,
            0.2,
        )(select, *ins, *after)
    )
    xs = [out.pop(0) if many else group[0][0] for many, group in zip(several, groups)]
    return xs, [out[n * len(places) : (n + 1) * len(places)] for n in range(len(groups))]


def pack_cols(geo, xs, firsts, rows, after):
    count, sides = 2 * len(xs), len(rows[0])
    rows = [piece for pair in rows for piece in pair]
    _, tokens, width = xs[0].shape

    def kernel(select_ref, *refs):
        x_refs, refs = refs[: len(xs)], refs[len(xs) :]
        row_refs, refs = refs[: len(rows)], refs[len(rows) + len(after) :]
        outs, tall = refs[:-1], refs[-1]
        chosen = select_ref[geo.which()]
        for a in range(count):
            tall[a, :tokens] = x_refs[a // 2][firsts[a // 2] + a % 2]
            for ref, (start, size) in zip(row_refs[a // 2 * sides :], geo.row_places):
                tall[a, start : start + size] = ref[a % 2]
            picked = dot_nn(chosen, tall[a]).astype(jnp.bfloat16)
            for out, (start, size) in zip(outs, geo.col_places):
                out[a] = picked[start - geo.tall : start - geo.tall + size]

    return call(
        kernel,
        "pack_cols",
        [whole()] * (1 + len(xs) + len(rows)) + [whole(pl.ANY)] * len(after),
        [whole()] * len(geo.col_places),
        [jax.ShapeDtypeStruct((count, size, width), jnp.bfloat16) for _, size in geo.col_places],
        [pltpu.VMEM((count, geo.tall, width), jnp.bfloat16)],
        12,
        0.2,
    )(geo.col_select, *xs, *rows, *after)


def set_bias(bias_ref, gap):
    for reach in range(1, RMAX + 1):
        bias_ref[reach - 1] = jnp.where(gap <= reach, 0.0, -jnp.inf)


def fit(x, lanes):
    return x if x.shape[1] == lanes else jnp.broadcast_to(x[:, :1], (x.shape[0], lanes))


def repeat(x, lanes):
    return jnp.concatenate([x] * (lanes // LANES), axis=1)


def spread(geo, parts, bases, wide):
    places = geo.row_places + geo.col_places
    if len(parts) > 1 + len(places):
        places = geo.places
    for a in range(2):
        for ref, base, (start, size) in zip(parts, bases, [(0, geo.tokens)] + places):
            wide[a, start : start + size] = ref[base + a]
        if geo.wide > geo.used:
            wide[a, geo.used :] = jnp.zeros((geo.wide - geo.used, wide.shape[-1]), jnp.bfloat16)


def lay_out(geo, heads, small, own, parts, bases):
    tokens, wide_rows = geo.tokens, geo.wide
    width = own.shape[-1]
    depth = width // heads
    scale = LOG2E / math.sqrt(depth)

    def kernel(radius_ref, live_ref, gap_ref, row_frame_ref, own_ref, *refs):
        parts_refs, (wide, products, bias_ref) = refs[: len(parts)], refs[len(parts) :]
        spread(geo, parts_refs, bases, wide)
        live = row_frame_ref[...] < live_ref[lax.axis_index("span")]
        set_bias(bias_ref, jnp.where(live, geo.near(gap_ref), FAR))
        for h in range(heads):
            lanes = slice(h * depth, (h + 1) * depth)
            score = dot_nt(own_ref[0, :, lanes], wide[0, :, lanes])
            products[0, h] = score * scale + bias_ref[radius_ref[h] - 1]
            products[1, h] = dot_nt(own_ref[1, :, lanes], wide[1, :, lanes])

    return call(
        kernel,
        "lay_out",
        [whole(pltpu.SMEM)] * 2 + [whole()] * (3 + len(parts)),
        [whole()] * 2,
        [
            jax.ShapeDtypeStruct((2, wide_rows, width), jnp.bfloat16),
            jax.ShapeDtypeStruct((2, heads, tokens, wide_rows), jnp.float32),
        ],
        [pltpu.VMEM((RMAX, tokens, wide_rows), jnp.float32)],
        16,
        0.5,
    )(*small, geo.gap, geo.frame[:tokens, None], own, *parts)


def forward(geo, heads, small, own, sources, parts, bases, state, last, after):
    tokens, wide_rows = geo.tokens, geo.wide
    width = own.shape[-1]
    depth = width // heads
    scale = LOG2E / math.sqrt(depth)
    per = len(parts)
    stat_rows = round_up(2 * heads, 8)
    first = state is None
    lanes = [slice(h * depth, (h + 1) * depth) for h in range(heads)]

    def kernel(
        radius_ref, live_ref, gap_ref, frame_ref, row_frame_ref, select_ref, own_ref, *refs
    ):
        parts_refs, refs = refs[:per], refs[per:]
        state_in, refs = (None, refs) if first else (refs[:3], refs[3:])
        wide, products, *refs = refs[len(after) :]
        if last:
            outs, (accum, top, total, bias_ref) = refs[:4], refs[4:]
        else:
            accum, top, total, bias_ref = refs
        place = lax.axis_index("span")
        source = place if first else pick(sources, place)
        active = source <= place

        spread(geo, parts_refs, bases, wide)
        if first:
            accum[...] = jnp.zeros(accum.shape, jnp.float32)
            top[...] = jnp.full(top.shape, -jnp.inf, jnp.float32)
            total[...] = jnp.zeros(total.shape, jnp.float32)
        else:
            for old, new in zip(state_in, (accum, top, total)):
                new[...] = old[...]

        def multiply(h, base):
            score = dot_nt(own_ref[base, :, lanes[h]], wide[0, :, lanes[h]])
            score = score * scale + bias_ref[radius_ref[h] - 1]
            products[0, h] = score
            products[1, h] = dot_nt(own_ref[base + 1, :, lanes[h]], wide[1, :, lanes[h]])
            return score

        def attend():
            live = frame_ref[...] < live_ref[source]
            set_bias(bias_ref, jnp.where(live, geo.near(gap_ref), FAR))
            ones = jnp.ones((wide_rows, LANES), jnp.bfloat16)
            ahead = multiply(0, 2)
            for h in range(heads):
                score = ahead
                if h + 1 < heads:
                    ahead = multiply(h + 1, 2)
                best = jnp.max(score, axis=1, keepdims=True)
                new_top = jnp.maximum(top[h], best)
                fading = jnp.exp2(top[h] - new_top)
                top[h] = new_top
                weight = jnp.exp2(score - repeat(new_top, wide_rows)).astype(jnp.bfloat16)
                value = jnp.concatenate([wide[1, :, lanes[h]], ones], axis=1)
                both = dot_nn(weight, value)
                accum[:, lanes[h]] = accum[:, lanes[h]] * fit(fading, depth) + both[:, :depth]
                total[h] = total[h] * fading + both[:, depth:]

        def keep():
            live = row_frame_ref[...] < live_ref[place]
            set_bias(bias_ref, jnp.where(live, geo.near(gap_ref), FAR))
            for h in range(heads):
                multiply(h, 0)

        def finish():
            attended_ref, lse_ref, delta_ref, packed_ref = outs
            lane = lax.broadcasted_iota(jnp.int32, (tokens, LANES), 1)
            column = jnp.zeros((tokens, LANES), jnp.float32)
            for h in range(heads):
                rounded = (accum[:, lanes[h]] / fit(total[h], depth)).astype(jnp.bfloat16)
                rounded = rounded.astype(jnp.float32)
                accum[:, lanes[h]] = rounded
                lse = top[h] + jnp.log2(total[h])
                grad = own_ref[3, :, lanes[h]].astype(jnp.float32)
                delta = jnp.sum(rounded * grad, axis=1, keepdims=True)
                delta = jnp.broadcast_to(delta, (tokens, LANES))
                lse_ref[h] = lse
                delta_ref[h] = delta
                column = jnp.where(lane == h, lse, column)
                column = jnp.where(lane == heads + h, delta, column)
            packed = jnp.zeros((wide_rows, LANES), jnp.float32)
            rest = column
            chosen = select_ref[geo.which()]
            for _ in range(3):
                part = rest.astype(jnp.bfloat16)
                rest = rest - part.astype(jnp.float32)
                packed = packed + dot_nn(chosen, part)
            packed_ref[...] = jnp.transpose(packed)[:stat_rows]
            for group in range(geo.groups):
                at = slice(group * geo.tile_h, (group + 1) * geo.tile_h)
                attended_ref[group] = accum[at, :].astype(jnp.bfloat16)

        if first:
            attend()
        else:
            pl.when(active)(attend)
            pl.when(jnp.logical_not(active))(keep)
        if last:
            finish()

    ins = [*small, geo.gap, geo.frame[None, :], geo.frame[:tokens, None], geo.select, own, *parts]
    ins += [] if first else list(state)
    stat = (heads, tokens, LANES)
    running = [(tokens, width), stat, stat]
    shapes = [
        jax.ShapeDtypeStruct((2, wide_rows, width), jnp.bfloat16),
        jax.ShapeDtypeStruct((2, heads, tokens, wide_rows), jnp.float32),
    ]
    scratch = []
    if last:
        shapes += [
            jax.ShapeDtypeStruct((geo.groups, geo.tile_h, width), jnp.bfloat16),
            jax.ShapeDtypeStruct(stat, jnp.float32),
            jax.ShapeDtypeStruct(stat, jnp.float32),
            jax.ShapeDtypeStruct((stat_rows, wide_rows), jnp.float32),
        ]
        scratch += [pltpu.VMEM(shape, jnp.float32) for shape in running]
    else:
        shapes += [jax.ShapeDtypeStruct(shape, jnp.float32) for shape in running]
    return call(
        kernel,
        "forward",
        [whole(pltpu.SMEM)] * 2 + [whole()] * (len(ins) - 2) + [whole(pl.ANY)] * len(after),
        [whole()] * len(shapes),
        shapes,
        scratch + [pltpu.VMEM((RMAX, tokens, wide_rows), jnp.float32)],
        20,
        1.5,
    )(*ins, *after)


def merge(geo, pieces, after):
    def kernel(*refs):
        out = refs[-1]
        row = refs[0][...]
        lane = lax.broadcasted_iota(jnp.int32, row.shape, 1)
        for ref, (start, *_) in zip(refs[1:], geo.ranges[1:]):
            row = jnp.where(lane >= start, ref[...], row)
        out[...] = row

    return call(
        kernel,
        "merge",
        [whole()] * len(pieces) + [whole(pl.ANY)] * len(after),
        whole(),
        jax.ShapeDtypeStruct(pieces[0].shape, jnp.float32),
        [],
        4,
        0.1,
    )(*pieces, *after)


def query_grads(geo, heads, lse, delta, sources, slots):
    tokens, wide_rows = geo.tokens, geo.wide
    width = slots[0][0].shape[-1]
    depth = width // heads
    natural = 1.0 / math.sqrt(depth)
    lanes = [slice(h * depth, (h + 1) * depth) for h in range(heads)]

    def kernel(lse_ref, delta_ref, *refs):
        slot_refs, (out, token, accum) = refs[: 2 * len(slots)], refs[2 * len(slots) :]
        token[...] = jnp.zeros(token.shape, jnp.float32)
        place = lax.axis_index("span")

        def step(wide, products, first):
            for h in range(heads):
                prob = jnp.exp2(products[0, h] - repeat(lse_ref[h], wide_rows))
                slope = prob * (products[1, h] - repeat(delta_ref[h], wide_rows))
                part = dot_nn(slope.astype(jnp.bfloat16), wide[0, :, lanes[h]])
                accum[:, lanes[h]] = part if first else accum[:, lanes[h]] + part

        for n, table in enumerate(sources):
            work = functools.partial(step, slot_refs[2 * n], slot_refs[2 * n + 1], n == 0)
            if n == 0:
                work()
            else:
                pl.when(pick(table, place) < place)(work)
        for group in range(geo.groups):
            at = slice(group * geo.tile_h, (group + 1) * geo.tile_h)
            out[group] = (accum[at, :] * natural).astype(jnp.bfloat16)

    flat = [x for slot in slots for x in slot]
    return call(
        kernel,
        "query_grads",
        [whole()] * (2 + len(flat)),
        [whole()] * 2,
        [
            jax.ShapeDtypeStruct((geo.groups, geo.tile_h, width), jnp.bfloat16),
            jax.ShapeDtypeStruct((8, LANES), jnp.float32),
        ],
        [pltpu.VMEM((tokens, width), jnp.float32)],
        8,
        2,
    )(lse, delta, *flat)


def key_grads(geo, blocks, heads, stats, sources, slots, state, last):
    tokens, wide_rows = geo.tokens, geo.wide
    width = slots[0][0].shape[-1]
    depth = width // heads
    natural = 1.0 / math.sqrt(depth)
    stat_rows = stats[0].shape[0]
    lanes = [slice(h * depth, (h + 1) * depth) for h in range(heads)]

    def kernel(*refs):
        slot_refs, refs = refs[: 2 * len(slots)], refs[2 * len(slots) :]
        stat_refs, refs = refs[: len(stats)], refs[len(stats) :]
        state_in, refs = (None, refs) if state is None else (refs[0], refs[1:])
        outs, refs = (refs[:2], refs[2:]) if last else (None, refs)
        accum, rows = refs
        place = lax.axis_index("span")
        accum[...] = jnp.zeros(accum.shape, jnp.float32) if state is None else state_in[...]
        for n, ref in enumerate(stat_refs):
            rows[n] = ref[...]

        def step(wide, products, rotation):
            for h in range(heads):
                prob = jnp.exp2(products[0, h] - rows[rotation, h : h + 1, :])
                accum[1, :, lanes[h]] += dot_nn(prob.astype(jnp.bfloat16), wide[1, :, lanes[h]])
                slope = prob * (products[1, h] - rows[rotation, heads + h : heads + h + 1, :])
                accum[0, :, lanes[h]] += dot_nn(slope.astype(jnp.bfloat16), wide[0, :, lanes[h]])

        for n, table in enumerate(sources):
            wide, products = slot_refs[2 * n : 2 * n + 2]
            if table == list(range(blocks)):
                step(wide, products, 0)
            else:
                source = pick(table, place)
                rotation = lax.rem(place - source + blocks, blocks) - 1
                pl.when(source > place)(functools.partial(step, wide, products, rotation))
        if last:
            for group in range(geo.groups):
                at = slice(group * geo.tile_h, (group + 1) * geo.tile_h)
                outs[0][group] = (accum[0, at, :] * natural).astype(jnp.bfloat16)
                outs[1][group] = accum[1, at, :].astype(jnp.bfloat16)

    ins = [x for slot in slots for x in slot] + list(stats)
    ins += [] if state is None else [state]
    running = (2, tokens, width)
    shapes = [jax.ShapeDtypeStruct(running, jnp.float32)]
    if last:
        shapes = [jax.ShapeDtypeStruct((geo.groups, geo.tile_h, width), jnp.bfloat16)] * 2
    return call(
        kernel,
        "key_grads",
        [whole()] * len(ins),
        [whole()] * len(shapes),
        shapes,
        ([pltpu.VMEM(running, jnp.float32)] if last else [])
        + [pltpu.VMEM((len(stats), stat_rows, wide_rows), jnp.float32)],
        8,
        2,
    )(*ins)


def rotate(x, by, blocks):
    return lax.ppermute(x, "span", [(i, (i + by) % blocks) for i in range(blocks)])


def shards(queries, cache_keys, cache_values, grad_attended, radius, frame_count, sizes):
    blocks, count_h, count_w = sizes
    frames, tile_h, tile_w, width = queries.shape[1:]
    heads = radius.shape[0]
    geo = Geometry(frames, tile_h, tile_w, count_h, count_w)
    small = (radius, frame_count)

    def grouped(x):
        return jnp.transpose(x[0], (0, 2, 1, 3)).reshape(geo.groups, tile_h, width)

    def restored(x):
        x = x.reshape(frames, tile_w, tile_h, width)
        return jnp.transpose(x, (0, 2, 1, 3))[None]

    arrays = [grouped(x) for x in (cache_keys, cache_values, queries, grad_attended)]
    payloads, moves, batches = transport(blocks)
    own, sends, messages, asked = tidy(geo, arrays, payloads)
    sources = [list(range(blocks))] + [table for _, _, table in batches]
    moved = []

    def send(move, after):
        x = sends[move.payload] if move.source is None else moved[move.source]
        after = after + [moved[n] for n in move.after]
        x = lax.optimization_barrier((x, *after))[0] if after else x
        moved.append(lax.ppermute(x, "span", list(enumerate(move.targets))))

    early = [move for move in moves if move.source is None and not move.after]
    for move in moves[: len(early)]:
        send(move, [])
    rows = geo.exchange_rows(messages)
    messages = pack_cols(geo, [own], [0], [rows], [])
    parts = [own] + rows + geo.exchange_cols(messages)
    asked = geo.exchange_rows(lax.optimization_barrier((*asked, messages[0]))[:-1])
    wide, products, *state = forward(
        geo, heads, small, own, sources[0], parts, [0] * len(parts), None, blocks == 1, []
    )
    slots = [[wide, products]]
    for move in moves[len(early) :]:
        send(move, [state[0]])

    def take(first, end, after, every):
        groups = [([moved[n] for n in ways], which, 0) for ways, which, _ in batches[first:end]]
        return pack_rows(geo, groups, after, every)

    messages = pack_cols(geo, [own], [2], [asked], [state[0]])
    parts = [own] + asked + geo.exchange_cols(messages)
    asked = lay_out(geo, heads, small, own, parts, [2] + [0] * len(parts[1:]))
    middle = [(n, min(n + 2, blocks - 2)) for n in range(0, blocks - 2, 2)]
    todo, after, pieces = [], [messages[0]], []
    for first, end in middle:
        xs, messages = take(first, end, after, False)
        rows = [geo.exchange_rows(group) for group in messages]
        messages = pack_cols(geo, xs, [0] * len(xs), rows, [])
        pieces = geo.exchange_cols(messages)
        after = list(messages[:1])
        for pair, (x, row) in enumerate(zip(xs, rows)):
            todo.append(([x] + row + pieces, [0] * (1 + len(row)) + [2 * pair] * len(pieces)))
    xs, (messages,) = take(blocks - 2, blocks - 1, after, True)
    after = list(messages[:1])
    after.append(asked[0])
    if middle:
        rest = lax.optimization_barrier((*messages[1:], pieces[-1]))[:-1]
        messages = [messages[0], *rest]
    parts = xs + geo.exchange_all(messages)
    todo.append((parts, [0] * len(parts)))
    for n, (parts, bases) in enumerate(todo, 1):
        wide, products, *state = forward(
            geo, heads, small, own, sources[n], parts, bases, state, n == len(todo), after
        )
        slots.append([wide, products])
        after = []
    attended, lse, delta, packed = state

    grad_q, token = query_grads(geo, heads, lse, delta, sources, slots)
    brought = geo.exchange_all([packed] * len(geo.places))
    own_stats = merge(geo, [packed] + brought, [token])
    stats = [rotate(own_stats, n, blocks) for n in range(1, blocks)]
    begun = key_grads(geo, blocks, heads, [own_stats], sources[:1], [asked], None, False)[0]
    grad_k, grad_v = key_grads(
        geo, blocks, heads, stats, sources[1:], slots[1:], begun, True
    )
    return tuple(restored(x) for x in (attended, grad_q, grad_k, grad_v))


def solution(mesh):
    placed = P("span", None, "ha", "wa", None)
    sizes = tuple(mesh.shape[name] for name in ("span", "ha", "wa"))
    return jax.shard_map(
        functools.partial(shards, sizes=sizes),
        mesh=mesh,
        in_specs=(placed,) * 4 + (P(), P()),
        out_specs=(placed,) * 4,
        check_vma=False,
    )
```

```python
import functools
import math

import jax
import jax.numpy as jnp
import ml_dtypes
import numpy as np
from jax import lax
from jax.experimental import pallas as pl
from jax.experimental.pallas import tpu as pltpu
from jax.sharding import PartitionSpec as P

RMAX = 2
FAR = 99.0
LOG2E = math.log2(math.e)
LANES = 128


def round_up(value, unit):
    return (value + unit - 1) // unit * unit


def dot_nt(a, b):
    return lax.dot_general(a, b, (((1,), (1,)), ((), ())), preferred_element_type=jnp.float32)


def dot_nn(a, b):
    return lax.dot_general(a, b, (((1,), (0,)), ((), ())), preferred_element_type=jnp.float32)


class Side:
    def __init__(self, kind, count, tile, variant):
        self.count = count
        self.swap = kind == "swap"
        if kind == "same":
            self.delta, self.start, self.length, self.send_start = 0, 0, tile, 0
        else:
            self.delta = 1 - 2 * variant if self.swap else kind
            send_up = (variant == 0) if self.swap else (kind < 0)
            self.length = RMAX
            self.start = tile if self.delta > 0 else -RMAX
            self.send_start = tile - RMAX if send_up else 0
        shift = 1 if self.swap else self.delta
        self.pairs = [((i + shift) % count, i) for i in range(count)]

    def place(self, index):
        delta = 1 - 2 * index if self.swap else self.delta
        other = index + delta
        inside = (other >= 0) & (other < self.count)
        return jnp.where(inside, other, index), inside


def sides(count, tile, variant):
    kinds = [] if count == 1 else ["swap"] if count == 2 else [-1, 1]
    return [Side(kind, count, tile, variant) for kind in ["same"] + kinds]


class Geometry:
    def __init__(self, frames, tile_h, tile_w, count_h, count_w):
        self.frames, self.tile_h, self.tile_w = frames, tile_h, tile_w
        self.count_h, self.count_w = count_h, count_w
        self.tokens = frames * tile_h * tile_w
        self.groups = frames * tile_w
        self.variants_h = 2 if count_h == 2 else 1
        self.variants_w = 2 if count_w == 2 else 1
        found = [
            self.variant(variant_h, variant_w)
            for variant_h in range(self.variants_h)
            for variant_w in range(self.variants_w)
        ]
        direct, tall, gap = (np.stack(arrays) for arrays in zip(*found))
        own = np.arange(self.tokens)
        starts = [start for start, *_ in self.ranges] + [self.used]
        self.places = [(a, b - a) for a, b in zip(starts, starts[1:])][1:]
        self.all_select = self.one_hot(direct[:, self.tokens : self.used], self.tokens)
        self.row_select = self.one_hot(direct[:, self.tokens : self.tall], self.tokens)
        self.col_select = self.one_hot(tall[:, self.tall : self.used], self.tall)
        self.select = self.one_hot(direct, self.tokens)
        self.gap = gap.astype(np.float32)
        assert (direct[:, : self.tokens] == own).all()

    def one_hot(self, index, count):
        return (index[..., None] == np.arange(count)).astype(ml_dtypes.bfloat16)

    def variant(self, variant_h, variant_w):
        row_own, *rows_of = sides(self.count_h, self.tile_h, variant_h)
        col_own, *cols_of = sides(self.count_w, self.tile_w, variant_w)
        self.row_sides, self.col_sides = rows_of, cols_of
        direct, tall, rows, cols, frame = [], [], [], [], []
        self.ranges = []

        def add(row, col, base):
            ff, xx, yy = np.unravel_index(
                np.arange(self.frames * col.length * row.length),
                (self.frames, col.length, row.length),
            )
            start = len(direct)
            own_x, own_y = col.send_start + xx, row.send_start + yy
            direct.extend((ff * self.tile_w + own_x) * self.tile_h + own_y)
            tall.extend(base + (ff * self.tile_w + own_x) * row.length + yy)
            rows.extend(row.start + yy)
            cols.extend(col.start + xx)
            frame.extend(ff)
            self.ranges.append((start, len(direct), row, col))

        def pad(unit):
            count = round_up(len(direct), unit) - len(direct)
            for array, value in zip((direct, tall, rows, cols, frame), (-1, -1, 1000, 1000, 0)):
                array.extend([value] * count)

        add(row_own, col_own, 0)
        bases = []
        self.row_places, self.col_places = [], []
        for row in rows_of:
            bases.append(len(direct))
            add(row, col_own, bases[-1])
            pad(16)
            self.row_places.append((bases[-1], len(direct) - bases[-1]))
        self.tall = len(direct)
        for col in cols_of:
            start = len(direct)
            for row, base in zip([row_own] + rows_of, [0] + bases):
                add(row, col, base)
                pad(16)
            self.col_places.append((start, len(direct) - start))
        self.used = len(direct)
        pad(LANES)
        self.wide = len(direct)
        self.frame = np.array(frame, np.int32)
        rows, cols = np.array(rows), np.array(cols)
        mine = slice(0, self.tokens)
        gap = np.maximum(
            np.abs(rows[mine][:, None] - rows[None, :]), np.abs(cols[mine][:, None] - cols[None, :])
        )
        return np.array(direct), np.array(tall), np.minimum(gap, FAR)

    def which(self):
        at_h = lax.axis_index("ha") if self.variants_h == 2 else 0
        at_w = lax.axis_index("wa") if self.variants_w == 2 else 0
        return at_h * self.variants_w + at_w

    def near(self, gap_ref):
        lane = lax.broadcasted_iota(jnp.int32, (1, self.wide), 1)
        far = jnp.zeros((1, self.wide), jnp.float32)
        for start, end, row, col in self.ranges[1:]:
            inside = row.place(lax.axis_index("ha"))[1] & col.place(lax.axis_index("wa"))[1]
            cost = jnp.where(inside, 0.0, FAR)
            far = jnp.where((lane >= start) & (lane < end), cost, far)
        return gap_ref[self.which()] + far

    def permute(self, row, col, x):
        pairs = [
            (a * self.count_w + c, b * self.count_w + d)
            for a, b in row.pairs
            for c, d in col.pairs
        ]
        return lax.ppermute(x, ("ha", "wa"), pairs)

    def exchange_rows(self, messages):
        own = self.ranges[0][3]
        return [self.permute(row, own, x) for row, x in zip(self.row_sides, messages)]

    def exchange_cols(self, messages):
        own = self.ranges[0][2]
        return [self.permute(own, col, x) for col, x in zip(self.col_sides, messages)]

    def exchange_all(self, messages):
        return [self.permute(row, col, x) for x, (_, _, row, col) in zip(messages, self.ranges[1:])]


def whole(memory=pltpu.VMEM):
    return pl.BlockSpec(memory_space=memory)


def call(kernel, name, in_specs, out_specs, out_shape, scratch, mib, cost, aliases=None):
    return pl.pallas_call(
        kernel,
        in_specs=in_specs,
        out_specs=out_specs,
        out_shape=out_shape,
        scratch_shapes=scratch,
        compiler_params=pltpu.CompilerParams(vmem_limit_bytes=mib * 1024 * 1024),
        cost_estimate=pl.CostEstimate(
            flops=int(cost * 1e9), bytes_accessed=int(cost * 2e6), transcendentals=0
        ),
        input_output_aliases=aliases or {},
        name=name,
    )


def pick(table, place):
    value = jnp.int32(table[0])
    for index, entry in enumerate(table[1:], 1):
        if entry != table[0]:
            value = jnp.where(place == index, entry, value)
    return value


def relay(blocks):
    held = [[(s, (s % 2 == 0) != bool(chain)) for s in range(blocks)] for chain in range(2)]
    fresh = [[] for _ in range(blocks)]
    for number in range(1, blocks):
        for chain in range(2):
            moved = [held[chain][a] for a in swap(blocks, chain, number)]
            held[chain] = moved
            for s, (block, keys) in enumerate(moved):
                if block != s and keys == (block < s) and block not in [b for _, b in fresh[s]]:
                    fresh[s].append(((chain, number), block))
    batches = []
    for n in range(blocks - 1):
        steps = sorted({fresh[s][n][0] for s in range(blocks)}, key=lambda step: step[::-1])
        which = [steps.index(fresh[s][n][0]) for s in range(blocks)]
        batches.append((steps, which, [fresh[s][n][1] for s in range(blocks)]))
    return batches


def swap(blocks, chain, number):
    start = (chain + number + 1) % 2
    partner = list(range(blocks))
    for low in range(start, blocks - 1, 2):
        partner[low], partner[low + 1] = low + 1, low
    return partner


def tidy(geo, arrays, blocks):
    width = arrays[0].shape[-1]
    tokens, tile_h = geo.tokens, geo.tile_h

    def kernel(*refs):
        ins, (own_ref, even_ref, odd_ref, stage, sems) = refs[:4], refs[4:]
        copies = [
            pltpu.make_async_copy(ref, stage.at[number], sems.at[number])
            for number, ref in enumerate(ins)
        ]
        for copy in copies:
            copy.start()
        for number, copy in enumerate(copies):
            copy.wait()
            for group in range(geo.groups):
                own_ref[number, group * tile_h : (group + 1) * tile_h, :] = stage[number, group]
        odd = lax.rem(lax.axis_index("span"), 2)
        even_ref[...] = own_ref[pl.ds(2 * odd, 2)]
        odd_ref[...] = own_ref[pl.ds(2 - 2 * odd, 2)]

    pair = jax.ShapeDtypeStruct((2, tokens, width), jnp.bfloat16)
    return call(
        kernel,
        "tidy",
        [whole(pltpu.HBM)] * 4,
        [whole()] * 3,
        [jax.ShapeDtypeStruct((4, tokens, width), jnp.bfloat16), pair, pair],
        [
            pltpu.VMEM((4, geo.groups, tile_h, width), jnp.bfloat16),
            pltpu.SemaphoreType.DMA((4,)),
        ],
        60,
        2,
    )(*arrays)


def pack_rows(geo, groups, after, every=False):
    places = geo.places if every else geo.row_places
    select = geo.all_select if every else geo.row_select
    ins = [x for candidates, _, _ in groups for x in candidates]
    _, tokens, width = ins[0].shape
    several = [len(candidates) > 1 for candidates, _, _ in groups]

    def kernel(select_ref, *refs):
        refs, outs = refs[: len(ins)], list(refs[len(ins) + len(after) :])
        chosen = select_ref[geo.which()]
        kept = [outs.pop(0) if many else None for many in several]
        place = lax.axis_index("span")

        def work(x_ref, first, pair):
            for a in range(2):
                x = x_ref[first + a]
                if kept[pair] is not None:
                    kept[pair][a] = x
                picked = dot_nn(chosen, x).astype(jnp.bfloat16)
                for out, (start, size) in zip(outs[pair * len(places) :], places):
                    out[a] = picked[start - tokens : start - tokens + size]

        at = 0
        for pair, (candidates, which, first) in enumerate(groups):
            for index in range(len(candidates)):
                job = functools.partial(work, refs[at + index], first, pair)
                if several[pair]:
                    pl.when(pick(which, place) == index)(job)
                else:
                    job()
            at += len(candidates)

    shapes = [jax.ShapeDtypeStruct((2, tokens, width), jnp.bfloat16)] * sum(several)
    shapes += [
        jax.ShapeDtypeStruct((2, size, width), jnp.bfloat16) for _, size in places * len(groups)
    ]
    out = list(
        call(
            kernel,
            "pack_rows",
            [whole()] * (1 + len(ins)) + [whole(pl.ANY)] * len(after),
            [whole()] * len(shapes),
            shapes,
            [],
            12,
            0.2,
        )(select, *ins, *after)
    )
    xs = [out.pop(0) if many else group[0][0] for many, group in zip(several, groups)]
    return xs, [out[n * len(places) : (n + 1) * len(places)] for n in range(len(groups))]


def pack_cols(geo, xs, firsts, rows, after):
    count, sides = 2 * len(xs), len(rows[0])
    rows = [piece for pair in rows for piece in pair]
    _, tokens, width = xs[0].shape

    def kernel(select_ref, *refs):
        x_refs, refs = refs[: len(xs)], refs[len(xs) :]
        row_refs, refs = refs[: len(rows)], refs[len(rows) + len(after) :]
        outs, tall = refs[:-1], refs[-1]
        chosen = select_ref[geo.which()]
        for a in range(count):
            tall[a, :tokens] = x_refs[a // 2][firsts[a // 2] + a % 2]
            for ref, (start, size) in zip(row_refs[a // 2 * sides :], geo.row_places):
                tall[a, start : start + size] = ref[a % 2]
            picked = dot_nn(chosen, tall[a]).astype(jnp.bfloat16)
            for out, (start, size) in zip(outs, geo.col_places):
                out[a] = picked[start - geo.tall : start - geo.tall + size]

    return call(
        kernel,
        "pack_cols",
        [whole()] * (1 + len(xs) + len(rows)) + [whole(pl.ANY)] * len(after),
        [whole()] * len(geo.col_places),
        [jax.ShapeDtypeStruct((count, size, width), jnp.bfloat16) for _, size in geo.col_places],
        [pltpu.VMEM((count, geo.tall, width), jnp.bfloat16)],
        12,
        0.2,
    )(geo.col_select, *xs, *rows, *after)


def set_bias(bias_ref, gap):
    for reach in range(1, RMAX + 1):
        bias_ref[reach - 1] = jnp.where(gap <= reach, 0.0, -jnp.inf)


def fit(x, lanes):
    return x if x.shape[1] == lanes else jnp.broadcast_to(x[:, :1], (x.shape[0], lanes))


def repeat(x, lanes):
    return jnp.concatenate([x] * (lanes // LANES), axis=1)


def spread(geo, parts, bases, wide):
    places = geo.row_places + geo.col_places
    if len(parts) > 1 + len(places):
        places = geo.places
    for a in range(2):
        for ref, base, (start, size) in zip(parts, bases, [(0, geo.tokens)] + places):
            wide[a, start : start + size] = ref[base + a]
        if geo.wide > geo.used:
            wide[a, geo.used :] = jnp.zeros((geo.wide - geo.used, wide.shape[-1]), jnp.bfloat16)


def lay_out(geo, heads, small, own, parts, bases):
    tokens, wide_rows = geo.tokens, geo.wide
    width = own.shape[-1]
    depth = width // heads
    scale = LOG2E / math.sqrt(depth)

    def kernel(radius_ref, live_ref, gap_ref, row_frame_ref, own_ref, *refs):
        parts_refs, (wide, products, bias_ref) = refs[: len(parts)], refs[len(parts) :]
        spread(geo, parts_refs, bases, wide)
        live = row_frame_ref[...] < live_ref[lax.axis_index("span")]
        set_bias(bias_ref, jnp.where(live, geo.near(gap_ref), FAR))
        for h in range(heads):
            lanes = slice(h * depth, (h + 1) * depth)
            score = dot_nt(own_ref[0, :, lanes], wide[0, :, lanes])
            products[0, h] = score * scale + bias_ref[radius_ref[h] - 1]
            products[1, h] = dot_nt(own_ref[1, :, lanes], wide[1, :, lanes])

    return call(
        kernel,
        "lay_out",
        [whole(pltpu.SMEM)] * 2 + [whole()] * (3 + len(parts)),
        [whole()] * 2,
        [
            jax.ShapeDtypeStruct((2, wide_rows, width), jnp.bfloat16),
            jax.ShapeDtypeStruct((2, heads, tokens, wide_rows), jnp.float32),
        ],
        [pltpu.VMEM((RMAX, tokens, wide_rows), jnp.float32)],
        16,
        0.5,
    )(*small, geo.gap, geo.frame[:tokens, None], own, *parts)


def forward(geo, heads, small, own, sources, parts, bases, state, last, after):
    tokens, wide_rows = geo.tokens, geo.wide
    width = own.shape[-1]
    depth = width // heads
    scale = LOG2E / math.sqrt(depth)
    per = len(parts)
    stat_rows = round_up(2 * heads, 8)
    first = state is None
    lanes = [slice(h * depth, (h + 1) * depth) for h in range(heads)]

    def kernel(
        radius_ref, live_ref, gap_ref, frame_ref, row_frame_ref, select_ref, own_ref, *refs
    ):
        parts_refs, refs = refs[:per], refs[per:]
        state_in, refs = (None, refs) if first else (refs[:3], refs[3:])
        wide, products, *refs = refs[len(after) :]
        if last:
            outs, (accum, top, total, bias_ref) = refs[:4], refs[4:]
        else:
            accum, top, total, bias_ref = refs
        place = lax.axis_index("span")
        source = place if first else pick(sources, place)
        active = source <= place

        spread(geo, parts_refs, bases, wide)
        if first:
            accum[...] = jnp.zeros(accum.shape, jnp.float32)
            top[...] = jnp.full(top.shape, -jnp.inf, jnp.float32)
            total[...] = jnp.zeros(total.shape, jnp.float32)
        else:
            for old, new in zip(state_in, (accum, top, total)):
                new[...] = old[...]

        def multiply(h, base):
            score = dot_nt(own_ref[base, :, lanes[h]], wide[0, :, lanes[h]])
            score = score * scale + bias_ref[radius_ref[h] - 1]
            products[0, h] = score
            products[1, h] = dot_nt(own_ref[base + 1, :, lanes[h]], wide[1, :, lanes[h]])
            return score

        def attend():
            live = frame_ref[...] < live_ref[source]
            set_bias(bias_ref, jnp.where(live, geo.near(gap_ref), FAR))
            ones = jnp.ones((wide_rows, LANES), jnp.bfloat16)
            ahead = multiply(0, 2)
            for h in range(heads):
                score = ahead
                if h + 1 < heads:
                    ahead = multiply(h + 1, 2)
                best = jnp.max(score, axis=1, keepdims=True)
                new_top = jnp.maximum(top[h], best)
                fading = jnp.exp2(top[h] - new_top)
                top[h] = new_top
                weight = jnp.exp2(score - repeat(new_top, wide_rows)).astype(jnp.bfloat16)
                value = jnp.concatenate([wide[1, :, lanes[h]], ones], axis=1)
                both = dot_nn(weight, value)
                accum[:, lanes[h]] = accum[:, lanes[h]] * fit(fading, depth) + both[:, :depth]
                total[h] = total[h] * fading + both[:, depth:]

        def keep():
            live = row_frame_ref[...] < live_ref[place]
            set_bias(bias_ref, jnp.where(live, geo.near(gap_ref), FAR))
            for h in range(heads):
                multiply(h, 0)

        def finish():
            attended_ref, lse_ref, delta_ref, packed_ref = outs
            lane = lax.broadcasted_iota(jnp.int32, (tokens, LANES), 1)
            column = jnp.zeros((tokens, LANES), jnp.float32)
            for h in range(heads):
                rounded = (accum[:, lanes[h]] / fit(total[h], depth)).astype(jnp.bfloat16)
                rounded = rounded.astype(jnp.float32)
                accum[:, lanes[h]] = rounded
                lse = top[h] + jnp.log2(total[h])
                grad = own_ref[3, :, lanes[h]].astype(jnp.float32)
                delta = jnp.sum(rounded * grad, axis=1, keepdims=True)
                delta = jnp.broadcast_to(delta, (tokens, LANES))
                lse_ref[h] = lse
                delta_ref[h] = delta
                column = jnp.where(lane == h, lse, column)
                column = jnp.where(lane == heads + h, delta, column)
            packed = jnp.zeros((wide_rows, LANES), jnp.float32)
            rest = column
            chosen = select_ref[geo.which()]
            for _ in range(3):
                part = rest.astype(jnp.bfloat16)
                rest = rest - part.astype(jnp.float32)
                packed = packed + dot_nn(chosen, part)
            packed_ref[...] = jnp.transpose(packed)[:stat_rows]
            for group in range(geo.groups):
                at = slice(group * geo.tile_h, (group + 1) * geo.tile_h)
                attended_ref[group] = accum[at, :].astype(jnp.bfloat16)

        if first:
            attend()
        else:
            pl.when(active)(attend)
            pl.when(jnp.logical_not(active))(keep)
        if last:
            finish()

    ins = [*small, geo.gap, geo.frame[None, :], geo.frame[:tokens, None], geo.select, own, *parts]
    ins += [] if first else list(state)
    stat = (heads, tokens, LANES)
    running = [(tokens, width), stat, stat]
    shapes = [
        jax.ShapeDtypeStruct((2, wide_rows, width), jnp.bfloat16),
        jax.ShapeDtypeStruct((2, heads, tokens, wide_rows), jnp.float32),
    ]
    scratch = []
    if last:
        shapes += [
            jax.ShapeDtypeStruct((geo.groups, geo.tile_h, width), jnp.bfloat16),
            jax.ShapeDtypeStruct(stat, jnp.float32),
            jax.ShapeDtypeStruct(stat, jnp.float32),
            jax.ShapeDtypeStruct((stat_rows, wide_rows), jnp.float32),
        ]
        scratch += [pltpu.VMEM(shape, jnp.float32) for shape in running]
    else:
        shapes += [jax.ShapeDtypeStruct(shape, jnp.float32) for shape in running]
    return call(
        kernel,
        "forward",
        [whole(pltpu.SMEM)] * 2 + [whole()] * (len(ins) - 2) + [whole(pl.ANY)] * len(after),
        [whole()] * len(shapes),
        shapes,
        scratch + [pltpu.VMEM((RMAX, tokens, wide_rows), jnp.float32)],
        20,
        1.5,
    )(*ins, *after)


def merge(geo, pieces, after):
    def kernel(*refs):
        out = refs[-1]
        row = refs[0][...]
        lane = lax.broadcasted_iota(jnp.int32, row.shape, 1)
        for ref, (start, *_) in zip(refs[1:], geo.ranges[1:]):
            row = jnp.where(lane >= start, ref[...], row)
        out[...] = row

    return call(
        kernel,
        "merge",
        [whole()] * len(pieces) + [whole(pl.ANY)] * len(after),
        whole(),
        jax.ShapeDtypeStruct(pieces[0].shape, jnp.float32),
        [],
        4,
        0.1,
    )(*pieces, *after)


def query_grads(geo, heads, lse, delta, sources, slots):
    tokens, wide_rows = geo.tokens, geo.wide
    width = slots[0][0].shape[-1]
    depth = width // heads
    natural = 1.0 / math.sqrt(depth)
    lanes = [slice(h * depth, (h + 1) * depth) for h in range(heads)]

    def kernel(lse_ref, delta_ref, *refs):
        slot_refs, (out, token, accum) = refs[: 2 * len(slots)], refs[2 * len(slots) :]
        token[...] = jnp.zeros(token.shape, jnp.float32)
        place = lax.axis_index("span")

        def step(wide, products, first):
            for h in range(heads):
                prob = jnp.exp2(products[0, h] - repeat(lse_ref[h], wide_rows))
                slope = prob * (products[1, h] - repeat(delta_ref[h], wide_rows))
                part = dot_nn(slope.astype(jnp.bfloat16), wide[0, :, lanes[h]])
                accum[:, lanes[h]] = part if first else accum[:, lanes[h]] + part

        for n, table in enumerate(sources):
            work = functools.partial(step, slot_refs[2 * n], slot_refs[2 * n + 1], n == 0)
            if n == 0:
                work()
            else:
                pl.when(pick(table, place) < place)(work)
        for group in range(geo.groups):
            at = slice(group * geo.tile_h, (group + 1) * geo.tile_h)
            out[group] = (accum[at, :] * natural).astype(jnp.bfloat16)

    flat = [x for slot in slots for x in slot]
    return call(
        kernel,
        "query_grads",
        [whole()] * (2 + len(flat)),
        [whole()] * 2,
        [
            jax.ShapeDtypeStruct((geo.groups, geo.tile_h, width), jnp.bfloat16),
            jax.ShapeDtypeStruct((8, LANES), jnp.float32),
        ],
        [pltpu.VMEM((tokens, width), jnp.float32)],
        8,
        2,
    )(lse, delta, *flat)


def key_grads(geo, blocks, heads, stats, sources, slots, state, last):
    tokens, wide_rows = geo.tokens, geo.wide
    width = slots[0][0].shape[-1]
    depth = width // heads
    natural = 1.0 / math.sqrt(depth)
    stat_rows = stats[0].shape[0]
    lanes = [slice(h * depth, (h + 1) * depth) for h in range(heads)]

    def kernel(*refs):
        slot_refs, refs = refs[: 2 * len(slots)], refs[2 * len(slots) :]
        stat_refs, refs = refs[: len(stats)], refs[len(stats) :]
        state_in, refs = (None, refs) if state is None else (refs[0], refs[1:])
        outs, refs = (refs[:2], refs[2:]) if last else (None, refs)
        accum, rows = refs
        place = lax.axis_index("span")
        accum[...] = jnp.zeros(accum.shape, jnp.float32) if state is None else state_in[...]
        for n, ref in enumerate(stat_refs):
            rows[n] = ref[...]

        def step(wide, products, rotation):
            for h in range(heads):
                prob = jnp.exp2(products[0, h] - rows[rotation, h : h + 1, :])
                accum[1, :, lanes[h]] += dot_nn(prob.astype(jnp.bfloat16), wide[1, :, lanes[h]])
                slope = prob * (products[1, h] - rows[rotation, heads + h : heads + h + 1, :])
                accum[0, :, lanes[h]] += dot_nn(slope.astype(jnp.bfloat16), wide[0, :, lanes[h]])

        for n, table in enumerate(sources):
            wide, products = slot_refs[2 * n : 2 * n + 2]
            if table == list(range(blocks)):
                step(wide, products, 0)
            else:
                source = pick(table, place)
                rotation = lax.rem(place - source + blocks, blocks) - 1
                pl.when(source > place)(functools.partial(step, wide, products, rotation))
        if last:
            for group in range(geo.groups):
                at = slice(group * geo.tile_h, (group + 1) * geo.tile_h)
                outs[0][group] = (accum[0, at, :] * natural).astype(jnp.bfloat16)
                outs[1][group] = accum[1, at, :].astype(jnp.bfloat16)

    ins = [x for slot in slots for x in slot] + list(stats)
    ins += [] if state is None else [state]
    running = (2, tokens, width)
    shapes = [jax.ShapeDtypeStruct(running, jnp.float32)]
    if last:
        shapes = [jax.ShapeDtypeStruct((geo.groups, geo.tile_h, width), jnp.bfloat16)] * 2
    return call(
        kernel,
        "key_grads",
        [whole()] * len(ins),
        [whole()] * len(shapes),
        shapes,
        ([pltpu.VMEM(running, jnp.float32)] if last else [])
        + [pltpu.VMEM((len(stats), stat_rows, wide_rows), jnp.float32)],
        8,
        2,
    )(*ins)


def rotate(x, by, blocks):
    return lax.ppermute(x, "span", [(i, (i + by) % blocks) for i in range(blocks)])


def shards(queries, cache_keys, cache_values, grad_attended, radius, frame_count, sizes):
    blocks, count_h, count_w = sizes
    frames, tile_h, tile_w, width = queries.shape[1:]
    heads = radius.shape[0]
    geo = Geometry(frames, tile_h, tile_w, count_h, count_w)
    small = (radius, frame_count)

    def grouped(x):
        return jnp.transpose(x[0], (0, 2, 1, 3)).reshape(geo.groups, tile_h, width)

    def restored(x):
        x = x.reshape(frames, tile_w, tile_h, width)
        return jnp.transpose(x, (0, 2, 1, 3))[None]

    arrays = [grouped(x) for x in (cache_keys, cache_values, queries, grad_attended)]
    own, *chains = tidy(geo, arrays, blocks)
    batches = relay(blocks)
    needed = {step for steps, _, _ in batches for step in steps}
    sources = [list(range(blocks))] + [blks for _, _, blks in batches]
    moved = {}

    def hop(chain, number, after):
        if any(c == chain and n >= number for c, n in needed):
            x = chains[chain]
            x = lax.optimization_barrier((x, *after))[0] if after else x
            pairs = list(enumerate(swap(blocks, chain, number)))
            moved[chain, number] = chains[chain] = lax.ppermute(x, "span", pairs)

    def take(n, after):
        steps, which, _ = batches[n - 1]
        group = ([moved[step] for step in steps], which, 0)
        (x,), (messages,) = pack_rows(geo, [group], after, n == blocks - 1)
        return x, messages

    hop(0, 1, [])
    hop(1, 1, [])
    xs, messages = pack_rows(geo, [([own], None, 0), ([own], None, 2)], [])
    own_rows = [geo.exchange_rows(group) for group in messages]
    hop(0, 2, messages[0][:1])
    x, messages = take(1, [])
    first = list(messages[:1])
    exchange = geo.exchange_all if blocks == 2 else geo.exchange_rows
    pieces = exchange(messages)
    messages = pack_cols(geo, xs, [0, 2], own_rows, first)
    hop(1, 2, list(messages[:1]))
    cols = geo.exchange_cols(messages)
    parts = [own] + own_rows[1] + cols
    bases = [2] + [0] * len(own_rows[1]) + [2] * len(cols)
    asked = lay_out(geo, heads, small, own, parts, bases)
    parts = [own] + own_rows[0] + cols
    wide, products, *state = forward(
        geo, heads, small, own, sources[0], parts, [0] * len(parts), None, False, first
    )
    slots = [[wide, products]]
    for n in range(1, blocks):
        last = n == blocks - 1
        after = [asked[0]]
        if last:
            parts = [x] + pieces
        else:
            messages = pack_cols(geo, [x], [0], [pieces], [state[0]])
            ready = list(messages[:1])
            parts = [x] + pieces + geo.exchange_cols(messages)
            hop(0, n + 2, [state[0]])
            x, messages = take(n + 1, ready)
            after += list(messages[:1])
            hop(1, n + 2, list(messages[:1]))
            exchange = geo.exchange_all if n == blocks - 2 else geo.exchange_rows
            pieces = exchange(messages)
        wide, products, *state = forward(
            geo, heads, small, own, sources[n], parts, [0] * len(parts), state, last, after
        )
        slots.append([wide, products])
    attended, lse, delta, packed = state

    grad_q, token = query_grads(geo, heads, lse, delta, sources, slots)
    brought = geo.exchange_all([packed] * len(geo.places))
    own_stats = merge(geo, [packed] + brought, [token])
    stats = [rotate(own_stats, n, blocks) for n in range(1, blocks)]
    begun = key_grads(geo, blocks, heads, [own_stats], sources[:1], [asked], None, False)[0]
    grad_k, grad_v = key_grads(
        geo, blocks, heads, stats, sources[1:], slots[1:], begun, True
    )
    return tuple(restored(x) for x in (attended, grad_q, grad_k, grad_v))


def solution(mesh):
    placed = P("span", None, "ha", "wa", None)
    sizes = tuple(mesh.shape[name] for name in ("span", "ha", "wa"))
    return jax.shard_map(
        functools.partial(shards, sizes=sizes),
        mesh=mesh,
        in_specs=(placed,) * 4 + (P(), P()),
        out_specs=(placed,) * 4,
        check_vma=False,
    )
```

```python
import functools
import math

import jax
import jax.numpy as jnp
import ml_dtypes
import numpy as np
from jax import lax
from jax.experimental import pallas as pl
from jax.experimental.pallas import tpu as pltpu
from jax.sharding import PartitionSpec as P

RMAX = 2
FAR = 99.0
LOG2E = math.log2(math.e)
LANES = 128


def round_up(value, unit):
    return (value + unit - 1) // unit * unit


def dot_nt(a, b):
    return lax.dot_general(a, b, (((1,), (1,)), ((), ())), preferred_element_type=jnp.float32)


def dot_nn(a, b):
    return lax.dot_general(a, b, (((1,), (0,)), ((), ())), preferred_element_type=jnp.float32)


class Side:
    def __init__(self, kind, count, tile, variant):
        self.kind, self.count = kind, count
        if kind == "same":
            self.start, self.length, self.send_start = 0, tile, 0
        else:
            delta = self.delta(variant)
            target = delta if kind in ("pair", "other") else -delta
            self.length = RMAX
            self.start = tile if delta > 0 else -RMAX
            self.send_start = tile - RMAX if target > 0 else 0
        if kind in ("pair", "other"):
            near = [i + self.delta(i % 2) for i in range(count)]
            self.pairs = [(j if 0 <= j < count else i, i) for i, j in enumerate(near)]
        else:
            self.pairs = [((i + self.delta(0)) % count, i) for i in range(count)]

    def delta(self, variant):
        if self.kind == "same":
            return 0
        if self.kind == "pair":
            return 1 - 2 * variant
        return 2 * variant - 1 if self.kind == "other" else self.kind

    def inside(self, index):
        other = index + self.delta(lax.rem(index, 2))
        return (other >= 0) & (other < self.count)


def sides(count, tile, variant):
    kinds = [] if count == 1 else ["pair"] if count == 2 else ["pair", "other"]
    if count % 2 and count > 1:
        kinds = [-1, 1]
    return [Side(kind, count, tile, variant) for kind in ["same"] + kinds]


class Geometry:
    def __init__(self, frames, tile_h, tile_w, count_h, count_w):
        self.frames, self.tile_h, self.tile_w = frames, tile_h, tile_w
        self.count_h, self.count_w = count_h, count_w
        self.tokens = frames * tile_h * tile_w
        self.groups = frames * tile_w
        self.variants_h = 2 - count_h % 2
        self.variants_w = 2 - count_w % 2
        found = [
            self.variant(variant_h, variant_w)
            for variant_h in range(self.variants_h)
            for variant_w in range(self.variants_w)
        ]
        direct, tall, gap = (np.stack(arrays) for arrays in zip(*found))
        own = np.arange(self.tokens)
        starts = [start for start, *_ in self.ranges] + [self.used]
        self.places = [(a, b - a) for a, b in zip(starts, starts[1:])][1:]
        self.all_select = self.one_hot(direct[:, self.tokens : self.used], self.tokens)
        self.row_select = self.one_hot(direct[:, self.tokens : self.tall], self.tokens)
        self.col_select = self.one_hot(tall[:, self.tall : self.used], self.tall)
        self.select = self.one_hot(direct, self.tokens)
        self.gap = gap.astype(np.float32)
        assert (direct[:, : self.tokens] == own).all()

    def one_hot(self, index, count):
        return (index[..., None] == np.arange(count)).astype(ml_dtypes.bfloat16)

    def variant(self, variant_h, variant_w):
        row_own, *rows_of = sides(self.count_h, self.tile_h, variant_h)
        col_own, *cols_of = sides(self.count_w, self.tile_w, variant_w)
        self.row_sides, self.col_sides = rows_of, cols_of
        direct, tall, rows, cols, frame = [], [], [], [], []
        self.ranges = []

        def add(row, col, base):
            ff, xx, yy = np.unravel_index(
                np.arange(self.frames * col.length * row.length),
                (self.frames, col.length, row.length),
            )
            start = len(direct)
            own_x, own_y = col.send_start + xx, row.send_start + yy
            direct.extend((ff * self.tile_w + own_x) * self.tile_h + own_y)
            tall.extend(base + (ff * self.tile_w + own_x) * row.length + yy)
            rows.extend(row.start + yy)
            cols.extend(col.start + xx)
            frame.extend(ff)
            self.ranges.append((start, len(direct), row, col))

        def pad(unit):
            count = round_up(len(direct), unit) - len(direct)
            for array, value in zip((direct, tall, rows, cols, frame), (-1, -1, 1000, 1000, 0)):
                array.extend([value] * count)

        add(row_own, col_own, 0)
        bases = []
        self.row_places, self.col_places = [], []
        for row in rows_of:
            bases.append(len(direct))
            add(row, col_own, bases[-1])
            pad(16)
            self.row_places.append((bases[-1], len(direct) - bases[-1]))
        self.tall = len(direct)
        for col in cols_of:
            start = len(direct)
            for row, base in zip([row_own] + rows_of, [0] + bases):
                add(row, col, base)
                pad(16)
            self.col_places.append((start, len(direct) - start))
        self.used = len(direct)
        pad(LANES)
        self.wide = len(direct)
        self.frame = np.array(frame, np.int32)
        rows, cols = np.array(rows), np.array(cols)
        mine = slice(0, self.tokens)
        gap = np.maximum(
            np.abs(rows[mine][:, None] - rows[None, :]), np.abs(cols[mine][:, None] - cols[None, :])
        )
        return np.array(direct), np.array(tall), np.minimum(gap, FAR)

    def which(self):
        at_h = lax.rem(lax.axis_index("ha"), self.variants_h)
        at_w = lax.rem(lax.axis_index("wa"), self.variants_w)
        return at_h * self.variants_w + at_w

    def near(self, gap_ref):
        lane = lax.broadcasted_iota(jnp.int32, (1, self.wide), 1)
        far = jnp.zeros((1, self.wide), jnp.float32)
        for start, end, row, col in self.ranges[1:]:
            inside = row.inside(lax.axis_index("ha")) & col.inside(lax.axis_index("wa"))
            cost = jnp.where(inside, 0.0, FAR)
            far = jnp.where((lane >= start) & (lane < end), cost, far)
        return gap_ref[self.which()] + far

    def permute(self, row, col, x):
        pairs = [
            (a * self.count_w + c, b * self.count_w + d)
            for a, b in row.pairs
            for c, d in col.pairs
        ]
        return lax.ppermute(x, ("ha", "wa"), pairs)

    def exchange_rows(self, messages):
        own = self.ranges[0][3]
        return [self.permute(row, own, x) for row, x in zip(self.row_sides, messages)]

    def exchange_cols(self, messages):
        own = self.ranges[0][2]
        return [self.permute(own, col, x) for col, x in zip(self.col_sides, messages)]

    def exchange_all(self, messages):
        return [self.permute(row, col, x) for x, (_, _, row, col) in zip(messages, self.ranges[1:])]


def whole(memory=pltpu.VMEM):
    return pl.BlockSpec(memory_space=memory)


def call(kernel, name, in_specs, out_specs, out_shape, scratch, mib, cost, aliases=None):
    return pl.pallas_call(
        kernel,
        in_specs=in_specs,
        out_specs=out_specs,
        out_shape=out_shape,
        scratch_shapes=scratch,
        compiler_params=pltpu.CompilerParams(vmem_limit_bytes=mib * 1024 * 1024),
        cost_estimate=pl.CostEstimate(
            flops=int(cost * 1e9), bytes_accessed=int(cost * 2e6), transcendentals=0
        ),
        input_output_aliases=aliases or {},
        name=name,
    )


def pick(table, place):
    value = jnp.int32(table[0])
    for index, entry in enumerate(table[1:], 1):
        if entry != table[0]:
            value = jnp.where(place == index, entry, value)
    return value


def relay(blocks):
    held = [[(s, (s % 2 == 0) != bool(chain)) for s in range(blocks)] for chain in range(2)]
    fresh = [[] for _ in range(blocks)]
    for number in range(1, blocks):
        for chain in range(2):
            moved = [held[chain][a] for a in swap(blocks, chain, number)]
            held[chain] = moved
            for s, (block, keys) in enumerate(moved):
                if block != s and keys == (block < s) and block not in [b for _, b in fresh[s]]:
                    fresh[s].append(((chain, number), block))
    batches = []
    for n in range(blocks - 1):
        steps = sorted({fresh[s][n][0] for s in range(blocks)}, key=lambda step: step[::-1])
        which = [steps.index(fresh[s][n][0]) for s in range(blocks)]
        batches.append((steps, which, [fresh[s][n][1] for s in range(blocks)]))
    return batches


def swap(blocks, chain, number):
    start = (chain + number + 1) % 2
    partner = list(range(blocks))
    for low in range(start, blocks - 1, 2):
        partner[low], partner[low + 1] = low + 1, low
    return partner


def tidy(geo, arrays, blocks):
    width = arrays[0].shape[-1]
    tokens, tile_h = geo.tokens, geo.tile_h

    def kernel(*refs):
        ins, (own_ref, even_ref, odd_ref, stage, sems) = refs[:4], refs[4:]
        copies = [
            pltpu.make_async_copy(ref, stage.at[number], sems.at[number])
            for number, ref in enumerate(ins)
        ]
        for copy in copies:
            copy.start()
        for number, copy in enumerate(copies):
            copy.wait()
            for group in range(geo.groups):
                own_ref[number, group * tile_h : (group + 1) * tile_h, :] = stage[number, group]
        odd = lax.rem(lax.axis_index("span"), 2)
        even_ref[...] = own_ref[pl.ds(2 * odd, 2)]
        odd_ref[...] = own_ref[pl.ds(2 - 2 * odd, 2)]

    pair = jax.ShapeDtypeStruct((2, tokens, width), jnp.bfloat16)
    return call(
        kernel,
        "tidy",
        [whole(pltpu.HBM)] * 4,
        [whole()] * 3,
        [jax.ShapeDtypeStruct((4, tokens, width), jnp.bfloat16), pair, pair],
        [
            pltpu.VMEM((4, geo.groups, tile_h, width), jnp.bfloat16),
            pltpu.SemaphoreType.DMA((4,)),
        ],
        60,
        2,
    )(*arrays)


def pack_rows(geo, groups, after, every=False):
    places = geo.places if every else geo.row_places
    select = geo.all_select if every else geo.row_select
    ins = [x for candidates, _, _ in groups for x in candidates]
    _, tokens, width = ins[0].shape
    several = [len(candidates) > 1 for candidates, _, _ in groups]

    def kernel(select_ref, *refs):
        refs, outs = refs[: len(ins)], list(refs[len(ins) + len(after) :])
        chosen = select_ref[geo.which()]
        kept = [outs.pop(0) if many else None for many in several]
        place = lax.axis_index("span")

        def work(x_ref, first, pair):
            for a in range(2):
                x = x_ref[first + a]
                if kept[pair] is not None:
                    kept[pair][a] = x
                picked = dot_nn(chosen, x).astype(jnp.bfloat16)
                for out, (start, size) in zip(outs[pair * len(places) :], places):
                    out[a] = picked[start - tokens : start - tokens + size]

        at = 0
        for pair, (candidates, which, first) in enumerate(groups):
            for index in range(len(candidates)):
                job = functools.partial(work, refs[at + index], first, pair)
                if several[pair]:
                    pl.when(pick(which, place) == index)(job)
                else:
                    job()
            at += len(candidates)

    shapes = [jax.ShapeDtypeStruct((2, tokens, width), jnp.bfloat16)] * sum(several)
    shapes += [
        jax.ShapeDtypeStruct((2, size, width), jnp.bfloat16) for _, size in places * len(groups)
    ]
    out = list(
        call(
            kernel,
            "pack_rows",
            [whole()] * (1 + len(ins)) + [whole(pl.ANY)] * len(after),
            [whole()] * len(shapes),
            shapes,
            [],
            12,
            0.2,
        )(select, *ins, *after)
    )
    xs = [out.pop(0) if many else group[0][0] for many, group in zip(several, groups)]
    return xs, [out[n * len(places) : (n + 1) * len(places)] for n in range(len(groups))]


def pack_cols(geo, xs, firsts, rows, after):
    count, sides = 2 * len(xs), len(rows[0])
    rows = [piece for pair in rows for piece in pair]
    _, tokens, width = xs[0].shape

    def kernel(select_ref, *refs):
        x_refs, refs = refs[: len(xs)], refs[len(xs) :]
        row_refs, refs = refs[: len(rows)], refs[len(rows) + len(after) :]
        outs, tall = refs[:-1], refs[-1]
        chosen = select_ref[geo.which()]
        for a in range(count):
            tall[a, :tokens] = x_refs[a // 2][firsts[a // 2] + a % 2]
            for ref, (start, size) in zip(row_refs[a // 2 * sides :], geo.row_places):
                tall[a, start : start + size] = ref[a % 2]
            picked = dot_nn(chosen, tall[a]).astype(jnp.bfloat16)
            for out, (start, size) in zip(outs, geo.col_places):
                out[a] = picked[start - geo.tall : start - geo.tall + size]

    return call(
        kernel,
        "pack_cols",
        [whole()] * (1 + len(xs) + len(rows)) + [whole(pl.ANY)] * len(after),
        [whole()] * len(geo.col_places),
        [jax.ShapeDtypeStruct((count, size, width), jnp.bfloat16) for _, size in geo.col_places],
        [pltpu.VMEM((count, geo.tall, width), jnp.bfloat16)],
        12,
        0.2,
    )(geo.col_select, *xs, *rows, *after)


def set_bias(bias_ref, gap):
    for reach in range(1, RMAX + 1):
        bias_ref[reach - 1] = jnp.where(gap <= reach, 0.0, -jnp.inf)


def fit(x, lanes):
    return x if x.shape[1] == lanes else jnp.broadcast_to(x[:, :1], (x.shape[0], lanes))


def repeat(x, lanes):
    return jnp.concatenate([x] * (lanes // LANES), axis=1)


def spread(geo, parts, bases, wide):
    places = geo.row_places + geo.col_places
    if len(parts) > 1 + len(places):
        places = geo.places
    for a in range(2):
        for ref, base, (start, size) in zip(parts, bases, [(0, geo.tokens)] + places):
            wide[a, start : start + size] = ref[base + a]
        if geo.wide > geo.used:
            wide[a, geo.used :] = jnp.zeros((geo.wide - geo.used, wide.shape[-1]), jnp.bfloat16)


def lay_out(geo, heads, small, own, parts, bases):
    tokens, wide_rows = geo.tokens, geo.wide
    width = own.shape[-1]
    depth = width // heads
    scale = LOG2E / math.sqrt(depth)

    def kernel(radius_ref, live_ref, gap_ref, row_frame_ref, own_ref, *refs):
        parts_refs, (wide, products, bias_ref) = refs[: len(parts)], refs[len(parts) :]
        spread(geo, parts_refs, bases, wide)
        live = row_frame_ref[...] < live_ref[lax.axis_index("span")]
        set_bias(bias_ref, jnp.where(live, geo.near(gap_ref), FAR))
        for h in range(heads):
            lanes = slice(h * depth, (h + 1) * depth)
            score = dot_nt(own_ref[0, :, lanes], wide[0, :, lanes])
            products[0, h] = score * scale + bias_ref[radius_ref[h] - 1]
            products[1, h] = dot_nt(own_ref[1, :, lanes], wide[1, :, lanes])

    return call(
        kernel,
        "lay_out",
        [whole(pltpu.SMEM)] * 2 + [whole()] * (3 + len(parts)),
        [whole()] * 2,
        [
            jax.ShapeDtypeStruct((2, wide_rows, width), jnp.bfloat16),
            jax.ShapeDtypeStruct((2, heads, tokens, wide_rows), jnp.float32),
        ],
        [pltpu.VMEM((RMAX, tokens, wide_rows), jnp.float32)],
        16,
        0.5,
    )(*small, geo.gap, geo.frame[:tokens, None], own, *parts)


def forward(geo, heads, small, own, sources, parts, bases, state, last, after):
    tokens, wide_rows = geo.tokens, geo.wide
    width = own.shape[-1]
    depth = width // heads
    scale = LOG2E / math.sqrt(depth)
    per = len(parts)
    stat_rows = round_up(2 * heads, 8)
    first = state is None
    lanes = [slice(h * depth, (h + 1) * depth) for h in range(heads)]

    def kernel(
        radius_ref, live_ref, gap_ref, frame_ref, row_frame_ref, select_ref, own_ref, *refs
    ):
        parts_refs, refs = refs[:per], refs[per:]
        state_in, refs = (None, refs) if first else (refs[:3], refs[3:])
        wide, products, *refs = refs[len(after) :]
        if last:
            outs, (accum, top, total, bias_ref) = refs[:4], refs[4:]
        else:
            accum, top, total, bias_ref = refs
        place = lax.axis_index("span")
        source = place if first else pick(sources, place)
        active = source <= place

        spread(geo, parts_refs, bases, wide)
        if first:
            accum[...] = jnp.zeros(accum.shape, jnp.float32)
            top[...] = jnp.full(top.shape, -jnp.inf, jnp.float32)
            total[...] = jnp.zeros(total.shape, jnp.float32)
        else:
            for old, new in zip(state_in, (accum, top, total)):
                new[...] = old[...]

        def multiply(h, base):
            score = dot_nt(own_ref[base, :, lanes[h]], wide[0, :, lanes[h]])
            score = score * scale + bias_ref[radius_ref[h] - 1]
            products[0, h] = score
            products[1, h] = dot_nt(own_ref[base + 1, :, lanes[h]], wide[1, :, lanes[h]])
            return score

        def attend():
            live = frame_ref[...] < live_ref[source]
            set_bias(bias_ref, jnp.where(live, geo.near(gap_ref), FAR))
            ones = jnp.ones((wide_rows, LANES), jnp.bfloat16)
            ahead = multiply(0, 2)
            for h in range(heads):
                score = ahead
                if h + 1 < heads:
                    ahead = multiply(h + 1, 2)
                best = jnp.max(score, axis=1, keepdims=True)
                new_top = jnp.maximum(top[h], best)
                fading = jnp.exp2(top[h] - new_top)
                top[h] = new_top
                weight = jnp.exp2(score - repeat(new_top, wide_rows)).astype(jnp.bfloat16)
                value = jnp.concatenate([wide[1, :, lanes[h]], ones], axis=1)
                both = dot_nn(weight, value)
                accum[:, lanes[h]] = accum[:, lanes[h]] * fit(fading, depth) + both[:, :depth]
                total[h] = total[h] * fading + both[:, depth:]

        def keep():
            live = row_frame_ref[...] < live_ref[place]
            set_bias(bias_ref, jnp.where(live, geo.near(gap_ref), FAR))
            for h in range(heads):
                multiply(h, 0)

        def finish():
            attended_ref, lse_ref, delta_ref, packed_ref = outs
            lane = lax.broadcasted_iota(jnp.int32, (tokens, LANES), 1)
            column = jnp.zeros((tokens, LANES), jnp.float32)
            for h in range(heads):
                rounded = (accum[:, lanes[h]] / fit(total[h], depth)).astype(jnp.bfloat16)
                rounded = rounded.astype(jnp.float32)
                accum[:, lanes[h]] = rounded
                lse = top[h] + jnp.log2(total[h])
                grad = own_ref[3, :, lanes[h]].astype(jnp.float32)
                delta = jnp.sum(rounded * grad, axis=1, keepdims=True)
                delta = jnp.broadcast_to(delta, (tokens, LANES))
                lse_ref[h] = lse
                delta_ref[h] = delta
                column = jnp.where(lane == h, lse, column)
                column = jnp.where(lane == heads + h, delta, column)
            packed = jnp.zeros((wide_rows, LANES), jnp.float32)
            rest = column
            chosen = select_ref[geo.which()]
            for _ in range(3):
                part = rest.astype(jnp.bfloat16)
                rest = rest - part.astype(jnp.float32)
                packed = packed + dot_nn(chosen, part)
            packed_ref[...] = jnp.transpose(packed)[:stat_rows]
            for group in range(geo.groups):
                at = slice(group * geo.tile_h, (group + 1) * geo.tile_h)
                attended_ref[group] = accum[at, :].astype(jnp.bfloat16)

        if first:
            attend()
        else:
            pl.when(active)(attend)
            pl.when(jnp.logical_not(active))(keep)
        if last:
            finish()

    ins = [*small, geo.gap, geo.frame[None, :], geo.frame[:tokens, None], geo.select, own, *parts]
    ins += [] if first else list(state)
    stat = (heads, tokens, LANES)
    running = [(tokens, width), stat, stat]
    shapes = [
        jax.ShapeDtypeStruct((2, wide_rows, width), jnp.bfloat16),
        jax.ShapeDtypeStruct((2, heads, tokens, wide_rows), jnp.float32),
    ]
    scratch = []
    if last:
        shapes += [
            jax.ShapeDtypeStruct((geo.groups, geo.tile_h, width), jnp.bfloat16),
            jax.ShapeDtypeStruct(stat, jnp.float32),
            jax.ShapeDtypeStruct(stat, jnp.float32),
            jax.ShapeDtypeStruct((stat_rows, wide_rows), jnp.float32),
        ]
        scratch += [pltpu.VMEM(shape, jnp.float32) for shape in running]
    else:
        shapes += [jax.ShapeDtypeStruct(shape, jnp.float32) for shape in running]
    return call(
        kernel,
        "forward",
        [whole(pltpu.SMEM)] * 2 + [whole()] * (len(ins) - 2) + [whole(pl.ANY)] * len(after),
        [whole()] * len(shapes),
        shapes,
        scratch + [pltpu.VMEM((RMAX, tokens, wide_rows), jnp.float32)],
        20,
        1.5,
    )(*ins, *after)


def merge(geo, pieces, after):
    def kernel(*refs):
        out = refs[-1]
        row = refs[0][...]
        lane = lax.broadcasted_iota(jnp.int32, row.shape, 1)
        for ref, (start, *_) in zip(refs[1:], geo.ranges[1:]):
            row = jnp.where(lane >= start, ref[...], row)
        out[...] = row

    return call(
        kernel,
        "merge",
        [whole()] * len(pieces) + [whole(pl.ANY)] * len(after),
        whole(),
        jax.ShapeDtypeStruct(pieces[0].shape, jnp.float32),
        [],
        4,
        0.1,
    )(*pieces, *after)


def query_grads(geo, heads, lse, delta, sources, slots):
    tokens, wide_rows = geo.tokens, geo.wide
    width = slots[0][0].shape[-1]
    depth = width // heads
    natural = 1.0 / math.sqrt(depth)
    lanes = [slice(h * depth, (h + 1) * depth) for h in range(heads)]

    def kernel(lse_ref, delta_ref, *refs):
        slot_refs, (out, token, accum) = refs[: 2 * len(slots)], refs[2 * len(slots) :]
        token[...] = jnp.zeros(token.shape, jnp.float32)
        place = lax.axis_index("span")

        def step(wide, products, first):
            for h in range(heads):
                prob = jnp.exp2(products[0, h] - repeat(lse_ref[h], wide_rows))
                slope = prob * (products[1, h] - repeat(delta_ref[h], wide_rows))
                part = dot_nn(slope.astype(jnp.bfloat16), wide[0, :, lanes[h]])
                accum[:, lanes[h]] = part if first else accum[:, lanes[h]] + part

        for n, table in enumerate(sources):
            work = functools.partial(step, slot_refs[2 * n], slot_refs[2 * n + 1], n == 0)
            if n == 0:
                work()
            else:
                pl.when(pick(table, place) < place)(work)
        for group in range(geo.groups):
            at = slice(group * geo.tile_h, (group + 1) * geo.tile_h)
            out[group] = (accum[at, :] * natural).astype(jnp.bfloat16)

    flat = [x for slot in slots for x in slot]
    return call(
        kernel,
        "query_grads",
        [whole()] * (2 + len(flat)),
        [whole()] * 2,
        [
            jax.ShapeDtypeStruct((geo.groups, geo.tile_h, width), jnp.bfloat16),
            jax.ShapeDtypeStruct((8, LANES), jnp.float32),
        ],
        [pltpu.VMEM((tokens, width), jnp.float32)],
        8,
        2,
    )(lse, delta, *flat)


def key_grads(geo, blocks, heads, stats, sources, slots, state, last):
    tokens, wide_rows = geo.tokens, geo.wide
    width = slots[0][0].shape[-1]
    depth = width // heads
    natural = 1.0 / math.sqrt(depth)
    stat_rows = stats[0].shape[0]
    lanes = [slice(h * depth, (h + 1) * depth) for h in range(heads)]

    def kernel(*refs):
        slot_refs, refs = refs[: 2 * len(slots)], refs[2 * len(slots) :]
        stat_refs, refs = refs[: len(stats)], refs[len(stats) :]
        state_in, refs = (None, refs) if state is None else (refs[0], refs[1:])
        outs, refs = (refs[:2], refs[2:]) if last else (None, refs)
        accum, rows = refs
        place = lax.axis_index("span")
        accum[...] = jnp.zeros(accum.shape, jnp.float32) if state is None else state_in[...]
        for n, ref in enumerate(stat_refs):
            rows[n] = ref[...]

        def step(wide, products, rotation):
            for h in range(heads):
                prob = jnp.exp2(products[0, h] - rows[rotation, h : h + 1, :])
                accum[1, :, lanes[h]] += dot_nn(prob.astype(jnp.bfloat16), wide[1, :, lanes[h]])
                slope = prob * (products[1, h] - rows[rotation, heads + h : heads + h + 1, :])
                accum[0, :, lanes[h]] += dot_nn(slope.astype(jnp.bfloat16), wide[0, :, lanes[h]])

        for n, table in enumerate(sources):
            wide, products = slot_refs[2 * n : 2 * n + 2]
            if table == list(range(blocks)):
                step(wide, products, 0)
            else:
                source = pick(table, place)
                rotation = lax.rem(place - source + blocks, blocks) - 1
                pl.when(source > place)(functools.partial(step, wide, products, rotation))
        if last:
            for group in range(geo.groups):
                at = slice(group * geo.tile_h, (group + 1) * geo.tile_h)
                outs[0][group] = (accum[0, at, :] * natural).astype(jnp.bfloat16)
                outs[1][group] = accum[1, at, :].astype(jnp.bfloat16)

    ins = [x for slot in slots for x in slot] + list(stats)
    ins += [] if state is None else [state]
    running = (2, tokens, width)
    shapes = [jax.ShapeDtypeStruct(running, jnp.float32)]
    if last:
        shapes = [jax.ShapeDtypeStruct((geo.groups, geo.tile_h, width), jnp.bfloat16)] * 2
    return call(
        kernel,
        "key_grads",
        [whole()] * len(ins),
        [whole()] * len(shapes),
        shapes,
        ([pltpu.VMEM(running, jnp.float32)] if last else [])
        + [pltpu.VMEM((len(stats), stat_rows, wide_rows), jnp.float32)],
        8,
        2,
    )(*ins)


def rotate(x, by, blocks):
    return lax.ppermute(x, "span", [(i, (i + by) % blocks) for i in range(blocks)])


def shards(queries, cache_keys, cache_values, grad_attended, radius, frame_count, sizes):
    blocks, count_h, count_w = sizes
    frames, tile_h, tile_w, width = queries.shape[1:]
    heads = radius.shape[0]
    geo = Geometry(frames, tile_h, tile_w, count_h, count_w)
    small = (radius, frame_count)

    def grouped(x):
        return jnp.transpose(x[0], (0, 2, 1, 3)).reshape(geo.groups, tile_h, width)

    def restored(x):
        x = x.reshape(frames, tile_w, tile_h, width)
        return jnp.transpose(x, (0, 2, 1, 3))[None]

    arrays = [grouped(x) for x in (cache_keys, cache_values, queries, grad_attended)]
    own, *chains = tidy(geo, arrays, blocks)
    batches = relay(blocks)
    needed = {step for steps, _, _ in batches for step in steps}
    sources = [list(range(blocks))] + [blks for _, _, blks in batches]
    moved = {}

    def hop(chain, number, after):
        if any(c == chain and n >= number for c, n in needed):
            x = chains[chain]
            x = lax.optimization_barrier((x, *after))[0] if after else x
            pairs = list(enumerate(swap(blocks, chain, number)))
            moved[chain, number] = chains[chain] = lax.ppermute(x, "span", pairs)

    def take(n, after):
        steps, which, _ = batches[n - 1]
        group = ([moved[step] for step in steps], which, 0)
        (x,), (messages,) = pack_rows(geo, [group], after, n == blocks - 1)
        return x, messages

    hop(0, 1, [])
    hop(1, 1, [])
    xs, messages = pack_rows(geo, [([own], None, 0), ([own], None, 2)], [])
    own_rows = [geo.exchange_rows(group) for group in messages]
    hop(0, 2, messages[0][:1])
    x, messages = take(1, [])
    first = list(messages[:1])
    exchange = geo.exchange_all if blocks == 2 else geo.exchange_rows
    pieces = exchange(messages)
    messages = pack_cols(geo, xs, [0, 2], own_rows, first)
    hop(1, 2, list(messages[:1]))
    cols = geo.exchange_cols(messages)
    parts = [own] + own_rows[1] + cols
    bases = [2] + [0] * len(own_rows[1]) + [2] * len(cols)
    asked = lay_out(geo, heads, small, own, parts, bases)
    parts = [own] + own_rows[0] + cols
    wide, products, *state = forward(
        geo, heads, small, own, sources[0], parts, [0] * len(parts), None, False, first
    )
    slots = [[wide, products]]
    for n in range(1, blocks):
        last = n == blocks - 1
        after = [asked[0]]
        if last:
            parts = [x] + pieces
        else:
            messages = pack_cols(geo, [x], [0], [pieces], [state[0]])
            ready = list(messages[:1])
            parts = [x] + pieces + geo.exchange_cols(messages)
            hop(0, n + 2, [state[0]])
            x, messages = take(n + 1, ready)
            after += list(messages[:1])
            hop(1, n + 2, list(messages[:1]))
            exchange = geo.exchange_all if n == blocks - 2 else geo.exchange_rows
            pieces = exchange(messages)
        wide, products, *state = forward(
            geo, heads, small, own, sources[n], parts, [0] * len(parts), state, last, after
        )
        slots.append([wide, products])
    attended, lse, delta, packed = state

    grad_q, token = query_grads(geo, heads, lse, delta, sources, slots)
    brought = geo.exchange_all([packed] * len(geo.places))
    own_stats = merge(geo, [packed] + brought, [token])
    stats = [rotate(own_stats, n, blocks) for n in range(1, blocks)]
    begun = key_grads(geo, blocks, heads, [own_stats], sources[:1], [asked], None, False)[0]
    grad_k, grad_v = key_grads(
        geo, blocks, heads, stats, sources[1:], slots[1:], begun, True
    )
    return tuple(restored(x) for x in (attended, grad_q, grad_k, grad_v))


def solution(mesh):
    placed = P("span", None, "ha", "wa", None)
    sizes = tuple(mesh.shape[name] for name in ("span", "ha", "wa"))
    return jax.shard_map(
        functools.partial(shards, sizes=sizes),
        mesh=mesh,
        in_specs=(placed,) * 4 + (P(), P()),
        out_specs=(placed,) * 4,
        check_vma=False,
    )
```

```python
import functools
import math

import jax
import jax.numpy as jnp
import ml_dtypes
import numpy as np
from jax import lax
from jax.experimental import pallas as pl
from jax.experimental.pallas import tpu as pltpu
from jax.sharding import PartitionSpec as P

RMAX = 2
FAR = 99.0
LOG2E = math.log2(math.e)
LANES = 128


def round_up(value, unit):
    return (value + unit - 1) // unit * unit


def dot_nt(a, b):
    return lax.dot_general(a, b, (((1,), (1,)), ((), ())), preferred_element_type=jnp.float32)


def dot_nn(a, b):
    return lax.dot_general(a, b, (((1,), (0,)), ((), ())), preferred_element_type=jnp.float32)


class Side:
    def __init__(self, kind, count, tile, variant):
        self.count = count
        self.swap = kind == "swap"
        if kind == "same":
            self.delta, self.start, self.length, self.send_start = 0, 0, tile, 0
        else:
            self.delta = 1 - 2 * variant if self.swap else kind
            send_up = (variant == 0) if self.swap else (kind < 0)
            self.length = RMAX
            self.start = tile if self.delta > 0 else -RMAX
            self.send_start = tile - RMAX if send_up else 0
        shift = 1 if self.swap else self.delta
        self.pairs = [((i + shift) % count, i) for i in range(count)]

    def place(self, index):
        delta = 1 - 2 * index if self.swap else self.delta
        other = index + delta
        inside = (other >= 0) & (other < self.count)
        return jnp.where(inside, other, index), inside


def sides(count, tile, variant):
    kinds = [] if count == 1 else ["swap"] if count == 2 else [-1, 1]
    return [Side(kind, count, tile, variant) for kind in ["same"] + kinds]


class Geometry:
    def __init__(self, frames, tile_h, tile_w, count_h, count_w):
        self.frames, self.tile_h, self.tile_w = frames, tile_h, tile_w
        self.count_h, self.count_w = count_h, count_w
        self.tokens = frames * tile_h * tile_w
        self.groups = frames * tile_w
        self.variants_h = 2 if count_h == 2 else 1
        self.variants_w = 2 if count_w == 2 else 1
        found = [
            self.variant(variant_h, variant_w)
            for variant_h in range(self.variants_h)
            for variant_w in range(self.variants_w)
        ]
        direct, tall, gap = (np.stack(arrays) for arrays in zip(*found))
        own = np.arange(self.tokens)
        starts = [start for start, *_ in self.ranges] + [self.used]
        self.places = [(a, b - a) for a, b in zip(starts, starts[1:])][1:]
        self.all_select = self.one_hot(direct[:, self.tokens : self.used], self.tokens)
        self.row_select = self.one_hot(direct[:, self.tokens : self.tall], self.tokens)
        self.col_select = self.one_hot(tall[:, self.tall : self.used], self.tall)
        self.select = self.one_hot(direct, self.tokens)
        self.gap = gap.astype(np.float32)
        assert (direct[:, : self.tokens] == own).all()

    def one_hot(self, index, count):
        return (index[..., None] == np.arange(count)).astype(ml_dtypes.bfloat16)

    def variant(self, variant_h, variant_w):
        row_own, *rows_of = sides(self.count_h, self.tile_h, variant_h)
        col_own, *cols_of = sides(self.count_w, self.tile_w, variant_w)
        self.row_sides, self.col_sides = rows_of, cols_of
        direct, tall, rows, cols, frame = [], [], [], [], []
        self.ranges = []

        def add(row, col, base):
            ff, xx, yy = np.unravel_index(
                np.arange(self.frames * col.length * row.length),
                (self.frames, col.length, row.length),
            )
            start = len(direct)
            own_x, own_y = col.send_start + xx, row.send_start + yy
            direct.extend((ff * self.tile_w + own_x) * self.tile_h + own_y)
            tall.extend(base + (ff * self.tile_w + own_x) * row.length + yy)
            rows.extend(row.start + yy)
            cols.extend(col.start + xx)
            frame.extend(ff)
            self.ranges.append((start, len(direct), row, col))

        def pad(unit):
            count = round_up(len(direct), unit) - len(direct)
            for array, value in zip((direct, tall, rows, cols, frame), (-1, -1, 1000, 1000, 0)):
                array.extend([value] * count)

        add(row_own, col_own, 0)
        bases = []
        self.row_places, self.col_places = [], []
        for row in rows_of:
            bases.append(len(direct))
            add(row, col_own, bases[-1])
            pad(16)
            self.row_places.append((bases[-1], len(direct) - bases[-1]))
        self.tall = len(direct)
        for col in cols_of:
            start = len(direct)
            for row, base in zip([row_own] + rows_of, [0] + bases):
                add(row, col, base)
                pad(16)
            self.col_places.append((start, len(direct) - start))
        self.used = len(direct)
        pad(LANES)
        self.wide = len(direct)
        self.frame = np.array(frame, np.int32)
        rows, cols = np.array(rows), np.array(cols)
        mine = slice(0, self.tokens)
        gap = np.maximum(
            np.abs(rows[mine][:, None] - rows[None, :]), np.abs(cols[mine][:, None] - cols[None, :])
        )
        return np.array(direct), np.array(tall), np.minimum(gap, FAR)

    def which(self):
        at_h = lax.axis_index("ha") if self.variants_h == 2 else 0
        at_w = lax.axis_index("wa") if self.variants_w == 2 else 0
        return at_h * self.variants_w + at_w

    def near(self, gap_ref):
        lane = lax.broadcasted_iota(jnp.int32, (1, self.wide), 1)
        far = jnp.zeros((1, self.wide), jnp.float32)
        for start, end, row, col in self.ranges[1:]:
            inside = row.place(lax.axis_index("ha"))[1] & col.place(lax.axis_index("wa"))[1]
            cost = jnp.where(inside, 0.0, FAR)
            far = jnp.where((lane >= start) & (lane < end), cost, far)
        return gap_ref[self.which()] + far

    def permute(self, row, col, x):
        pairs = [
            (a * self.count_w + c, b * self.count_w + d)
            for a, b in row.pairs
            for c, d in col.pairs
        ]
        return lax.ppermute(x, ("ha", "wa"), pairs)

    def exchange_rows(self, messages):
        own = self.ranges[0][3]
        return [self.permute(row, own, x) for row, x in zip(self.row_sides, messages)]

    def exchange_cols(self, messages):
        own = self.ranges[0][2]
        return [self.permute(own, col, x) for col, x in zip(self.col_sides, messages)]

    def exchange_all(self, messages):
        return [self.permute(row, col, x) for x, (_, _, row, col) in zip(messages, self.ranges[1:])]


def whole(memory=pltpu.VMEM):
    return pl.BlockSpec(memory_space=memory)


def call(kernel, name, in_specs, out_specs, out_shape, scratch, mib, cost, aliases=None):
    return pl.pallas_call(
        kernel,
        in_specs=in_specs,
        out_specs=out_specs,
        out_shape=out_shape,
        scratch_shapes=scratch,
        compiler_params=pltpu.CompilerParams(vmem_limit_bytes=mib * 1024 * 1024),
        cost_estimate=pl.CostEstimate(
            flops=int(cost * 1e9), bytes_accessed=int(cost * 2e6), transcendentals=0
        ),
        input_output_aliases=aliases or {},
        name=name,
    )


def pick(table, place):
    value = jnp.int32(table[0])
    for index, entry in enumerate(table[1:], 1):
        if entry != table[0]:
            value = jnp.where(place == index, entry, value)
    return value


def relay(blocks):
    held = [[(s, (s % 2 == 0) != bool(chain)) for s in range(blocks)] for chain in range(2)]
    fresh = [[] for _ in range(blocks)]
    for number in range(1, blocks):
        for chain in range(2):
            moved = [held[chain][a] for a in swap(blocks, chain, number)]
            held[chain] = moved
            for s, (block, keys) in enumerate(moved):
                if block != s and keys == (block < s) and block not in [b for _, b in fresh[s]]:
                    fresh[s].append(((chain, number), block))
    batches = []
    for n in range(blocks - 1):
        steps = sorted({fresh[s][n][0] for s in range(blocks)}, key=lambda step: step[::-1])
        which = [steps.index(fresh[s][n][0]) for s in range(blocks)]
        batches.append((steps, which, [fresh[s][n][1] for s in range(blocks)]))
    return batches


def swap(blocks, chain, number):
    start = (chain + number + 1) % 2
    partner = list(range(blocks))
    for low in range(start, blocks - 1, 2):
        partner[low], partner[low + 1] = low + 1, low
    return partner


def tidy(geo, arrays, blocks):
    width = arrays[0].shape[-1]
    tokens, tile_h = geo.tokens, geo.tile_h

    def kernel(*refs):
        ins, (own_ref, even_ref, odd_ref, stage, sems) = refs[:4], refs[4:]
        copies = [
            pltpu.make_async_copy(ref, stage.at[number], sems.at[number])
            for number, ref in enumerate(ins)
        ]
        for copy in copies:
            copy.start()
        for number, copy in enumerate(copies):
            copy.wait()
            for group in range(geo.groups):
                own_ref[number, group * tile_h : (group + 1) * tile_h, :] = stage[number, group]
        odd = lax.rem(lax.axis_index("span"), 2)
        even_ref[...] = own_ref[pl.ds(2 * odd, 2)]
        odd_ref[...] = own_ref[pl.ds(2 - 2 * odd, 2)]

    pair = jax.ShapeDtypeStruct((2, tokens, width), jnp.bfloat16)
    return call(
        kernel,
        "tidy",
        [whole(pltpu.HBM)] * 4,
        [whole()] * 3,
        [jax.ShapeDtypeStruct((4, tokens, width), jnp.bfloat16), pair, pair],
        [
            pltpu.VMEM((4, geo.groups, tile_h, width), jnp.bfloat16),
            pltpu.SemaphoreType.DMA((4,)),
        ],
        60,
        2,
    )(*arrays)


def pack_rows(geo, groups, after, every=False):
    places = geo.places if every else geo.row_places
    select = geo.all_select if every else geo.row_select
    ins = [x for candidates, _, _ in groups for x in candidates]
    _, tokens, width = ins[0].shape
    several = [len(candidates) > 1 for candidates, _, _ in groups]

    def kernel(select_ref, *refs):
        refs, outs = refs[: len(ins)], list(refs[len(ins) + len(after) :])
        chosen = select_ref[geo.which()]
        kept = [outs.pop(0) if many else None for many in several]
        place = lax.axis_index("span")

        def work(x_ref, first, pair):
            for a in range(2):
                x = x_ref[first + a]
                if kept[pair] is not None:
                    kept[pair][a] = x
                picked = dot_nn(chosen, x).astype(jnp.bfloat16)
                for out, (start, size) in zip(outs[pair * len(places) :], places):
                    out[a] = picked[start - tokens : start - tokens + size]

        at = 0
        for pair, (candidates, which, first) in enumerate(groups):
            for index in range(len(candidates)):
                job = functools.partial(work, refs[at + index], first, pair)
                if several[pair]:
                    pl.when(pick(which, place) == index)(job)
                else:
                    job()
            at += len(candidates)

    shapes = [jax.ShapeDtypeStruct((2, tokens, width), jnp.bfloat16)] * sum(several)
    shapes += [
        jax.ShapeDtypeStruct((2, size, width), jnp.bfloat16) for _, size in places * len(groups)
    ]
    out = list(
        call(
            kernel,
            "pack_rows",
            [whole()] * (1 + len(ins)) + [whole(pl.ANY)] * len(after),
            [whole()] * len(shapes),
            shapes,
            [],
            12,
            0.2,
        )(select, *ins, *after)
    )
    xs = [out.pop(0) if many else group[0][0] for many, group in zip(several, groups)]
    return xs, [out[n * len(places) : (n + 1) * len(places)] for n in range(len(groups))]


def pack_cols(geo, xs, firsts, rows, after):
    count, sides = 2 * len(xs), len(rows[0])
    rows = [piece for pair in rows for piece in pair]
    _, tokens, width = xs[0].shape

    def kernel(select_ref, *refs):
        x_refs, refs = refs[: len(xs)], refs[len(xs) :]
        row_refs, refs = refs[: len(rows)], refs[len(rows) + len(after) :]
        outs, tall = refs[:-1], refs[-1]
        chosen = select_ref[geo.which()]
        for a in range(count):
            tall[a, :tokens] = x_refs[a // 2][firsts[a // 2] + a % 2]
            for ref, (start, size) in zip(row_refs[a // 2 * sides :], geo.row_places):
                tall[a, start : start + size] = ref[a % 2]
            picked = dot_nn(chosen, tall[a]).astype(jnp.bfloat16)
            for out, (start, size) in zip(outs, geo.col_places):
                out[a] = picked[start - geo.tall : start - geo.tall + size]

    return call(
        kernel,
        "pack_cols",
        [whole()] * (1 + len(xs) + len(rows)) + [whole(pl.ANY)] * len(after),
        [whole()] * len(geo.col_places),
        [jax.ShapeDtypeStruct((count, size, width), jnp.bfloat16) for _, size in geo.col_places],
        [pltpu.VMEM((count, geo.tall, width), jnp.bfloat16)],
        12,
        0.2,
    )(geo.col_select, *xs, *rows, *after)


def set_bias(bias_ref, gap):
    for reach in range(1, RMAX + 1):
        bias_ref[reach - 1] = jnp.where(gap <= reach, 0.0, -jnp.inf)


def fit(x, lanes):
    return x if x.shape[1] == lanes else jnp.broadcast_to(x[:, :1], (x.shape[0], lanes))


def repeat(x, lanes):
    return jnp.concatenate([x] * (lanes // LANES), axis=1)


def spread(geo, parts, bases, wide):
    places = geo.row_places + geo.col_places
    if len(parts) > 1 + len(places):
        places = geo.places
    for a in range(2):
        for ref, base, (start, size) in zip(parts, bases, [(0, geo.tokens)] + places):
            wide[a, start : start + size] = ref[base + a]
        if geo.wide > geo.used:
            wide[a, geo.used :] = jnp.zeros((geo.wide - geo.used, wide.shape[-1]), jnp.bfloat16)


def lay_out(geo, heads, small, own, parts, bases):
    tokens, wide_rows = geo.tokens, geo.wide
    width = own.shape[-1]
    depth = width // heads
    scale = LOG2E / math.sqrt(depth)

    def kernel(radius_ref, live_ref, gap_ref, row_frame_ref, own_ref, *refs):
        parts_refs, (wide, products, bias_ref) = refs[: len(parts)], refs[len(parts) :]
        spread(geo, parts_refs, bases, wide)
        live = row_frame_ref[...] < live_ref[lax.axis_index("span")]
        set_bias(bias_ref, jnp.where(live, geo.near(gap_ref), FAR))
        for h in range(heads):
            lanes = slice(h * depth, (h + 1) * depth)
            score = dot_nt(own_ref[0, :, lanes], wide[0, :, lanes])
            products[0, h] = score * scale + bias_ref[radius_ref[h] - 1]
            products[1, h] = dot_nt(own_ref[1, :, lanes], wide[1, :, lanes])

    return call(
        kernel,
        "lay_out",
        [whole(pltpu.SMEM)] * 2 + [whole()] * (3 + len(parts)),
        [whole()] * 2,
        [
            jax.ShapeDtypeStruct((2, wide_rows, width), jnp.bfloat16),
            jax.ShapeDtypeStruct((2, heads, tokens, wide_rows), jnp.float32),
        ],
        [pltpu.VMEM((RMAX, tokens, wide_rows), jnp.float32)],
        16,
        0.5,
    )(*small, geo.gap, geo.frame[:tokens, None], own, *parts)


def forward(geo, heads, small, own, sources, parts, bases, state, last, after):
    tokens, wide_rows = geo.tokens, geo.wide
    width = own.shape[-1]
    depth = width // heads
    scale = LOG2E / math.sqrt(depth)
    per = len(parts)
    stat_rows = round_up(2 * heads, 8)
    first = state is None
    lanes = [slice(h * depth, (h + 1) * depth) for h in range(heads)]

    def kernel(
        radius_ref, live_ref, gap_ref, frame_ref, row_frame_ref, select_ref, own_ref, *refs
    ):
        parts_refs, refs = refs[:per], refs[per:]
        state_in, refs = (None, refs) if first else (refs[:3], refs[3:])
        wide, products, *refs = refs[len(after) :]
        if last:
            outs, (accum, top, total, bias_ref) = refs[:4], refs[4:]
        else:
            accum, top, total, bias_ref = refs
        place = lax.axis_index("span")
        source = place if first else pick(sources, place)
        active = source <= place

        spread(geo, parts_refs, bases, wide)
        if first:
            accum[...] = jnp.zeros(accum.shape, jnp.float32)
            top[...] = jnp.full(top.shape, -jnp.inf, jnp.float32)
            total[...] = jnp.zeros(total.shape, jnp.float32)
        else:
            for old, new in zip(state_in, (accum, top, total)):
                new[...] = old[...]

        def multiply(h, base):
            score = dot_nt(own_ref[base, :, lanes[h]], wide[0, :, lanes[h]])
            score = score * scale + bias_ref[radius_ref[h] - 1]
            products[0, h] = score
            products[1, h] = dot_nt(own_ref[base + 1, :, lanes[h]], wide[1, :, lanes[h]])
            return score

        def attend():
            live = frame_ref[...] < live_ref[source]
            set_bias(bias_ref, jnp.where(live, geo.near(gap_ref), FAR))
            ones = jnp.ones((wide_rows, LANES), jnp.bfloat16)
            ahead = multiply(0, 2)
            for h in range(heads):
                score = ahead
                if h + 1 < heads:
                    ahead = multiply(h + 1, 2)
                best = jnp.max(score, axis=1, keepdims=True)
                new_top = jnp.maximum(top[h], best)
                fading = jnp.exp2(top[h] - new_top)
                top[h] = new_top
                weight = jnp.exp2(score - repeat(new_top, wide_rows)).astype(jnp.bfloat16)
                value = jnp.concatenate([wide[1, :, lanes[h]], ones], axis=1)
                both = dot_nn(weight, value)
                accum[:, lanes[h]] = accum[:, lanes[h]] * fit(fading, depth) + both[:, :depth]
                total[h] = total[h] * fading + both[:, depth:]

        def keep():
            live = row_frame_ref[...] < live_ref[place]
            set_bias(bias_ref, jnp.where(live, geo.near(gap_ref), FAR))
            for h in range(heads):
                multiply(h, 0)

        def finish():
            attended_ref, lse_ref, delta_ref, packed_ref = outs
            lane = lax.broadcasted_iota(jnp.int32, (tokens, LANES), 1)
            column = jnp.zeros((tokens, LANES), jnp.float32)
            for h in range(heads):
                rounded = (accum[:, lanes[h]] / fit(total[h], depth)).astype(jnp.bfloat16)
                rounded = rounded.astype(jnp.float32)
                accum[:, lanes[h]] = rounded
                lse = top[h] + jnp.log2(total[h])
                grad = own_ref[3, :, lanes[h]].astype(jnp.float32)
                delta = jnp.sum(rounded * grad, axis=1, keepdims=True)
                delta = jnp.broadcast_to(delta, (tokens, LANES))
                lse_ref[h] = lse
                delta_ref[h] = delta
                column = jnp.where(lane == h, lse, column)
                column = jnp.where(lane == heads + h, delta, column)
            packed = jnp.zeros((wide_rows, LANES), jnp.float32)
            rest = column
            chosen = select_ref[geo.which()]
            for _ in range(3):
                part = rest.astype(jnp.bfloat16)
                rest = rest - part.astype(jnp.float32)
                packed = packed + dot_nn(chosen, part)
            packed_ref[...] = jnp.transpose(packed)[:stat_rows]
            for group in range(geo.groups):
                at = slice(group * geo.tile_h, (group + 1) * geo.tile_h)
                attended_ref[group] = accum[at, :].astype(jnp.bfloat16)

        if first:
            attend()
        else:
            pl.when(active)(attend)
            pl.when(jnp.logical_not(active))(keep)
        if last:
            finish()

    ins = [*small, geo.gap, geo.frame[None, :], geo.frame[:tokens, None], geo.select, own, *parts]
    ins += [] if first else list(state)
    stat = (heads, tokens, LANES)
    running = [(tokens, width), stat, stat]
    shapes = [
        jax.ShapeDtypeStruct((2, wide_rows, width), jnp.bfloat16),
        jax.ShapeDtypeStruct((2, heads, tokens, wide_rows), jnp.float32),
    ]
    scratch = []
    if last:
        shapes += [
            jax.ShapeDtypeStruct((geo.groups, geo.tile_h, width), jnp.bfloat16),
            jax.ShapeDtypeStruct(stat, jnp.float32),
            jax.ShapeDtypeStruct(stat, jnp.float32),
            jax.ShapeDtypeStruct((stat_rows, wide_rows), jnp.float32),
        ]
        scratch += [pltpu.VMEM(shape, jnp.float32) for shape in running]
    else:
        shapes += [jax.ShapeDtypeStruct(shape, jnp.float32) for shape in running]
    return call(
        kernel,
        "forward",
        [whole(pltpu.SMEM)] * 2 + [whole()] * (len(ins) - 2) + [whole(pl.ANY)] * len(after),
        [whole()] * len(shapes),
        shapes,
        scratch + [pltpu.VMEM((RMAX, tokens, wide_rows), jnp.float32)],
        20,
        1.5,
    )(*ins, *after)


def merge(geo, pieces, after):
    def kernel(*refs):
        out = refs[-1]
        row = refs[0][...]
        lane = lax.broadcasted_iota(jnp.int32, row.shape, 1)
        for ref, (start, *_) in zip(refs[1:], geo.ranges[1:]):
            row = jnp.where(lane >= start, ref[...], row)
        out[...] = row

    return call(
        kernel,
        "merge",
        [whole()] * len(pieces) + [whole(pl.ANY)] * len(after),
        whole(),
        jax.ShapeDtypeStruct(pieces[0].shape, jnp.float32),
        [],
        4,
        0.1,
    )(*pieces, *after)


def query_grads(geo, heads, lse, delta, sources, slots):
    tokens, wide_rows = geo.tokens, geo.wide
    width = slots[0][0].shape[-1]
    depth = width // heads
    natural = 1.0 / math.sqrt(depth)
    lanes = [slice(h * depth, (h + 1) * depth) for h in range(heads)]

    def kernel(lse_ref, delta_ref, *refs):
        slot_refs, (out, token, accum) = refs[: 2 * len(slots)], refs[2 * len(slots) :]
        token[...] = jnp.zeros(token.shape, jnp.float32)
        place = lax.axis_index("span")

        def step(wide, products, first):
            for h in range(heads):
                prob = jnp.exp2(products[0, h] - repeat(lse_ref[h], wide_rows))
                slope = prob * (products[1, h] - repeat(delta_ref[h], wide_rows))
                part = dot_nn(slope.astype(jnp.bfloat16), wide[0, :, lanes[h]])
                accum[:, lanes[h]] = part if first else accum[:, lanes[h]] + part

        for n, table in enumerate(sources):
            work = functools.partial(step, slot_refs[2 * n], slot_refs[2 * n + 1], n == 0)
            if n == 0:
                work()
            else:
                pl.when(pick(table, place) < place)(work)
        for group in range(geo.groups):
            at = slice(group * geo.tile_h, (group + 1) * geo.tile_h)
            out[group] = (accum[at, :] * natural).astype(jnp.bfloat16)

    flat = [x for slot in slots for x in slot]
    return call(
        kernel,
        "query_grads",
        [whole()] * (2 + len(flat)),
        [whole()] * 2,
        [
            jax.ShapeDtypeStruct((geo.groups, geo.tile_h, width), jnp.bfloat16),
            jax.ShapeDtypeStruct((8, LANES), jnp.float32),
        ],
        [pltpu.VMEM((tokens, width), jnp.float32)],
        8,
        2,
    )(lse, delta, *flat)


def key_grads(geo, blocks, heads, stats, sources, slots, state, last):
    tokens, wide_rows = geo.tokens, geo.wide
    width = slots[0][0].shape[-1]
    depth = width // heads
    natural = 1.0 / math.sqrt(depth)
    stat_rows = stats[0].shape[0]
    lanes = [slice(h * depth, (h + 1) * depth) for h in range(heads)]

    def kernel(*refs):
        slot_refs, refs = refs[: 2 * len(slots)], refs[2 * len(slots) :]
        stat_refs, refs = refs[: len(stats)], refs[len(stats) :]
        state_in, refs = (None, refs) if state is None else (refs[0], refs[1:])
        outs, refs = (refs[:2], refs[2:]) if last else (None, refs)
        accum, rows = refs
        place = lax.axis_index("span")
        accum[...] = jnp.zeros(accum.shape, jnp.float32) if state is None else state_in[...]
        for n, ref in enumerate(stat_refs):
            rows[n] = ref[...]

        def step(wide, products, rotation):
            for h in range(heads):
                prob = jnp.exp2(products[0, h] - rows[rotation, h : h + 1, :])
                accum[1, :, lanes[h]] += dot_nn(prob.astype(jnp.bfloat16), wide[1, :, lanes[h]])
                slope = prob * (products[1, h] - rows[rotation, heads + h : heads + h + 1, :])
                accum[0, :, lanes[h]] += dot_nn(slope.astype(jnp.bfloat16), wide[0, :, lanes[h]])

        for n, table in enumerate(sources):
            wide, products = slot_refs[2 * n : 2 * n + 2]
            if table == list(range(blocks)):
                step(wide, products, 0)
            else:
                source = pick(table, place)
                rotation = lax.rem(place - source + blocks, blocks) - 1
                pl.when(source > place)(functools.partial(step, wide, products, rotation))
        if last:
            for group in range(geo.groups):
                at = slice(group * geo.tile_h, (group + 1) * geo.tile_h)
                outs[0][group] = (accum[0, at, :] * natural).astype(jnp.bfloat16)
                outs[1][group] = accum[1, at, :].astype(jnp.bfloat16)

    ins = [x for slot in slots for x in slot] + list(stats)
    ins += [] if state is None else [state]
    running = (2, tokens, width)
    shapes = [jax.ShapeDtypeStruct(running, jnp.float32)]
    if last:
        shapes = [jax.ShapeDtypeStruct((geo.groups, geo.tile_h, width), jnp.bfloat16)] * 2
    return call(
        kernel,
        "key_grads",
        [whole()] * len(ins),
        [whole()] * len(shapes),
        shapes,
        ([pltpu.VMEM(running, jnp.float32)] if last else [])
        + [pltpu.VMEM((len(stats), stat_rows, wide_rows), jnp.float32)],
        8,
        2,
    )(*ins)


def rotate(x, by, blocks):
    return lax.ppermute(x, "span", [(i, (i + by) % blocks) for i in range(blocks)])


def shards(queries, cache_keys, cache_values, grad_attended, radius, frame_count, sizes):
    blocks, count_h, count_w = sizes
    frames, tile_h, tile_w, width = queries.shape[1:]
    heads = radius.shape[0]
    geo = Geometry(frames, tile_h, tile_w, count_h, count_w)
    small = (radius, frame_count)

    def grouped(x):
        return jnp.transpose(x[0], (0, 2, 1, 3)).reshape(geo.groups, tile_h, width)

    def restored(x):
        x = x.reshape(frames, tile_w, tile_h, width)
        return jnp.transpose(x, (0, 2, 1, 3))[None]

    arrays = [grouped(x) for x in (cache_keys, cache_values, queries, grad_attended)]
    own, *chains = tidy(geo, arrays, blocks)
    batches = relay(blocks)
    needed = {step for steps, _, _ in batches for step in steps}
    sources = [list(range(blocks))] + [blks for _, _, blks in batches]
    moved = {}

    def hop(chain, number, after):
        if any(c == chain and n >= number for c, n in needed):
            x = chains[chain]
            x = lax.optimization_barrier((x, *after))[0] if after else x
            pairs = list(enumerate(swap(blocks, chain, number)))
            moved[chain, number] = chains[chain] = lax.ppermute(x, "span", pairs)

    def take(n, after):
        steps, which, _ = batches[n - 1]
        group = ([moved[step] for step in steps], which, 0)
        (x,), (messages,) = pack_rows(geo, [group], after, n == blocks - 1)
        return x, messages

    hop(0, 1, [])
    hop(1, 1, [])
    xs, (messages, asked) = pack_rows(geo, [([own], None, 0), ([own], None, 2)], [])
    x, pieces = own, geo.exchange_rows(messages)
    slots, state = [], None
    for n in range(blocks):
        last = n == blocks - 1
        after = []
        if n == 0 or not last:
            before = [] if n == 0 else [state[0]] if n == 1 else [state[0], asked[0]]
            messages = pack_cols(geo, [x], [0], [pieces], before)
            ready = list(messages[:1])
            pieces = pieces + geo.exchange_cols(messages)
        parts = [x] + pieces
        if n == 0:
            asked = geo.exchange_rows(lax.optimization_barrier((*asked, *ready))[:-1])
        if not last:
            hop(0, n + 2, [state[0]] if state else ready)
            x, messages = take(n + 1, ready)
            after = list(messages[:1])
            hop(1, n + 2, after)
        if n == min(1, blocks - 1):
            cols = geo.exchange_cols(pack_cols(geo, [own], [2], [asked], after))
            asked = [own] + asked + cols
            asked = lay_out(geo, heads, small, own, asked, [2] + [0] * len(asked[1:]))
        if not last:
            exchange = geo.exchange_all if n == blocks - 2 else geo.exchange_rows
            pieces = exchange(messages)
        wide, products, *state = forward(
            geo, heads, small, own, sources[n], parts, [0] * len(parts), state, last, after
        )
        slots.append([wide, products])
    attended, lse, delta, packed = state

    grad_q, token = query_grads(geo, heads, lse, delta, sources, slots)
    brought = geo.exchange_all([packed] * len(geo.places))
    own_stats = merge(geo, [packed] + brought, [token])
    stats = [rotate(own_stats, n, blocks) for n in range(1, blocks)]
    begun = key_grads(geo, blocks, heads, [own_stats], sources[:1], [asked], None, False)[0]
    grad_k, grad_v = key_grads(
        geo, blocks, heads, stats, sources[1:], slots[1:], begun, True
    )
    return tuple(restored(x) for x in (attended, grad_q, grad_k, grad_v))


def solution(mesh):
    placed = P("span", None, "ha", "wa", None)
    sizes = tuple(mesh.shape[name] for name in ("span", "ha", "wa"))
    return jax.shard_map(
        functools.partial(shards, sizes=sizes),
        mesh=mesh,
        in_specs=(placed,) * 4 + (P(), P()),
        out_specs=(placed,) * 4,
        check_vma=False,
    )
```

```python
import functools
import math

import jax
import jax.numpy as jnp
import ml_dtypes
import numpy as np
from jax import lax
from jax.experimental import pallas as pl
from jax.experimental.pallas import tpu as pltpu
from jax.sharding import PartitionSpec as P

RMAX = 2
FAR = 99.0
LOG2E = math.log2(math.e)
LANES = 128


def round_up(value, unit):
    return (value + unit - 1) // unit * unit


def dot_nt(a, b):
    return lax.dot_general(a, b, (((1,), (1,)), ((), ())), preferred_element_type=jnp.float32)


def dot_nn(a, b):
    return lax.dot_general(a, b, (((1,), (0,)), ((), ())), preferred_element_type=jnp.float32)


class Side:
    def __init__(self, kind, count, tile, variant):
        self.count = count
        self.swap = kind == "swap"
        if kind == "same":
            self.delta, self.start, self.length, self.send_start = 0, 0, tile, 0
        else:
            self.delta = 1 - 2 * variant if self.swap else kind
            send_up = (variant == 0) if self.swap else (kind < 0)
            self.length = RMAX
            self.start = tile if self.delta > 0 else -RMAX
            self.send_start = tile - RMAX if send_up else 0
        shift = 1 if self.swap else self.delta
        self.pairs = [((i + shift) % count, i) for i in range(count)]

    def place(self, index):
        delta = 1 - 2 * index if self.swap else self.delta
        other = index + delta
        inside = (other >= 0) & (other < self.count)
        return jnp.where(inside, other, index), inside


def sides(count, tile, variant):
    kinds = [] if count == 1 else ["swap"] if count == 2 else [-1, 1]
    return [Side(kind, count, tile, variant) for kind in ["same"] + kinds]


class Geometry:
    def __init__(self, frames, tile_h, tile_w, count_h, count_w):
        self.frames, self.tile_h, self.tile_w = frames, tile_h, tile_w
        self.count_h, self.count_w = count_h, count_w
        self.tokens = frames * tile_h * tile_w
        self.groups = frames * tile_w
        self.variants_h = 2 if count_h == 2 else 1
        self.variants_w = 2 if count_w == 2 else 1
        found = [
            self.variant(variant_h, variant_w)
            for variant_h in range(self.variants_h)
            for variant_w in range(self.variants_w)
        ]
        direct, tall, gap = (np.stack(arrays) for arrays in zip(*found))
        own = np.arange(self.tokens)
        starts = [start for start, *_ in self.ranges] + [self.used]
        self.places = [(a, b - a) for a, b in zip(starts, starts[1:])][1:]
        self.all_select = self.one_hot(direct[:, self.tokens : self.used], self.tokens)
        self.row_select = self.one_hot(direct[:, self.tokens : self.tall], self.tokens)
        self.col_select = self.one_hot(tall[:, self.tall : self.used], self.tall)
        self.select = self.one_hot(direct, self.tokens)
        self.gap = gap.astype(np.float32)
        assert (direct[:, : self.tokens] == own).all()

    def one_hot(self, index, count):
        return (index[..., None] == np.arange(count)).astype(ml_dtypes.bfloat16)

    def variant(self, variant_h, variant_w):
        row_own, *rows_of = sides(self.count_h, self.tile_h, variant_h)
        col_own, *cols_of = sides(self.count_w, self.tile_w, variant_w)
        self.row_sides, self.col_sides = rows_of, cols_of
        direct, tall, rows, cols, frame = [], [], [], [], []
        self.ranges = []

        def add(row, col, base):
            ff, xx, yy = np.unravel_index(
                np.arange(self.frames * col.length * row.length),
                (self.frames, col.length, row.length),
            )
            start = len(direct)
            own_x, own_y = col.send_start + xx, row.send_start + yy
            direct.extend((ff * self.tile_w + own_x) * self.tile_h + own_y)
            tall.extend(base + (ff * self.tile_w + own_x) * row.length + yy)
            rows.extend(row.start + yy)
            cols.extend(col.start + xx)
            frame.extend(ff)
            self.ranges.append((start, len(direct), row, col))

        def pad(unit):
            count = round_up(len(direct), unit) - len(direct)
            for array, value in zip((direct, tall, rows, cols, frame), (-1, -1, 1000, 1000, 0)):
                array.extend([value] * count)

        add(row_own, col_own, 0)
        bases = []
        self.row_places, self.col_places = [], []
        for row in rows_of:
            bases.append(len(direct))
            add(row, col_own, bases[-1])
            pad(16)
            self.row_places.append((bases[-1], len(direct) - bases[-1]))
        self.tall = len(direct)
        for col in cols_of:
            start = len(direct)
            for row, base in zip([row_own] + rows_of, [0] + bases):
                add(row, col, base)
                pad(16)
            self.col_places.append((start, len(direct) - start))
        self.used = len(direct)
        pad(LANES)
        self.wide = len(direct)
        self.frame = np.array(frame, np.int32)
        rows, cols = np.array(rows), np.array(cols)
        mine = slice(0, self.tokens)
        gap = np.maximum(
            np.abs(rows[mine][:, None] - rows[None, :]), np.abs(cols[mine][:, None] - cols[None, :])
        )
        return np.array(direct), np.array(tall), np.minimum(gap, FAR)

    def which(self):
        at_h = lax.axis_index("ha") if self.variants_h == 2 else 0
        at_w = lax.axis_index("wa") if self.variants_w == 2 else 0
        return at_h * self.variants_w + at_w

    def near(self, gap_ref):
        lane = lax.broadcasted_iota(jnp.int32, (1, self.wide), 1)
        far = jnp.zeros((1, self.wide), jnp.float32)
        for start, end, row, col in self.ranges[1:]:
            inside = row.place(lax.axis_index("ha"))[1] & col.place(lax.axis_index("wa"))[1]
            cost = jnp.where(inside, 0.0, FAR)
            far = jnp.where((lane >= start) & (lane < end), cost, far)
        return gap_ref[self.which()] + far

    def permute(self, row, col, x):
        pairs = [
            (a * self.count_w + c, b * self.count_w + d)
            for a, b in row.pairs
            for c, d in col.pairs
        ]
        return lax.ppermute(x, ("ha", "wa"), pairs)

    def exchange_rows(self, messages):
        own = self.ranges[0][3]
        return [self.permute(row, own, x) for row, x in zip(self.row_sides, messages)]

    def exchange_cols(self, messages):
        own = self.ranges[0][2]
        return [self.permute(own, col, x) for col, x in zip(self.col_sides, messages)]

    def exchange_all(self, messages):
        return [self.permute(row, col, x) for x, (_, _, row, col) in zip(messages, self.ranges[1:])]


def whole(memory=pltpu.VMEM):
    return pl.BlockSpec(memory_space=memory)


def call(kernel, name, in_specs, out_specs, out_shape, scratch, mib, cost, aliases=None):
    return pl.pallas_call(
        kernel,
        in_specs=in_specs,
        out_specs=out_specs,
        out_shape=out_shape,
        scratch_shapes=scratch,
        compiler_params=pltpu.CompilerParams(vmem_limit_bytes=mib * 1024 * 1024),
        cost_estimate=pl.CostEstimate(
            flops=int(cost * 1e9), bytes_accessed=int(cost * 2e6), transcendentals=0
        ),
        input_output_aliases=aliases or {},
        name=name,
    )


def pick(table, place):
    value = jnp.int32(table[0])
    for index, entry in enumerate(table[1:], 1):
        if entry != table[0]:
            value = jnp.where(place == index, entry, value)
    return value


def relay(blocks):
    held = [[(s, (s % 2 == 0) != bool(chain)) for s in range(blocks)] for chain in range(2)]
    fresh = [[] for _ in range(blocks)]
    for number in range(1, blocks):
        for chain in range(2):
            moved = [held[chain][a] for a in swap(blocks, chain, number)]
            held[chain] = moved
            for s, (block, keys) in enumerate(moved):
                if block != s and keys == (block < s) and block not in [b for _, b in fresh[s]]:
                    fresh[s].append(((chain, number), block))
    batches = []
    for n in range(blocks - 1):
        steps = sorted({fresh[s][n][0] for s in range(blocks)}, key=lambda step: step[::-1])
        which = [steps.index(fresh[s][n][0]) for s in range(blocks)]
        batches.append((steps, which, [fresh[s][n][1] for s in range(blocks)]))
    return batches


def swap(blocks, chain, number):
    start = (chain + number + 1) % 2
    partner = list(range(blocks))
    for low in range(start, blocks - 1, 2):
        partner[low], partner[low + 1] = low + 1, low
    return partner


def tidy(geo, arrays, blocks):
    width = arrays[0].shape[-1]
    tokens, tile_h = geo.tokens, geo.tile_h

    def kernel(*refs):
        ins, (own_ref, even_ref, odd_ref, stage, sems) = refs[:4], refs[4:]
        copies = [
            pltpu.make_async_copy(ref, stage.at[number], sems.at[number])
            for number, ref in enumerate(ins)
        ]
        for copy in copies:
            copy.start()
        for number, copy in enumerate(copies):
            copy.wait()
            for group in range(geo.groups):
                own_ref[number, group * tile_h : (group + 1) * tile_h, :] = stage[number, group]
        odd = lax.rem(lax.axis_index("span"), 2)
        even_ref[...] = own_ref[pl.ds(2 * odd, 2)]
        odd_ref[...] = own_ref[pl.ds(2 - 2 * odd, 2)]

    pair = jax.ShapeDtypeStruct((2, tokens, width), jnp.bfloat16)
    return call(
        kernel,
        "tidy",
        [whole(pltpu.HBM)] * 4,
        [whole()] * 3,
        [jax.ShapeDtypeStruct((4, tokens, width), jnp.bfloat16), pair, pair],
        [
            pltpu.VMEM((4, geo.groups, tile_h, width), jnp.bfloat16),
            pltpu.SemaphoreType.DMA((4,)),
        ],
        60,
        2,
    )(*arrays)


def pack_rows(geo, groups, after, every=False):
    places = geo.places if every else geo.row_places
    select = geo.all_select if every else geo.row_select
    ins = [x for candidates, _, _ in groups for x in candidates]
    _, tokens, width = ins[0].shape
    several = [len(candidates) > 1 for candidates, _, _ in groups]

    def kernel(select_ref, *refs):
        refs, outs = refs[: len(ins)], list(refs[len(ins) + len(after) :])
        chosen = select_ref[geo.which()]
        kept = [outs.pop(0) if many else None for many in several]
        place = lax.axis_index("span")

        def work(x_ref, first, pair):
            for a in range(2):
                x = x_ref[first + a]
                if kept[pair] is not None:
                    kept[pair][a] = x
                picked = dot_nn(chosen, x).astype(jnp.bfloat16)
                for out, (start, size) in zip(outs[pair * len(places) :], places):
                    out[a] = picked[start - tokens : start - tokens + size]

        at = 0
        for pair, (candidates, which, first) in enumerate(groups):
            for index in range(len(candidates)):
                job = functools.partial(work, refs[at + index], first, pair)
                if several[pair]:
                    pl.when(pick(which, place) == index)(job)
                else:
                    job()
            at += len(candidates)

    shapes = [jax.ShapeDtypeStruct((2, tokens, width), jnp.bfloat16)] * sum(several)
    shapes += [
        jax.ShapeDtypeStruct((2, size, width), jnp.bfloat16) for _, size in places * len(groups)
    ]
    out = list(
        call(
            kernel,
            "pack_rows",
            [whole()] * (1 + len(ins)) + [whole(pl.ANY)] * len(after),
            [whole()] * len(shapes),
            shapes,
            [],
            12,
            0.2,
        )(select, *ins, *after)
    )
    xs = [out.pop(0) if many else group[0][0] for many, group in zip(several, groups)]
    return xs, [out[n * len(places) : (n + 1) * len(places)] for n in range(len(groups))]


def pack_cols(geo, xs, firsts, rows, after):
    count, sides = 2 * len(xs), len(rows[0])
    rows = [piece for pair in rows for piece in pair]
    _, tokens, width = xs[0].shape

    def kernel(select_ref, *refs):
        x_refs, refs = refs[: len(xs)], refs[len(xs) :]
        row_refs, refs = refs[: len(rows)], refs[len(rows) + len(after) :]
        outs, tall = refs[:-1], refs[-1]
        chosen = select_ref[geo.which()]
        for a in range(count):
            tall[a, :tokens] = x_refs[a // 2][firsts[a // 2] + a % 2]
            for ref, (start, size) in zip(row_refs[a // 2 * sides :], geo.row_places):
                tall[a, start : start + size] = ref[a % 2]
            picked = dot_nn(chosen, tall[a]).astype(jnp.bfloat16)
            for out, (start, size) in zip(outs, geo.col_places):
                out[a] = picked[start - geo.tall : start - geo.tall + size]

    return call(
        kernel,
        "pack_cols",
        [whole()] * (1 + len(xs) + len(rows)) + [whole(pl.ANY)] * len(after),
        [whole()] * len(geo.col_places),
        [jax.ShapeDtypeStruct((count, size, width), jnp.bfloat16) for _, size in geo.col_places],
        [pltpu.VMEM((count, geo.tall, width), jnp.bfloat16)],
        12,
        0.2,
    )(geo.col_select, *xs, *rows, *after)


def set_bias(bias_ref, gap):
    for reach in range(1, RMAX + 1):
        bias_ref[reach - 1] = jnp.where(gap <= reach, 0.0, -jnp.inf)


def fit(x, lanes):
    return x if x.shape[1] == lanes else jnp.broadcast_to(x[:, :1], (x.shape[0], lanes))


def repeat(x, lanes):
    return jnp.concatenate([x] * (lanes // LANES), axis=1)


def spread(geo, parts, bases, wide):
    places = geo.row_places + geo.col_places
    if len(parts) > 1 + len(places):
        places = geo.places
    for a in range(2):
        for ref, base, (start, size) in zip(parts, bases, [(0, geo.tokens)] + places):
            wide[a, start : start + size] = ref[base + a]
        if geo.wide > geo.used:
            wide[a, geo.used :] = jnp.zeros((geo.wide - geo.used, wide.shape[-1]), jnp.bfloat16)


def lay_out(geo, heads, small, own, parts, bases):
    tokens, wide_rows = geo.tokens, geo.wide
    width = own.shape[-1]
    depth = width // heads
    scale = LOG2E / math.sqrt(depth)

    def kernel(radius_ref, live_ref, gap_ref, row_frame_ref, own_ref, *refs):
        parts_refs, (wide, products, bias_ref) = refs[: len(parts)], refs[len(parts) :]
        spread(geo, parts_refs, bases, wide)
        live = row_frame_ref[...] < live_ref[lax.axis_index("span")]
        set_bias(bias_ref, jnp.where(live, geo.near(gap_ref), FAR))
        for h in range(heads):
            lanes = slice(h * depth, (h + 1) * depth)
            score = dot_nt(own_ref[0, :, lanes], wide[0, :, lanes])
            products[0, h] = score * scale + bias_ref[radius_ref[h] - 1]
            products[1, h] = dot_nt(own_ref[1, :, lanes], wide[1, :, lanes])

    return call(
        kernel,
        "lay_out",
        [whole(pltpu.SMEM)] * 2 + [whole()] * (3 + len(parts)),
        [whole()] * 2,
        [
            jax.ShapeDtypeStruct((2, wide_rows, width), jnp.bfloat16),
            jax.ShapeDtypeStruct((2, heads, tokens, wide_rows), jnp.float32),
        ],
        [pltpu.VMEM((RMAX, tokens, wide_rows), jnp.float32)],
        16,
        0.5,
    )(*small, geo.gap, geo.frame[:tokens, None], own, *parts)


def forward(geo, heads, small, own, sources, parts, bases, state, last, after):
    tokens, wide_rows = geo.tokens, geo.wide
    width = own.shape[-1]
    depth = width // heads
    scale = LOG2E / math.sqrt(depth)
    per = len(parts)
    stat_rows = round_up(2 * heads, 8)
    first = state is None
    lanes = [slice(h * depth, (h + 1) * depth) for h in range(heads)]

    def kernel(
        radius_ref, live_ref, gap_ref, frame_ref, row_frame_ref, select_ref, own_ref, *refs
    ):
        parts_refs, refs = refs[:per], refs[per:]
        state_in, refs = (None, refs) if first else (refs[:3], refs[3:])
        wide, products, *refs = refs[len(after) :]
        if last:
            outs, (accum, top, total, bias_ref) = refs[:4], refs[4:]
        else:
            accum, top, total, bias_ref = refs
        place = lax.axis_index("span")
        source = place if first else pick(sources, place)
        active = source <= place

        spread(geo, parts_refs, bases, wide)
        if first:
            accum[...] = jnp.zeros(accum.shape, jnp.float32)
            top[...] = jnp.full(top.shape, -jnp.inf, jnp.float32)
            total[...] = jnp.zeros(total.shape, jnp.float32)
        else:
            for old, new in zip(state_in, (accum, top, total)):
                new[...] = old[...]

        def multiply(h, base):
            score = dot_nt(own_ref[base, :, lanes[h]], wide[0, :, lanes[h]])
            score = score * scale + bias_ref[radius_ref[h] - 1]
            products[0, h] = score
            products[1, h] = dot_nt(own_ref[base + 1, :, lanes[h]], wide[1, :, lanes[h]])
            return score

        def attend():
            live = frame_ref[...] < live_ref[source]
            set_bias(bias_ref, jnp.where(live, geo.near(gap_ref), FAR))
            ones = jnp.ones((wide_rows, LANES), jnp.bfloat16)
            ahead = multiply(0, 2)
            for h in range(heads):
                score = ahead
                if h + 1 < heads:
                    ahead = multiply(h + 1, 2)
                best = jnp.max(score, axis=1, keepdims=True)
                new_top = jnp.maximum(top[h], best)
                fading = jnp.exp2(top[h] - new_top)
                top[h] = new_top
                weight = jnp.exp2(score - repeat(new_top, wide_rows)).astype(jnp.bfloat16)
                value = jnp.concatenate([wide[1, :, lanes[h]], ones], axis=1)
                both = dot_nn(weight, value)
                accum[:, lanes[h]] = accum[:, lanes[h]] * fit(fading, depth) + both[:, :depth]
                total[h] = total[h] * fading + both[:, depth:]

        def keep():
            live = row_frame_ref[...] < live_ref[place]
            set_bias(bias_ref, jnp.where(live, geo.near(gap_ref), FAR))
            for h in range(heads):
                multiply(h, 0)

        def finish():
            attended_ref, lse_ref, delta_ref, packed_ref = outs
            lane = lax.broadcasted_iota(jnp.int32, (tokens, LANES), 1)
            column = jnp.zeros((tokens, LANES), jnp.float32)
            for h in range(heads):
                rounded = (accum[:, lanes[h]] / fit(total[h], depth)).astype(jnp.bfloat16)
                rounded = rounded.astype(jnp.float32)
                accum[:, lanes[h]] = rounded
                lse = top[h] + jnp.log2(total[h])
                grad = own_ref[3, :, lanes[h]].astype(jnp.float32)
                delta = jnp.sum(rounded * grad, axis=1, keepdims=True)
                delta = jnp.broadcast_to(delta, (tokens, LANES))
                lse_ref[h] = lse
                delta_ref[h] = delta
                column = jnp.where(lane == h, lse, column)
                column = jnp.where(lane == heads + h, delta, column)
            packed = jnp.zeros((wide_rows, LANES), jnp.float32)
            rest = column
            chosen = select_ref[geo.which()]
            for _ in range(3):
                part = rest.astype(jnp.bfloat16)
                rest = rest - part.astype(jnp.float32)
                packed = packed + dot_nn(chosen, part)
            packed_ref[...] = jnp.transpose(packed)[:stat_rows]
            for group in range(geo.groups):
                at = slice(group * geo.tile_h, (group + 1) * geo.tile_h)
                attended_ref[group] = accum[at, :].astype(jnp.bfloat16)

        if first:
            attend()
        else:
            pl.when(active)(attend)
            pl.when(jnp.logical_not(active))(keep)
        if last:
            finish()

    ins = [*small, geo.gap, geo.frame[None, :], geo.frame[:tokens, None], geo.select, own, *parts]
    ins += [] if first else list(state)
    stat = (heads, tokens, LANES)
    running = [(tokens, width), stat, stat]
    shapes = [
        jax.ShapeDtypeStruct((2, wide_rows, width), jnp.bfloat16),
        jax.ShapeDtypeStruct((2, heads, tokens, wide_rows), jnp.float32),
    ]
    scratch = []
    if last:
        shapes += [
            jax.ShapeDtypeStruct((geo.groups, geo.tile_h, width), jnp.bfloat16),
            jax.ShapeDtypeStruct(stat, jnp.float32),
            jax.ShapeDtypeStruct(stat, jnp.float32),
            jax.ShapeDtypeStruct((stat_rows, wide_rows), jnp.float32),
        ]
        scratch += [pltpu.VMEM(shape, jnp.float32) for shape in running]
    else:
        shapes += [jax.ShapeDtypeStruct(shape, jnp.float32) for shape in running]
    return call(
        kernel,
        "forward",
        [whole(pltpu.SMEM)] * 2 + [whole()] * (len(ins) - 2) + [whole(pl.ANY)] * len(after),
        [whole()] * len(shapes),
        shapes,
        scratch + [pltpu.VMEM((RMAX, tokens, wide_rows), jnp.float32)],
        20,
        1.5,
    )(*ins, *after)


def merge(geo, pieces, after):
    def kernel(*refs):
        out = refs[-1]
        row = refs[0][...]
        lane = lax.broadcasted_iota(jnp.int32, row.shape, 1)
        for ref, (start, *_) in zip(refs[1:], geo.ranges[1:]):
            row = jnp.where(lane >= start, ref[...], row)
        out[...] = row

    return call(
        kernel,
        "merge",
        [whole()] * len(pieces) + [whole(pl.ANY)] * len(after),
        whole(),
        jax.ShapeDtypeStruct(pieces[0].shape, jnp.float32),
        [],
        4,
        0.1,
    )(*pieces, *after)


def query_grads(geo, heads, lse, delta, sources, slots):
    tokens, wide_rows = geo.tokens, geo.wide
    width = slots[0][0].shape[-1]
    depth = width // heads
    natural = 1.0 / math.sqrt(depth)
    lanes = [slice(h * depth, (h + 1) * depth) for h in range(heads)]

    def kernel(lse_ref, delta_ref, *refs):
        slot_refs, (out, token, accum) = refs[: 2 * len(slots)], refs[2 * len(slots) :]
        token[...] = jnp.zeros(token.shape, jnp.float32)
        place = lax.axis_index("span")

        def step(wide, products, first):
            for h in range(heads):
                prob = jnp.exp2(products[0, h] - repeat(lse_ref[h], wide_rows))
                slope = prob * (products[1, h] - repeat(delta_ref[h], wide_rows))
                part = dot_nn(slope.astype(jnp.bfloat16), wide[0, :, lanes[h]])
                accum[:, lanes[h]] = part if first else accum[:, lanes[h]] + part

        for n, table in enumerate(sources):
            work = functools.partial(step, slot_refs[2 * n], slot_refs[2 * n + 1], n == 0)
            if n == 0:
                work()
            else:
                pl.when(pick(table, place) < place)(work)
        for group in range(geo.groups):
            at = slice(group * geo.tile_h, (group + 1) * geo.tile_h)
            out[group] = (accum[at, :] * natural).astype(jnp.bfloat16)

    flat = [x for slot in slots for x in slot]
    return call(
        kernel,
        "query_grads",
        [whole()] * (2 + len(flat)),
        [whole()] * 2,
        [
            jax.ShapeDtypeStruct((geo.groups, geo.tile_h, width), jnp.bfloat16),
            jax.ShapeDtypeStruct((8, LANES), jnp.float32),
        ],
        [pltpu.VMEM((tokens, width), jnp.float32)],
        8,
        2,
    )(lse, delta, *flat)


def key_grads(geo, blocks, heads, stats, sources, slots, state, last):
    tokens, wide_rows = geo.tokens, geo.wide
    width = slots[0][0].shape[-1]
    depth = width // heads
    natural = 1.0 / math.sqrt(depth)
    lanes = [slice(h * depth, (h + 1) * depth) for h in range(heads)]

    def kernel(*refs):
        slot_refs, refs = refs[: 2 * len(slots)], refs[2 * len(slots) :]
        rows, refs = refs[0], refs[1:]
        state_in, refs = (None, refs) if state is None else (refs[0], refs[1:])
        outs, refs = (refs[:2], refs[2:]) if last else (None, refs)
        (accum,) = refs
        place = lax.axis_index("span")
        accum[...] = jnp.zeros(accum.shape, jnp.float32) if state is None else state_in[...]

        def step(wide, products, block):
            for h in range(heads):
                prob = jnp.exp2(products[0, h] - rows[block, h : h + 1, :])
                accum[1, :, lanes[h]] += dot_nn(prob.astype(jnp.bfloat16), wide[1, :, lanes[h]])
                slope = prob * (products[1, h] - rows[block, heads + h : heads + h + 1, :])
                accum[0, :, lanes[h]] += dot_nn(slope.astype(jnp.bfloat16), wide[0, :, lanes[h]])

        for n, table in enumerate(sources):
            wide, products = slot_refs[2 * n : 2 * n + 2]
            if table == list(range(blocks)):
                step(wide, products, 0)
            else:
                source = pick(table, place)
                pl.when(source > place)(functools.partial(step, wide, products, source))
        if last:
            for group in range(geo.groups):
                at = slice(group * geo.tile_h, (group + 1) * geo.tile_h)
                outs[0][group] = (accum[0, at, :] * natural).astype(jnp.bfloat16)
                outs[1][group] = accum[1, at, :].astype(jnp.bfloat16)

    ins = [x for slot in slots for x in slot] + [stats]
    ins += [] if state is None else [state]
    running = (2, tokens, width)
    shapes = [jax.ShapeDtypeStruct(running, jnp.float32)]
    if last:
        shapes = [jax.ShapeDtypeStruct((geo.groups, geo.tile_h, width), jnp.bfloat16)] * 2
    return call(
        kernel,
        "key_grads",
        [whole()] * len(ins),
        [whole()] * len(shapes),
        shapes,
        [pltpu.VMEM(running, jnp.float32)] if last else [],
        8,
        2,
    )(*ins)


def shards(queries, cache_keys, cache_values, grad_attended, radius, frame_count, sizes):
    blocks, count_h, count_w = sizes
    frames, tile_h, tile_w, width = queries.shape[1:]
    heads = radius.shape[0]
    geo = Geometry(frames, tile_h, tile_w, count_h, count_w)
    small = (radius, frame_count)

    def grouped(x):
        return jnp.transpose(x[0], (0, 2, 1, 3)).reshape(geo.groups, tile_h, width)

    def restored(x):
        x = x.reshape(frames, tile_w, tile_h, width)
        return jnp.transpose(x, (0, 2, 1, 3))[None]

    arrays = [grouped(x) for x in (cache_keys, cache_values, queries, grad_attended)]
    own, *chains = tidy(geo, arrays, blocks)
    batches = relay(blocks)
    needed = {step for steps, _, _ in batches for step in steps}
    sources = [list(range(blocks))] + [blks for _, _, blks in batches]
    moved = {}

    def hop(chain, number, after):
        if any(c == chain and n >= number for c, n in needed):
            x = chains[chain]
            x = lax.optimization_barrier((x, *after))[0] if after else x
            pairs = list(enumerate(swap(blocks, chain, number)))
            moved[chain, number] = chains[chain] = lax.ppermute(x, "span", pairs)

    def take(n, after):
        steps, which, _ = batches[n - 1]
        group = ([moved[step] for step in steps], which, 0)
        (x,), (messages,) = pack_rows(geo, [group], after, n == blocks - 1)
        return x, messages

    hop(0, 1, [])
    hop(1, 1, [])
    xs, (messages, asked) = pack_rows(geo, [([own], None, 0), ([own], None, 2)], [])
    x, pieces = own, geo.exchange_rows(messages)
    slots, state = [], None
    for n in range(blocks):
        last = n == blocks - 1
        after = []
        if n == 0 or not last:
            before = [] if n == 0 else [state[0]] if n == 1 else [state[0], asked[0]]
            messages = pack_cols(geo, [x], [0], [pieces], before)
            ready = list(messages[:1])
            pieces = pieces + geo.exchange_cols(messages)
        parts = [x] + pieces
        if n == 0:
            asked = geo.exchange_rows(lax.optimization_barrier((*asked, *ready))[:-1])
        if not last:
            hop(0, n + 2, [state[0]] if state else ready)
            x, messages = take(n + 1, ready)
            after = list(messages[:1])
            hop(1, n + 2, after)
        if n == min(1, blocks - 1):
            cols = geo.exchange_cols(pack_cols(geo, [own], [2], [asked], after))
            asked = [own] + asked + cols
            asked = lay_out(geo, heads, small, own, asked, [2] + [0] * len(asked[1:]))
        if not last:
            if n == blocks - 2:
                corner = [r.length != tile_h and c.length != tile_w for _, _, r, c in geo.ranges[1:]]
                late = lax.optimization_barrier(
                    (*[m for m, flag in zip(messages, corner) if flag], parts[-1])
                )
                late = iter(late[:-1])
                messages = [next(late) if flag else m for m, flag in zip(messages, corner)]
                pieces = geo.exchange_all(messages)
            else:
                pieces = geo.exchange_rows(messages)
        wide, products, *state = forward(
            geo, heads, small, own, sources[n], parts, [0] * len(parts), state, last, after
        )
        slots.append([wide, products])
    attended, lse, delta, packed = state

    grad_q, token = query_grads(geo, heads, lse, delta, sources, slots)
    brought = geo.exchange_all([packed] * len(geo.places))
    own_stats = merge(geo, [packed] + brought, [token])
    stats = lax.all_gather(own_stats, "span")
    begun = key_grads(geo, blocks, heads, own_stats[None], sources[:1], [asked], None, False)[0]
    grad_k, grad_v = key_grads(
        geo, blocks, heads, stats, sources[1:], slots[1:], begun, True
    )
    return tuple(restored(x) for x in (attended, grad_q, grad_k, grad_v))


def solution(mesh):
    placed = P("span", None, "ha", "wa", None)
    sizes = tuple(mesh.shape[name] for name in ("span", "ha", "wa"))
    return jax.shard_map(
        functools.partial(shards, sizes=sizes),
        mesh=mesh,
        in_specs=(placed,) * 4 + (P(), P()),
        out_specs=(placed,) * 4,
        check_vma=False,
    )
```

```python
import functools
import math

import jax
import jax.numpy as jnp
import ml_dtypes
import numpy as np
from jax import lax
from jax.experimental import pallas as pl
from jax.experimental.pallas import tpu as pltpu
from jax.sharding import PartitionSpec as P

RMAX = 2
FAR = 99.0
LOG2E = math.log2(math.e)
LANES = 128


def round_up(value, unit):
    return (value + unit - 1) // unit * unit


def dot_nt(a, b):
    return lax.dot_general(a, b, (((1,), (1,)), ((), ())), preferred_element_type=jnp.float32)


def dot_nn(a, b):
    return lax.dot_general(a, b, (((1,), (0,)), ((), ())), preferred_element_type=jnp.float32)


class Side:
    def __init__(self, kind, count, tile, variant):
        self.count = count
        self.swap = kind == "swap"
        if kind == "same":
            self.delta, self.start, self.length, self.send_start = 0, 0, tile, 0
        else:
            self.delta = 1 - 2 * variant if self.swap else kind
            send_up = (variant == 0) if self.swap else (kind < 0)
            self.length = RMAX
            self.start = tile if self.delta > 0 else -RMAX
            self.send_start = tile - RMAX if send_up else 0
        shift = 1 if self.swap else self.delta
        self.pairs = [((i + shift) % count, i) for i in range(count)]

    def place(self, index):
        delta = 1 - 2 * index if self.swap else self.delta
        other = index + delta
        inside = (other >= 0) & (other < self.count)
        return jnp.where(inside, other, index), inside


def sides(count, tile, variant):
    kinds = [] if count == 1 else ["swap"] if count == 2 else [-1, 1]
    return [Side(kind, count, tile, variant) for kind in ["same"] + kinds]


class Geometry:
    def __init__(self, frames, tile_h, tile_w, count_h, count_w):
        self.frames, self.tile_h, self.tile_w = frames, tile_h, tile_w
        self.count_h, self.count_w = count_h, count_w
        self.tokens = frames * tile_h * tile_w
        self.groups = frames * tile_w
        self.variants_h = 2 if count_h == 2 else 1
        self.variants_w = 2 if count_w == 2 else 1
        found = [
            self.variant(variant_h, variant_w)
            for variant_h in range(self.variants_h)
            for variant_w in range(self.variants_w)
        ]
        direct, tall, gap = (np.stack(arrays) for arrays in zip(*found))
        own = np.arange(self.tokens)
        starts = [start for start, *_ in self.ranges] + [self.used]
        self.places = [(a, b - a) for a, b in zip(starts, starts[1:])][1:]
        self.all_select = self.one_hot(direct[:, self.tokens : self.used], self.tokens)
        self.row_select = self.one_hot(direct[:, self.tokens : self.tall], self.tokens)
        self.col_select = self.one_hot(tall[:, self.tall : self.used], self.tall)
        self.select = self.one_hot(direct, self.tokens)
        self.gap = gap.astype(np.float32)
        assert (direct[:, : self.tokens] == own).all()

    def one_hot(self, index, count):
        return (index[..., None] == np.arange(count)).astype(ml_dtypes.bfloat16)

    def variant(self, variant_h, variant_w):
        row_own, *rows_of = sides(self.count_h, self.tile_h, variant_h)
        col_own, *cols_of = sides(self.count_w, self.tile_w, variant_w)
        self.row_sides, self.col_sides = rows_of, cols_of
        direct, tall, rows, cols, frame = [], [], [], [], []
        self.ranges = []

        def add(row, col, base):
            ff, xx, yy = np.unravel_index(
                np.arange(self.frames * col.length * row.length),
                (self.frames, col.length, row.length),
            )
            start = len(direct)
            own_x, own_y = col.send_start + xx, row.send_start + yy
            direct.extend((ff * self.tile_w + own_x) * self.tile_h + own_y)
            tall.extend(base + (ff * self.tile_w + own_x) * row.length + yy)
            rows.extend(row.start + yy)
            cols.extend(col.start + xx)
            frame.extend(ff)
            self.ranges.append((start, len(direct), row, col))

        def pad(unit):
            count = round_up(len(direct), unit) - len(direct)
            for array, value in zip((direct, tall, rows, cols, frame), (-1, -1, 1000, 1000, 0)):
                array.extend([value] * count)

        add(row_own, col_own, 0)
        bases = []
        self.row_places, self.col_places = [], []
        for row in rows_of:
            bases.append(len(direct))
            add(row, col_own, bases[-1])
            pad(16)
            self.row_places.append((bases[-1], len(direct) - bases[-1]))
        self.tall = len(direct)
        for col in cols_of:
            start = len(direct)
            for row, base in zip([row_own] + rows_of, [0] + bases):
                add(row, col, base)
                pad(16)
            self.col_places.append((start, len(direct) - start))
        self.used = len(direct)
        pad(LANES)
        self.wide = len(direct)
        self.frame = np.array(frame, np.int32)
        rows, cols = np.array(rows), np.array(cols)
        mine = slice(0, self.tokens)
        gap = np.maximum(
            np.abs(rows[mine][:, None] - rows[None, :]), np.abs(cols[mine][:, None] - cols[None, :])
        )
        return np.array(direct), np.array(tall), np.minimum(gap, FAR)

    def which(self):
        at_h = lax.axis_index("ha") if self.variants_h == 2 else 0
        at_w = lax.axis_index("wa") if self.variants_w == 2 else 0
        return at_h * self.variants_w + at_w

    def near(self, gap_ref):
        lane = lax.broadcasted_iota(jnp.int32, (1, self.wide), 1)
        far = jnp.zeros((1, self.wide), jnp.float32)
        for start, end, row, col in self.ranges[1:]:
            inside = row.place(lax.axis_index("ha"))[1] & col.place(lax.axis_index("wa"))[1]
            cost = jnp.where(inside, 0.0, FAR)
            far = jnp.where((lane >= start) & (lane < end), cost, far)
        return gap_ref[self.which()] + far

    def permute(self, row, col, x):
        pairs = [
            (a * self.count_w + c, b * self.count_w + d)
            for a, b in row.pairs
            for c, d in col.pairs
        ]
        return lax.ppermute(x, ("ha", "wa"), pairs)

    def exchange_rows(self, messages):
        own = self.ranges[0][3]
        return [self.permute(row, own, x) for row, x in zip(self.row_sides, messages)]

    def exchange_cols(self, messages):
        own = self.ranges[0][2]
        return [self.permute(own, col, x) for col, x in zip(self.col_sides, messages)]

    def exchange_all(self, messages):
        return [self.permute(row, col, x) for x, (_, _, row, col) in zip(messages, self.ranges[1:])]


def whole(memory=pltpu.VMEM):
    return pl.BlockSpec(memory_space=memory)


def call(kernel, name, in_specs, out_specs, out_shape, scratch, mib, cost, aliases=None):
    return pl.pallas_call(
        kernel,
        in_specs=in_specs,
        out_specs=out_specs,
        out_shape=out_shape,
        scratch_shapes=scratch,
        compiler_params=pltpu.CompilerParams(vmem_limit_bytes=mib * 1024 * 1024),
        cost_estimate=pl.CostEstimate(
            flops=int(cost * 1e9), bytes_accessed=int(cost * 2e6), transcendentals=0
        ),
        input_output_aliases=aliases or {},
        name=name,
    )


def pick(table, place):
    value = jnp.int32(table[0])
    for index, entry in enumerate(table[1:], 1):
        if entry != table[0]:
            value = jnp.where(place == index, entry, value)
    return value


def relay(blocks):
    held = [[(s, (s % 2 == 0) != bool(chain)) for s in range(blocks)] for chain in range(2)]
    fresh = [[] for _ in range(blocks)]
    for number in range(1, blocks):
        for chain in range(2):
            moved = [held[chain][a] for a in swap(blocks, chain, number)]
            held[chain] = moved
            for s, (block, keys) in enumerate(moved):
                if block != s and keys == (block < s) and block not in [b for _, b in fresh[s]]:
                    fresh[s].append(((chain, number), block))
    batches = []
    for n in range(blocks - 1):
        steps = sorted({fresh[s][n][0] for s in range(blocks)}, key=lambda step: step[::-1])
        which = [steps.index(fresh[s][n][0]) for s in range(blocks)]
        batches.append((steps, which, [fresh[s][n][1] for s in range(blocks)]))
    return batches


def swap(blocks, chain, number):
    start = (chain + number + 1) % 2
    partner = list(range(blocks))
    for low in range(start, blocks - 1, 2):
        partner[low], partner[low + 1] = low + 1, low
    return partner


def tidy(geo, arrays, blocks):
    width = arrays[0].shape[-1]
    tokens, tile_h = geo.tokens, geo.tile_h

    def kernel(*refs):
        ins, (own_ref, even_ref, odd_ref, stage, sems) = refs[:4], refs[4:]
        copies = [
            pltpu.make_async_copy(ref, stage.at[number], sems.at[number])
            for number, ref in enumerate(ins)
        ]
        for copy in copies:
            copy.start()
        for number, copy in enumerate(copies):
            copy.wait()
            for group in range(geo.groups):
                own_ref[number, group * tile_h : (group + 1) * tile_h, :] = stage[number, group]
        odd = lax.rem(lax.axis_index("span"), 2)
        even_ref[...] = own_ref[pl.ds(2 * odd, 2)]
        odd_ref[...] = own_ref[pl.ds(2 - 2 * odd, 2)]

    pair = jax.ShapeDtypeStruct((2, tokens, width), jnp.bfloat16)
    return call(
        kernel,
        "tidy",
        [whole(pltpu.HBM)] * 4,
        [whole()] * 3,
        [jax.ShapeDtypeStruct((4, tokens, width), jnp.bfloat16), pair, pair],
        [
            pltpu.VMEM((4, geo.groups, tile_h, width), jnp.bfloat16),
            pltpu.SemaphoreType.DMA((4,)),
        ],
        60,
        2,
    )(*arrays)


def pack_rows(geo, groups, after, every=False):
    places = geo.places if every else geo.row_places
    select = geo.all_select if every else geo.row_select
    ins = [x for candidates, _, _ in groups for x in candidates]
    _, tokens, width = ins[0].shape
    several = [len(candidates) > 1 for candidates, _, _ in groups]

    def kernel(select_ref, *refs):
        refs, outs = refs[: len(ins)], list(refs[len(ins) + len(after) :])
        chosen = select_ref[geo.which()]
        kept = [outs.pop(0) if many else None for many in several]
        place = lax.axis_index("span")

        def work(x_ref, first, pair):
            for a in range(2):
                x = x_ref[first + a]
                if kept[pair] is not None:
                    kept[pair][a] = x
                picked = dot_nn(chosen, x).astype(jnp.bfloat16)
                for out, (start, size) in zip(outs[pair * len(places) :], places):
                    out[a] = picked[start - tokens : start - tokens + size]

        at = 0
        for pair, (candidates, which, first) in enumerate(groups):
            for index in range(len(candidates)):
                job = functools.partial(work, refs[at + index], first, pair)
                if several[pair]:
                    pl.when(pick(which, place) == index)(job)
                else:
                    job()
            at += len(candidates)

    shapes = [jax.ShapeDtypeStruct((2, tokens, width), jnp.bfloat16)] * sum(several)
    shapes += [
        jax.ShapeDtypeStruct((2, size, width), jnp.bfloat16) for _, size in places * len(groups)
    ]
    out = list(
        call(
            kernel,
            "pack_rows",
            [whole()] * (1 + len(ins)) + [whole(pl.ANY)] * len(after),
            [whole()] * len(shapes),
            shapes,
            [],
            12,
            0.2,
        )(select, *ins, *after)
    )
    xs = [out.pop(0) if many else group[0][0] for many, group in zip(several, groups)]
    return xs, [out[n * len(places) : (n + 1) * len(places)] for n in range(len(groups))]


def pack_cols(geo, xs, firsts, rows, after):
    count, sides = 2 * len(xs), len(rows[0])
    rows = [piece for pair in rows for piece in pair]
    _, tokens, width = xs[0].shape

    def kernel(select_ref, *refs):
        x_refs, refs = refs[: len(xs)], refs[len(xs) :]
        row_refs, refs = refs[: len(rows)], refs[len(rows) + len(after) :]
        outs, tall = refs[:-1], refs[-1]
        chosen = select_ref[geo.which()]
        for a in range(count):
            tall[a, :tokens] = x_refs[a // 2][firsts[a // 2] + a % 2]
            for ref, (start, size) in zip(row_refs[a // 2 * sides :], geo.row_places):
                tall[a, start : start + size] = ref[a % 2]
            picked = dot_nn(chosen, tall[a]).astype(jnp.bfloat16)
            for out, (start, size) in zip(outs, geo.col_places):
                out[a] = picked[start - geo.tall : start - geo.tall + size]

    return call(
        kernel,
        "pack_cols",
        [whole()] * (1 + len(xs) + len(rows)) + [whole(pl.ANY)] * len(after),
        [whole()] * len(geo.col_places),
        [jax.ShapeDtypeStruct((count, size, width), jnp.bfloat16) for _, size in geo.col_places],
        [pltpu.VMEM((count, geo.tall, width), jnp.bfloat16)],
        12,
        0.2,
    )(geo.col_select, *xs, *rows, *after)


def set_bias(bias_ref, gap):
    for reach in range(1, RMAX + 1):
        bias_ref[reach - 1] = jnp.where(gap <= reach, 0.0, -jnp.inf)


def fit(x, lanes):
    return x if x.shape[1] == lanes else jnp.broadcast_to(x[:, :1], (x.shape[0], lanes))


def repeat(x, lanes):
    return jnp.concatenate([x] * (lanes // LANES), axis=1)


def spread(geo, parts, bases, wide):
    places = geo.row_places + geo.col_places
    if len(parts) > 1 + len(places):
        places = geo.places
    for a in range(2):
        for ref, base, (start, size) in zip(parts, bases, [(0, geo.tokens)] + places):
            wide[a, start : start + size] = ref[base + a]
        if geo.wide > geo.used:
            wide[a, geo.used :] = jnp.zeros((geo.wide - geo.used, wide.shape[-1]), jnp.bfloat16)


def lay_out(geo, heads, small, own, parts, bases):
    tokens, wide_rows = geo.tokens, geo.wide
    width = own.shape[-1]
    depth = width // heads
    scale = LOG2E / math.sqrt(depth)

    def kernel(radius_ref, live_ref, gap_ref, row_frame_ref, own_ref, *refs):
        parts_refs, (wide, products, bias_ref) = refs[: len(parts)], refs[len(parts) :]
        spread(geo, parts_refs, bases, wide)
        live = row_frame_ref[...] < live_ref[lax.axis_index("span")]
        set_bias(bias_ref, jnp.where(live, geo.near(gap_ref), FAR))
        for h in range(heads):
            lanes = slice(h * depth, (h + 1) * depth)
            score = dot_nt(own_ref[0, :, lanes], wide[0, :, lanes])
            products[0, h] = score * scale + bias_ref[radius_ref[h] - 1]
            products[1, h] = dot_nt(own_ref[1, :, lanes], wide[1, :, lanes])

    return call(
        kernel,
        "lay_out",
        [whole(pltpu.SMEM)] * 2 + [whole()] * (3 + len(parts)),
        [whole()] * 2,
        [
            jax.ShapeDtypeStruct((2, wide_rows, width), jnp.bfloat16),
            jax.ShapeDtypeStruct((2, heads, tokens, wide_rows), jnp.float32),
        ],
        [pltpu.VMEM((RMAX, tokens, wide_rows), jnp.float32)],
        16,
        0.5,
    )(*small, geo.gap, geo.frame[:tokens, None], own, *parts)


def forward(geo, heads, small, own, sources, parts, bases, state, last, after):
    tokens, wide_rows = geo.tokens, geo.wide
    width = own.shape[-1]
    depth = width // heads
    scale = LOG2E / math.sqrt(depth)
    per = len(parts)
    stat_rows = round_up(2 * heads, 8)
    first = state is None
    lanes = [slice(h * depth, (h + 1) * depth) for h in range(heads)]

    def kernel(
        radius_ref, live_ref, gap_ref, frame_ref, row_frame_ref, select_ref, own_ref, *refs
    ):
        parts_refs, refs = refs[:per], refs[per:]
        state_in, refs = (None, refs) if first else (refs[:3], refs[3:])
        wide, products, *refs = refs[len(after) :]
        if last:
            outs, (accum, top, total, bias_ref) = refs[:4], refs[4:]
        else:
            accum, top, total, bias_ref = refs
        place = lax.axis_index("span")
        source = place if first else pick(sources, place)
        active = source <= place

        spread(geo, parts_refs, bases, wide)
        if first:
            accum[...] = jnp.zeros(accum.shape, jnp.float32)
            top[...] = jnp.full(top.shape, -jnp.inf, jnp.float32)
            total[...] = jnp.zeros(total.shape, jnp.float32)
        else:
            for old, new in zip(state_in, (accum, top, total)):
                new[...] = old[...]

        def multiply(h, base):
            score = dot_nt(own_ref[base, :, lanes[h]], wide[0, :, lanes[h]])
            score = score * scale + bias_ref[radius_ref[h] - 1]
            products[0, h] = score
            products[1, h] = dot_nt(own_ref[base + 1, :, lanes[h]], wide[1, :, lanes[h]])
            return score

        def attend():
            live = frame_ref[...] < live_ref[source]
            set_bias(bias_ref, jnp.where(live, geo.near(gap_ref), FAR))
            ones = jnp.ones((wide_rows, LANES), jnp.bfloat16)
            ahead = multiply(0, 2)
            for h in range(heads):
                score = ahead
                if h + 1 < heads:
                    ahead = multiply(h + 1, 2)
                best = jnp.max(score, axis=1, keepdims=True)
                new_top = jnp.maximum(top[h], best)
                fading = jnp.exp2(top[h] - new_top)
                top[h] = new_top
                weight = jnp.exp2(score - repeat(new_top, wide_rows)).astype(jnp.bfloat16)
                value = jnp.concatenate([wide[1, :, lanes[h]], ones], axis=1)
                both = dot_nn(weight, value)
                accum[:, lanes[h]] = accum[:, lanes[h]] * fit(fading, depth) + both[:, :depth]
                total[h] = total[h] * fading + both[:, depth:]

        def keep():
            live = row_frame_ref[...] < live_ref[place]
            set_bias(bias_ref, jnp.where(live, geo.near(gap_ref), FAR))
            for h in range(heads):
                multiply(h, 0)

        def finish():
            attended_ref, lse_ref, delta_ref, packed_ref = outs
            lane = lax.broadcasted_iota(jnp.int32, (tokens, LANES), 1)
            column = jnp.zeros((tokens, LANES), jnp.float32)
            for h in range(heads):
                rounded = (accum[:, lanes[h]] / fit(total[h], depth)).astype(jnp.bfloat16)
                rounded = rounded.astype(jnp.float32)
                accum[:, lanes[h]] = rounded
                lse = top[h] + jnp.log2(total[h])
                grad = own_ref[3, :, lanes[h]].astype(jnp.float32)
                delta = jnp.sum(rounded * grad, axis=1, keepdims=True)
                delta = jnp.broadcast_to(delta, (tokens, LANES))
                lse_ref[h] = lse
                delta_ref[h] = delta
                column = jnp.where(lane == h, lse, column)
                column = jnp.where(lane == heads + h, delta, column)
            packed = jnp.zeros((wide_rows, LANES), jnp.float32)
            rest = column
            chosen = select_ref[geo.which()]
            for _ in range(3):
                part = rest.astype(jnp.bfloat16)
                rest = rest - part.astype(jnp.float32)
                packed = packed + dot_nn(chosen, part)
            packed_ref[...] = jnp.transpose(packed)[:stat_rows]
            for group in range(geo.groups):
                at = slice(group * geo.tile_h, (group + 1) * geo.tile_h)
                attended_ref[group] = accum[at, :].astype(jnp.bfloat16)

        if first:
            attend()
        else:
            pl.when(active)(attend)
            pl.when(jnp.logical_not(active))(keep)
        if last:
            finish()

    ins = [*small, geo.gap, geo.frame[None, :], geo.frame[:tokens, None], geo.select, own, *parts]
    ins += [] if first else list(state)
    stat = (heads, tokens, LANES)
    running = [(tokens, width), stat, stat]
    shapes = [
        jax.ShapeDtypeStruct((2, wide_rows, width), jnp.bfloat16),
        jax.ShapeDtypeStruct((2, heads, tokens, wide_rows), jnp.float32),
    ]
    scratch = []
    if last:
        shapes += [
            jax.ShapeDtypeStruct((geo.groups, geo.tile_h, width), jnp.bfloat16),
            jax.ShapeDtypeStruct(stat, jnp.float32),
            jax.ShapeDtypeStruct(stat, jnp.float32),
            jax.ShapeDtypeStruct((stat_rows, wide_rows), jnp.float32),
        ]
        scratch += [pltpu.VMEM(shape, jnp.float32) for shape in running]
    else:
        shapes += [jax.ShapeDtypeStruct(shape, jnp.float32) for shape in running]
    return call(
        kernel,
        "forward",
        [whole(pltpu.SMEM)] * 2 + [whole()] * (len(ins) - 2) + [whole(pl.ANY)] * len(after),
        [whole()] * len(shapes),
        shapes,
        scratch + [pltpu.VMEM((RMAX, tokens, wide_rows), jnp.float32)],
        20,
        1.5,
    )(*ins, *after)


def merge(geo, pieces, after):
    def kernel(*refs):
        out = refs[-1]
        row = refs[0][...]
        lane = lax.broadcasted_iota(jnp.int32, row.shape, 1)
        for ref, (start, *_) in zip(refs[1:], geo.ranges[1:]):
            row = jnp.where(lane >= start, ref[...], row)
        out[...] = row

    return call(
        kernel,
        "merge",
        [whole()] * len(pieces) + [whole(pl.ANY)] * len(after),
        whole(),
        jax.ShapeDtypeStruct(pieces[0].shape, jnp.float32),
        [],
        4,
        0.1,
    )(*pieces, *after)


def query_grads(geo, heads, lse, delta, sources, slots):
    tokens, wide_rows = geo.tokens, geo.wide
    width = slots[0][0].shape[-1]
    depth = width // heads
    natural = 1.0 / math.sqrt(depth)
    lanes = [slice(h * depth, (h + 1) * depth) for h in range(heads)]

    def kernel(lse_ref, delta_ref, *refs):
        slot_refs, (out, token, accum) = refs[: 2 * len(slots)], refs[2 * len(slots) :]
        token[...] = jnp.zeros(token.shape, jnp.float32)
        place = lax.axis_index("span")

        def step(wide, products, first):
            for h in range(heads):
                prob = jnp.exp2(products[0, h] - repeat(lse_ref[h], wide_rows))
                slope = prob * (products[1, h] - repeat(delta_ref[h], wide_rows))
                part = dot_nn(slope.astype(jnp.bfloat16), wide[0, :, lanes[h]])
                accum[:, lanes[h]] = part if first else accum[:, lanes[h]] + part

        for n, table in enumerate(sources):
            work = functools.partial(step, slot_refs[2 * n], slot_refs[2 * n + 1], n == 0)
            if n == 0:
                work()
            else:
                pl.when(pick(table, place) < place)(work)
        for group in range(geo.groups):
            at = slice(group * geo.tile_h, (group + 1) * geo.tile_h)
            out[group] = (accum[at, :] * natural).astype(jnp.bfloat16)

    flat = [x for slot in slots for x in slot]
    return call(
        kernel,
        "query_grads",
        [whole()] * (2 + len(flat)),
        [whole()] * 2,
        [
            jax.ShapeDtypeStruct((geo.groups, geo.tile_h, width), jnp.bfloat16),
            jax.ShapeDtypeStruct((8, LANES), jnp.float32),
        ],
        [pltpu.VMEM((tokens, width), jnp.float32)],
        8,
        2,
    )(lse, delta, *flat)


def key_grads(geo, blocks, heads, stats, sources, slots, state, last):
    tokens, wide_rows = geo.tokens, geo.wide
    width = slots[0][0].shape[-1]
    depth = width // heads
    natural = 1.0 / math.sqrt(depth)
    stat_rows = stats[0].shape[0]
    lanes = [slice(h * depth, (h + 1) * depth) for h in range(heads)]

    def kernel(*refs):
        slot_refs, refs = refs[: 2 * len(slots)], refs[2 * len(slots) :]
        stat_refs, refs = refs[: len(stats)], refs[len(stats) :]
        state_in, refs = (None, refs) if state is None else (refs[0], refs[1:])
        outs, refs = (refs[:2], refs[2:]) if last else (None, refs)
        accum, rows = refs
        place = lax.axis_index("span")
        accum[...] = jnp.zeros(accum.shape, jnp.float32) if state is None else state_in[...]
        for n, ref in enumerate(stat_refs):
            rows[n] = ref[...]

        def step(wide, products, rotation):
            for h in range(heads):
                prob = jnp.exp2(products[0, h] - rows[rotation, h : h + 1, :])
                accum[1, :, lanes[h]] += dot_nn(prob.astype(jnp.bfloat16), wide[1, :, lanes[h]])
                slope = prob * (products[1, h] - rows[rotation, heads + h : heads + h + 1, :])
                accum[0, :, lanes[h]] += dot_nn(slope.astype(jnp.bfloat16), wide[0, :, lanes[h]])

        for n, table in enumerate(sources):
            wide, products = slot_refs[2 * n : 2 * n + 2]
            if table == list(range(blocks)):
                step(wide, products, 0)
            else:
                source = pick(table, place)
                rotation = lax.rem(place - source + blocks, blocks) - 1
                pl.when(source > place)(functools.partial(step, wide, products, rotation))
        if last:
            for group in range(geo.groups):
                at = slice(group * geo.tile_h, (group + 1) * geo.tile_h)
                outs[0][group] = (accum[0, at, :] * natural).astype(jnp.bfloat16)
                outs[1][group] = accum[1, at, :].astype(jnp.bfloat16)

    ins = [x for slot in slots for x in slot] + list(stats)
    ins += [] if state is None else [state]
    running = (2, tokens, width)
    shapes = [jax.ShapeDtypeStruct(running, jnp.float32)]
    if last:
        shapes = [jax.ShapeDtypeStruct((geo.groups, geo.tile_h, width), jnp.bfloat16)] * 2
    return call(
        kernel,
        "key_grads",
        [whole()] * len(ins),
        [whole()] * len(shapes),
        shapes,
        ([pltpu.VMEM(running, jnp.float32)] if last else [])
        + [pltpu.VMEM((len(stats), stat_rows, wide_rows), jnp.float32)],
        8,
        2,
    )(*ins)


def rotate(x, by, blocks):
    return lax.ppermute(x, "span", [(i, (i + by) % blocks) for i in range(blocks)])


def shards(queries, cache_keys, cache_values, grad_attended, radius, frame_count, sizes):
    blocks, count_h, count_w = sizes
    frames, tile_h, tile_w, width = queries.shape[1:]
    heads = radius.shape[0]
    geo = Geometry(frames, tile_h, tile_w, count_h, count_w)
    small = (radius, frame_count)

    def grouped(x):
        return jnp.transpose(x[0], (0, 2, 1, 3)).reshape(geo.groups, tile_h, width)

    def restored(x):
        x = x.reshape(frames, tile_w, tile_h, width)
        return jnp.transpose(x, (0, 2, 1, 3))[None]

    arrays = [grouped(x) for x in (cache_keys, cache_values, queries, grad_attended)]
    own, *chains = tidy(geo, arrays, blocks)
    batches = relay(blocks)
    needed = {step for steps, _, _ in batches for step in steps}
    sources = [list(range(blocks))] + [blks for _, _, blks in batches]
    moved = {}

    def hop(chain, number, after):
        if any(c == chain and n >= number for c, n in needed):
            x = chains[chain]
            x = lax.optimization_barrier((x, *after))[0] if after else x
            pairs = list(enumerate(swap(blocks, chain, number)))
            moved[chain, number] = chains[chain] = lax.ppermute(x, "span", pairs)

    def take(n, after):
        steps, which, _ = batches[n - 1]
        group = ([moved[step] for step in steps], which, 0)
        (x,), (messages,) = pack_rows(geo, [group], after, n == blocks - 1)
        return x, messages

    hop(0, 1, [])
    hop(1, 1, [])
    xs, (messages, asked) = pack_rows(geo, [([own], None, 0), ([own], None, 2)], [])
    x, pieces = own, geo.exchange_rows(messages)
    slots, state = [], None
    for n in range(blocks):
        last = n == blocks - 1
        after = []
        if n == 0 or not last:
            before = [] if n == 0 else [state[0]] if n == 1 else [state[0], asked[0]]
            messages = pack_cols(geo, [x], [0], [pieces], before)
            ready = list(messages[:1])
            pieces = pieces + geo.exchange_cols(messages)
        parts = [x] + pieces
        if n == 0:
            asked = geo.exchange_rows(lax.optimization_barrier((*asked, *ready))[:-1])
        if not last:
            hop(0, n + 2, [state[0]] if state else ready)
            x, messages = take(n + 1, ready)
            after = list(messages[:1])
            hop(1, n + 2, after)
        if n == min(1, blocks - 1):
            cols = geo.exchange_cols(pack_cols(geo, [own], [2], [asked], after))
            asked = [own] + asked + cols
            asked = lay_out(geo, heads, small, own, asked, [2] + [0] * len(asked[1:]))
        if not last:
            if n == blocks - 2:
                corner = [r.length != tile_h and c.length != tile_w for _, _, r, c in geo.ranges[1:]]
                late = lax.optimization_barrier(
                    (*[m for m, flag in zip(messages, corner) if flag], parts[-1])
                )
                late = iter(late[:-1])
                messages = [next(late) if flag else m for m, flag in zip(messages, corner)]
                pieces = geo.exchange_all(messages)
            else:
                pieces = geo.exchange_rows(messages)
        wide, products, *state = forward(
            geo, heads, small, own, sources[n], parts, [0] * len(parts), state, last, after
        )
        slots.append([wide, products])
    attended, lse, delta, packed = state

    grad_q, token = query_grads(geo, heads, lse, delta, sources, slots)
    brought = geo.exchange_all([packed] * len(geo.places))
    own_stats = merge(geo, [packed] + brought, [token])
    stats = [rotate(own_stats, n, blocks) for n in range(1, blocks)]
    begun = key_grads(geo, blocks, heads, [own_stats], sources[:1], [asked], None, False)[0]
    grad_k, grad_v = key_grads(
        geo, blocks, heads, stats, sources[1:], slots[1:], begun, True
    )
    return tuple(restored(x) for x in (attended, grad_q, grad_k, grad_v))


def solution(mesh):
    placed = P("span", None, "ha", "wa", None)
    sizes = tuple(mesh.shape[name] for name in ("span", "ha", "wa"))
    return jax.shard_map(
        functools.partial(shards, sizes=sizes),
        mesh=mesh,
        in_specs=(placed,) * 4 + (P(), P()),
        out_specs=(placed,) * 4,
        check_vma=False,
    )
```
